128 devices in a mesh: dp: 16 (over x, y), section: 8 (over z, core).
Axes of the slice: x: 4, y: 4, z: 4, core: 2. Of those that a mesh axis runs over, the one named last changes fastest.
Arguments:
- patches: bfloat16 [16, 256, 1280], P('dp'), may hold values from -6 to 6
- cotangent: bfloat16 [16, 256, 1280], P('dp'), may hold values from -6 to 6
- keep_order: int32 [16, 256], P('dp'), may hold values from 0 to 255, each once within a row
- keep_count: int32 [16], P('dp'), may hold values from 104 to 192, as said below
- destination: int32 [16, 192], P('dp'), may hold values from 0 to 15, as said below
- norm_gain: float32 [16, 1280], P('section'), may hold values from 0.1 to 1.9
- up_blocks: bfloat16 [16, 96, 128, 128], P('section'), may hold values from -0.25 to 0.25
- up_index: int32 [16, 96], P('section'), may hold values from 0 to 199, as said below
- down_blocks: bfloat16 [16, 96, 128, 128], P('section'), may hold values from -0.15625 to 0.15625
- down_index: int32 [16, 96], P('section'), may hold values from 0 to 199, as said below
- layer_count: int32 [8], P('section'), may hold values from 1 to 2, as said below
- regrow_mask: int32 [16, 400], P('section', 'dp'), may hold values 0 or 1
Outputs:
- scores: float32 [16, 400], P('section', 'dp')
The draws below stay inside these ranges and needn't reach their ends.
Inputs may be any that keep to these rules, and one draw needn't show every extreme that they name: `keep_order`: each row is an ordering of 0 to 255. `keep_count`: some image keeps exactly 192 patches and some exactly 104. `destination`: the kept rows of one replica, image by image and j ascending, are dealt to the replicas in turn from a replica drawn for that replica; so at most 12 of one replica's kept rows go to one replica, and some replica sends exactly 12 to every replica; entries with j >= keep_count are arbitrary. `up_index`: each row lists 96 different block numbers. `down_index`: each row lists 96 different block numbers. `layer_count`: some section uses 2 layers and some uses 1.
All inputs are finite; a program needn't handle non-finite values. No bound on the sum of `regrow_mask` on one device may be relied on, other than what follows from the above.
Results may differ from the reference program's by a relative error of at most 0.0095.
Values may be sent and summed in bfloat16 or wider, within the bound.
A program may use at most 192 MiB of HBM per device.

```python
import jax
import jax.numpy as jnp
from jax import lax

D = 1280
P_SIZE = 256
FF = 2560
BLK = 128
KMIN = 104
KMAX = 192
LMAX = 2
NLIVE = 96
IMG_DEV = 1
IMAGES = 16
LAYERS = 16
NB = 200
CAP = 12
N_DP = 16


def kept_counts(key):
    counts = jax.random.randint(jax.random.fold_in(key, 11), (IMAGES,), KMIN, KMAX + 1)
    order = jax.random.permutation(jax.random.fold_in(key, 12), IMAGES)
    counts = counts.at[order[0]].set(KMAX)
    return counts.at[order[1]].set(KMIN).astype(jnp.int32)


def draw_keep_count(key, part):
    return kept_counts(key)


def draw_destination(key, part):
    counts = kept_counts(key)
    replicas = IMAGES // IMG_DEV
    alive = (jnp.arange(KMAX)[None, :] < counts[:, None]).astype(jnp.int32)
    per_replica = alive.reshape(replicas, IMG_DEV * KMAX)
    dealt_rank = jnp.cumsum(per_replica, axis=1) - 1
    first_target = jax.random.randint(jax.random.fold_in(key, 13), (replicas, 1), 0, replicas)
    dealt = (dealt_rank + first_target) % replicas
    filler = jax.random.randint(jax.random.fold_in(key, 14), (replicas, IMG_DEV * KMAX), 0, replicas)
    return jnp.where(per_replica > 0, dealt, filler).reshape(IMAGES, KMAX).astype(jnp.int32)


def live_blocks(key):
    ranking = jax.random.randint(key, (LAYERS, NB), 0, 1 << 20) * NB + jnp.arange(NB)[None, :]
    return jnp.argsort(ranking, axis=1)[:, :NLIVE].astype(jnp.int32)


def draw_up_index(key, part):
    return live_blocks(jax.random.fold_in(key, 21))


def draw_down_index(key, part):
    return live_blocks(jax.random.fold_in(key, 22))


def draw_layer_count(key, part):
    section_total = LAYERS // LMAX
    counts = jax.random.randint(jax.random.fold_in(key, 31), (section_total,), 1, LMAX + 1)
    order = jax.random.permutation(jax.random.fold_in(key, 32), section_total)
    counts = counts.at[order[0]].set(LMAX)
    return counts.at[order[1]].set(1).astype(jnp.int32)


def set_ends(array, key, smallest, largest):
    longest = array.shape.index(max(array.shape))
    spots = []
    for shift in (0, 1):
        where = [jax.random.randint(jax.random.fold_in(key, axis), (), 0, length) for axis, length in enumerate(array.shape)]
        where[longest] = (where[longest] + shift) % array.shape[longest]
        spots.append(tuple(where))
    return array.at[spots[0]].set(smallest).at[spots[1]].set(largest)


def level_of(key, extent, pieces, smallest, largest):
    def one(axis_at, parts):
        heights = jax.random.uniform(jax.random.fold_in(jax.random.fold_in(key, 6), axis_at), (parts,), jnp.float32, smallest / len(pieces), largest / len(pieces))
        return jnp.repeat(jnp.exp(heights), extent[axis_at] // parts).reshape((-1,) + (1,) * (len(extent) - axis_at - 1))

    level = one(*pieces[0])
    for cut in pieces[1:]:
        level = level * one(*cut)
    return level


def scatter_about(own_key, extent, spread, reach, shards=(), kind=jnp.bfloat16):
    result = spread * jax.random.normal(own_key, extent, jnp.float32)
    if shards:
        result = result * level_of(own_key, extent, shards, -0.22, 0.18)
    return jnp.clip(result, -reach, reach).astype(kind)


def setup_inputs(seed: int = 0) -> dict:
    key_list = jax.random.split(jax.random.key(seed), 13)
    return {
        "patches": scatter_about(key_list[0], (IMAGES, P_SIZE, D), 1.0, 6.0, ((0, 16),)),
        "cotangent": scatter_about(key_list[1], (IMAGES, P_SIZE, D), 1.0, 6.0, ((0, 16),)),
        "keep_order": jax.vmap(lambda own: jax.random.permutation(own, P_SIZE))(jax.random.split(key_list[2], IMAGES)).reshape((IMAGES, P_SIZE)).astype(jnp.int32),
        "keep_count": draw_keep_count(jax.random.fold_in(key_list[12], 71), 0),
        "destination": draw_destination(jax.random.fold_in(key_list[12], 71), 0),
        "norm_gain": jnp.clip(1.0 + 0.18 * jax.random.normal(key_list[5], (LAYERS, D), jnp.float32), 0.1, 1.9),
        "up_blocks": scatter_about(key_list[6], (LAYERS, NLIVE, BLK, BLK), (D // 2) ** -0.5, 0.25, ((0, 8),)),
        "up_index": draw_up_index(jax.random.fold_in(key_list[12], 71), 0),
        "down_blocks": scatter_about(key_list[8], (LAYERS, NLIVE, BLK, BLK), (FF // 2) ** -0.5, 0.15625, ((0, 8),)),
        "down_index": draw_down_index(jax.random.fold_in(key_list[12], 71), 0),
        "layer_count": draw_layer_count(jax.random.fold_in(key_list[12], 71), 0),
        "regrow_mask": set_ends((jax.random.randint(key_list[11], (LAYERS, 2 * NB), 0, 2) < 1).astype(jnp.int32), jax.random.fold_in(key_list[11], 1), 0, 1),
    }


EPS_NORM = 1e-06
EPS_SCORE = 1e-06

def dense_matrix(blocks, index, rows, cols):
    edge = blocks.shape[-1]
    total = rows // edge * (cols // edge)
    placed = jnp.zeros((total, edge, edge), blocks.dtype).at[index].set(blocks)
    grid = placed.reshape(rows // edge, cols // edge, edge, edge)
    return grid.transpose(0, 2, 1, 3).reshape(rows, cols)

def to_blocks(matrix, edge):
    rows, cols = matrix.shape
    grid = matrix.reshape(rows // edge, edge, cols // edge, edge)
    return grid.transpose(0, 2, 1, 3).reshape(-1, edge, edge)

def contract_rows(left, right):
    return lax.dot_general(left, right, (((0,), (0,)), ((), ())), preferred_element_type=jnp.float32)

def contract_cols(left, right):
    return lax.dot_general(left, right, (((1,), (1,)), ((), ())), preferred_element_type=jnp.float32)

def forward_parts(rows_in, gain, w_up):
    x_float = rows_in.astype(jnp.float32)
    centred = x_float - lax.optimization_barrier(jnp.mean(x_float, axis=-1, keepdims=True))
    inv_std = lax.rsqrt(lax.optimization_barrier(jnp.mean(centred * centred, axis=-1, keepdims=True)) + EPS_NORM)
    normed = centred * inv_std
    act = (normed * gain).astype(jnp.bfloat16)
    pre = jnp.dot(act, w_up, preferred_element_type=jnp.float32)
    return (x_float, normed, inv_std, act, pre)

def gelu_tanh(values):
    return jax.nn.gelu(values, approximate=True)

def layer_forward(rows_in, gain, w_up, w_down):
    x_float, normed, inv_std, act, pre = forward_parts(rows_in, gain, w_up)
    hidden = gelu_tanh(pre).astype(jnp.bfloat16)
    out = jnp.dot(hidden, w_down, preferred_element_type=jnp.float32)
    return (x_float + out).astype(jnp.bfloat16)

def layer_backward(rows_in, grad_out, gain, w_up, w_down):
    x_float, normed, inv_std, act, pre = forward_parts(rows_in, gain, w_up)
    hidden_float, gelu_back = jax.vjp(gelu_tanh, pre)
    hidden = hidden_float.astype(jnp.bfloat16)
    grad_hidden = contract_cols(grad_out, w_down)
    grad_pre = gelu_back(grad_hidden)[0].astype(jnp.bfloat16)
    grad_normed = contract_cols(grad_pre, w_up) * gain
    grad_norm = inv_std * (grad_normed - lax.optimization_barrier(jnp.mean(grad_normed, axis=-1, keepdims=True)) - normed * lax.optimization_barrier(jnp.mean(grad_normed * normed, axis=-1, keepdims=True)))
    grad_in = (grad_out.astype(jnp.float32) + grad_norm).astype(jnp.bfloat16)
    return (grad_in, act, grad_pre, hidden)

def block_scores(up_total, down_total, rows_total):
    stacked = jnp.concatenate([to_blocks(up_total, BLK), to_blocks(down_total, BLK)], axis=0)
    return jnp.sqrt(lax.optimization_barrier(jnp.mean(stacked * stacked, axis=(1, 2))) / rows_total + EPS_SCORE)

def inboxes(rows_x, rows_ct, keep_count, destination):
    slots_dev = IMG_DEV * KMAX
    alive = (jnp.arange(KMAX)[None, :] < keep_count[:, None]).reshape(N_DP, slots_dev)
    target_id = destination.reshape(N_DP, slots_dev)
    hits = jnp.logical_and(target_id[:, :, None] == jnp.arange(N_DP)[None, None, :], alive[:, :, None]).astype(jnp.int32)
    position = lax.optimization_barrier(jnp.sum((jnp.cumsum(hits, axis=1) - 1) * hits, axis=2))
    landing = jnp.where(alive, target_id * CAP + position, slots_dev).astype(jnp.int32)

    def place(values, spots):
        return jnp.zeros((slots_dev, D), values.dtype).at[spots].set(values, mode='drop')

    def regroup(sent):
        return sent.reshape(N_DP, N_DP, CAP, D).transpose(1, 0, 2, 3).reshape(N_DP, N_DP * CAP, D)
    sent_x = jax.vmap(place)(rows_x.reshape(N_DP, slots_dev, D), landing)
    sent_ct = jax.vmap(place)(rows_ct.reshape(N_DP, slots_dev, D), landing)
    return (regroup(sent_x), regroup(sent_ct))

def reference(patches, cotangent, keep_order, keep_count, destination, norm_gain, up_blocks, up_index, down_blocks, down_index, layer_count, regrow_mask):
    kept = keep_order[:, :KMAX]
    rows_x = jax.vmap(lambda image, order: image[order])(patches, kept)
    rows_ct = jax.vmap(lambda image, order: image[order])(cotangent, kept)
    inbox_x, inbox_ct = inboxes(rows_x, rows_ct, keep_count, destination)
    w_up = jax.vmap(lambda blocks, index: dense_matrix(blocks, index, D, FF))(up_blocks, up_index)
    w_down = jax.vmap(lambda blocks, index: dense_matrix(blocks, index, FF, D))(down_blocks, down_index)
    layer_ids = jnp.arange(LAYERS)
    active = layer_ids % LMAX < layer_count[layer_ids // LMAX]

    def one_replica(totals, inputs):
        rows_in, grads_in = inputs
        saved_inputs = []
        current = rows_in
        for layer in range(LAYERS):
            saved_inputs.append(current)
            moved = layer_forward(current, norm_gain[layer], w_up[layer], w_down[layer])
            current = jnp.where(active[layer], moved, current)
        grad_now = grads_in
        up_terms = [None] * LAYERS
        down_terms = [None] * LAYERS
        for layer in reversed(range(LAYERS)):
            grad_in, act, grad_pre, hidden = layer_backward(saved_inputs[layer], grad_now, norm_gain[layer], w_up[layer], w_down[layer])
            up_terms[layer] = jnp.where(active[layer], contract_rows(act, grad_pre), 0.0)
            down_terms[layer] = jnp.where(active[layer], contract_rows(hidden, grad_now), 0.0)
            grad_now = jnp.where(active[layer], grad_in, grad_now)
        up_part = lax.optimization_barrier(jnp.stack(up_terms).astype(jnp.bfloat16)).astype(jnp.float32)
        down_part = lax.optimization_barrier(jnp.stack(down_terms).astype(jnp.bfloat16)).astype(jnp.float32)
        return ((totals[0] + up_part, totals[1] + down_part), None)
    start = (jnp.zeros((LAYERS, D, FF), jnp.float32), jnp.zeros((LAYERS, FF, D), jnp.float32))
    (up_total, down_total), _ = lax.scan(one_replica, start, (inbox_x, inbox_ct))
    rows_total = float(N_DP * IMG_DEV * KMAX)
    every_score = jax.vmap(lambda upper, lower: block_scores(upper, lower, rows_total))(up_total, down_total)
    live_up = jnp.any(up_index[:, :, None] == jnp.arange(NB)[None, None, :], axis=1)
    live_down = jnp.any(down_index[:, :, None] == jnp.arange(NB)[None, None, :], axis=1)
    live_all = jnp.concatenate([live_up, live_down], axis=1)
    eligible = jnp.logical_and(jnp.logical_not(live_all), regrow_mask == 1)
    return jnp.where(eligible, every_score, 0.0)
```

```python
import functools
import jax
import jax.numpy as jnp
from jax import lax
from jax.experimental import pallas as pl
from jax.experimental.pallas import tpu as pltpu
from jax.sharding import PartitionSpec as P

D = 1280
FF = 2560
BLK = 128
KMAX = 192
LMAX = 2
NB = 200
NLIVE = 96
NDEAD = NB - NLIVE
UP_COLS = FF // BLK
DOWN_COLS = D // BLK
PARTS = 2 * LMAX
EPS_NORM = 1e-06
EPS_SCORE = 1e-06
MICRO = 2
ROWS = KMAX // MICRO
CHUNK = 512
MESH = pl.DeviceIdType.MESH
F32 = jnp.float32
BF16 = jnp.bfloat16
GELU_A = 0.7978845608028654
GELU_B = 0.044715


def dot(a, b):
    return jnp.dot(a, b, preferred_element_type=F32)


def dot_t(a, b):
    return lax.dot_general(a, b, (((1,), (1,)), ((), ())), preferred_element_type=F32)


def gelu(v):
    return 0.5 * v * (1.0 + jnp.tanh(GELU_A * (v + GELU_B * (v * v * v))))


def gelu_slope(v):
    sq = v * v
    t = jnp.tanh(GELU_A * (v + GELU_B * (v * sq)))
    return 0.5 * (1.0 + t) + 0.5 * v * (1.0 - t * t) * (GELU_A * (1.0 + 3.0 * GELU_B * sq))


def chain_kernel(
    inv_ref, dead_row, dead_col,
    active, pick_ref, patches, cotangent, gain, up_hbm, down_hbm,
    out_hbm,
    stage_a, stage_b, w_up, w_down, xs, gs, normed, inv_std, act, hidden, pre, grad_pre,
    act_t, hidden_t, grad_pre_b, gs_b,
    stage_sem, out_sem, x_send, x_recv, g_send, g_recv,
):
    sections = lax.axis_size("section")
    replica = lax.axis_index("dp")
    section = lax.axis_index("section")
    first = section == 0
    last = section == sections - 1
    stages = (stage_a, stage_b)
    packs = stages

    def flag(l):
        return active[l:l + 1, :1] == 1

    def load(part):
        l, kind = part // 2, part % 2
        src = (up_hbm, down_hbm)[kind].at[l]
        return pltpu.make_async_copy(src, stages[part % 2].at[pl.ds(0, NLIVE)], stage_sem.at[part])

    stage_a[NLIVE] = jnp.zeros((BLK, BLK), BF16)
    stage_b[NLIVE] = jnp.zeros((BLK, BLK), BF16)
    load(0).start()
    load(1).start()

    barrier = pltpu.get_barrier_semaphore()

    @pl.when(jnp.logical_not(first))
    def _():
        pl.semaphore_signal(barrier, inc=1, device_id=(replica, section - 1), device_id_type=MESH)

    @pl.when(jnp.logical_not(last))
    def _():
        pl.semaphore_signal(barrier, inc=1, device_id=(replica, section + 1), device_id_type=MESH)

    @pl.when(jnp.logical_or(first, last))
    def _():
        pl.semaphore_wait(barrier, 1)

    @pl.when(jnp.logical_not(jnp.logical_or(first, last)))
    def _():
        pl.semaphore_wait(barrier, 2)

    def picked(table):
        hot = pick_ref[:, :1] == lax.broadcasted_iota(jnp.int32, (KMAX, table.shape[0]), 1)
        return dot(hot.astype(BF16), table[...]).astype(BF16)

    @pl.when(first)
    def _():
        xs[0] = picked(patches)

    @pl.when(last)
    def _():
        gs[LMAX] = picked(cotangent)

    for part in range(PARTS):
      with jax.named_scope("dense"):
        load(part).wait()
        l, kind = part // 2, part % 2
        target, cols = ((w_up, UP_COLS), (w_down, DOWN_COLS))[kind]

        def place(q, carry, l=l, target=target, cols=cols, part=part):
            rb = q // cols
            cb = q - rb * cols
            target[
                l,
                pl.ds(pl.multiple_of(rb * BLK, BLK), BLK),
                pl.ds(pl.multiple_of(cb * BLK, BLK), BLK),
            ] = stages[part % 2][inv_ref[part * NB + q]]
            return carry

        lax.fori_loop(0, NB, place, 0, unroll=4)
      if part + 2 < PARTS:
        load(part + 2).start()

    def rows_of(mb):
        return pl.ds(pl.multiple_of(mb * ROWS, ROWS), ROWS)

    def cols_of(j, size):
        return pl.ds(pl.multiple_of(j * size, size), size)

    def send_x(mb):
        return pltpu.make_async_remote_copy(
            src_ref=xs.at[LMAX, rows_of(mb)], dst_ref=xs.at[0, rows_of(mb)],
            send_sem=x_send.at[mb], recv_sem=x_recv.at[mb],
            device_id=(replica, section + 1), device_id_type=MESH,
        )

    def send_g(mb):
        return pltpu.make_async_remote_copy(
            src_ref=gs.at[0, rows_of(mb)], dst_ref=gs.at[LMAX, rows_of(mb)],
            send_sem=g_send.at[mb], recv_sem=g_recv.at[mb],
            device_id=(replica, section - 1), device_id_type=MESH,
        )

    def forward(mb, carry):
        r = rows_of(mb)

        @pl.when(jnp.logical_not(first))
        def _():
            send_x(mb).wait_recv()

        for l in range(LMAX):
            x = xs[l, r, :].astype(F32)
            centred = x - jnp.mean(x, axis=-1, keepdims=True)
            inv = lax.rsqrt(jnp.mean(centred * centred, axis=-1, keepdims=True) + EPS_NORM)
            n = centred * inv
            normed[l, r, :] = n
            inv_std[l, r, :] = jnp.broadcast_to(inv, (ROWS, BLK))
            act[l, r, :] = (n * gain[l:l + 1, :]).astype(BF16)

            def up_chunk(j, c, l=l):
                cs = cols_of(j, CHUNK)
                v = dot(act[l, r, :], w_up[l, :, cs])
                pre[l, r, cs] = v
                hidden[l, r, cs] = gelu(v).astype(BF16)
                return c

            with jax.named_scope("f_up"):
                lax.fori_loop(0, FF // CHUNK, up_chunk, 0, unroll=UNROLL)

            def down_chunk(j, c, l=l):
                cs = cols_of(j, 256)
                v = dot(hidden[l, r, :], w_down[l, :, cs])
                had = xs[l, r, cs]
                moved = (had.astype(F32) + v).astype(BF16)
                xs[l + 1, r, cs] = jnp.where(flag(l), moved, had)
                return c

            with jax.named_scope("f_down"):
                lax.fori_loop(0, D // 256, down_chunk, 0, unroll=UNROLL)

        @pl.when(jnp.logical_not(last))
        def _():
            send_x(mb).start()

        return carry

    lax.fori_loop(0, MICRO, forward, 0)

    for l in range(LMAX):
        def slopes(j, c, l=l):
            cs = cols_of(j, BLK)
            pre[l, :, cs] = gelu_slope(pre[l, :, cs])
            h = jnp.where(flag(l), hidden[l, :, cs], jnp.zeros((KMAX, BLK), BF16))
            hidden_t[l, j] = h.T
            return c

        with jax.named_scope("slopes"):
            lax.fori_loop(0, FF // BLK, slopes, 0)

        def turn(j, c, l=l):
            a = jnp.where(flag(l), act[l, :, cols_of(j, BLK)], jnp.zeros((KMAX, BLK), BF16))
            act_t[l, j] = a.T
            return c

        with jax.named_scope("turn"):
            lax.fori_loop(0, D // BLK, turn, 0)

    def backward(mb, carry):
        r = rows_of(mb)

        @pl.when(jnp.logical_not(last))
        def _():
            send_g(mb).wait_recv()

        for l in reversed(range(LMAX)):
            def hidden_chunk(j, c, l=l):
                cs = cols_of(j, CHUNK)
                v = dot_t(gs[l + 1, r, :], w_down[l, cs, :])
                p = (pre[l, r, cs] * v).astype(BF16)
                grad_pre[l, r, cs] = p
                for b in range(CHUNK // BLK):
                    grad_pre_b[l, j * (CHUNK // BLK) + b, r, :] = p[:, b * BLK:(b + 1) * BLK]
                return c

            with jax.named_scope("b_down"):
                lax.fori_loop(0, FF // CHUNK, hidden_chunk, 0, unroll=UNROLL)

            def act_chunk(j, c, l=l):
                cs = cols_of(j, 256)
                v = dot_t(grad_pre[l, r, :], w_up[l, cs, :])
                pre[l, r, cs] = v * gain[l:l + 1, cs]
                return c

            with jax.named_scope("b_up"):
                lax.fori_loop(0, D // 256, act_chunk, 0, unroll=UNROLL)
            u = pre[l, r, :D]
            n = normed[l, r, :]
            step = inv_std[l, r, :1] * (
                u - jnp.mean(u, axis=-1, keepdims=True) - n * jnp.mean(u * n, axis=-1, keepdims=True)
            )
            had = gs[l + 1, r, :]
            for b in range(DOWN_COLS):
                gs_b[l, b, r, :] = had[:, b * BLK:(b + 1) * BLK]
            gs[l, r, :] = jnp.where(flag(l), (had.astype(F32) + step).astype(BF16), had)

        @pl.when(jnp.logical_not(first))
        def _():
            send_g(mb).start()

        return carry

    lax.fori_loop(0, MICRO, backward, 0)

    def store(i):
        l, kind = LMAX - 1 - i // 2, i % 2
        return pltpu.make_async_copy(packs[i % 2], out_hbm.at[l, pl.ds(kind * NDEAD, NDEAD)], out_sem.at[i])

    for i in range(PARTS):
        l, kind = LMAX - 1 - i // 2, i % 2
        if i >= 2:
            store(i - 2).wait()
        left, right = ((act_t, grad_pre_b), (hidden_t, gs_b))[kind]

        def one(k, c, l=l, kind=kind, left=left, right=right, i=i):
            where = (l * 2 + kind) * NDEAD + k
            v = dot(left[l, dead_row[where]], right[l, dead_col[where]])
            packs[i % 2][k] = v.astype(BF16)
            return c

        with jax.named_scope("grads"):
            lax.fori_loop(0, NDEAD, one, 0, unroll=4)
        store(i).start()
    for i in range(PARTS - 2, PARTS):
        store(i).wait()

    def drain(mb, carry):
        @pl.when(jnp.logical_not(last))
        def _():
            send_x(mb).wait_send()

        @pl.when(jnp.logical_not(first))
        def _():
            send_g(mb).wait_send()

        return carry

    lax.fori_loop(0, MICRO, drain, 0)


UNROLL = 1


def chain(inv, dead_row, dead_col, active, pick, patches, cotangent, gain, up, down):
    smem = pl.BlockSpec(memory_space=pltpu.SMEM)
    vmem = pl.BlockSpec(memory_space=pltpu.VMEM)
    hbm = pl.BlockSpec(memory_space=pl.ANY)
    return pl.pallas_call(
        chain_kernel,
        out_shape=jax.ShapeDtypeStruct((LMAX, 2 * NDEAD, BLK, BLK), BF16),
        in_specs=[smem] * 3 + [vmem] * 5 + [hbm] * 2,
        out_specs=hbm,
        scratch_shapes=[
            pltpu.VMEM((NDEAD, BLK, BLK), BF16),
            pltpu.VMEM((NDEAD, BLK, BLK), BF16),
            pltpu.VMEM((LMAX, D, FF), BF16),
            pltpu.VMEM((LMAX, FF, D), BF16),
            pltpu.VMEM((LMAX + 1, KMAX, D), BF16),
            pltpu.VMEM((LMAX + 1, KMAX, D), BF16),
            pltpu.VMEM((LMAX, KMAX, D), F32),
            pltpu.VMEM((LMAX, KMAX, BLK), F32),
            pltpu.VMEM((LMAX, KMAX, D), BF16),
            pltpu.VMEM((LMAX, KMAX, FF), BF16),
            pltpu.VMEM((LMAX, KMAX, FF), F32),
            pltpu.VMEM((LMAX, KMAX, FF), BF16),
            pltpu.VMEM((LMAX, D // BLK, BLK, KMAX), BF16),
            pltpu.VMEM((LMAX, FF // BLK, BLK, KMAX), BF16),
            pltpu.VMEM((LMAX, UP_COLS, KMAX, BLK), BF16),
            pltpu.VMEM((LMAX, DOWN_COLS, KMAX, BLK), BF16),
            pltpu.SemaphoreType.DMA((PARTS,)),
            pltpu.SemaphoreType.DMA((PARTS,)),
            pltpu.SemaphoreType.DMA((MICRO,)),
            pltpu.SemaphoreType.DMA((MICRO,)),
            pltpu.SemaphoreType.DMA((MICRO,)),
            pltpu.SemaphoreType.DMA((MICRO,)),
        ],
        compiler_params=pltpu.CompilerParams(
            collective_id=0, has_side_effects=True, vmem_limit_bytes=60 * 1024 * 1024
        ),
        cost_estimate=pl.CostEstimate(flops=35_000_000_000, bytes_accessed=30_000_000, transcendentals=2_000_000),
    )(inv, dead_row, dead_col, active, pick, patches, cotangent, gain, up, down)


def tables(up_index, down_index):
    listed = jnp.stack([up_index, down_index], axis=1).reshape(PARTS, NLIVE)
    hit = listed[:, :, None] == jnp.arange(NB)[None, None, :]
    live = jnp.any(hit, axis=1)
    inv = jnp.where(live, jnp.sum(jnp.where(hit, jnp.arange(NLIVE)[None, :, None], 0), axis=1), NLIVE)
    q = jnp.arange(NB)
    dead = jnp.logical_not(live)
    rank = jnp.sum((dead[:, :, None] & (q[:, None] < q[None, :])[None]).astype(jnp.int32), axis=1)
    k = jnp.arange(NDEAD)
    at = dead[:, None, :] & (rank[:, None, :] == k[None, :, None])
    number = jnp.sum(jnp.where(at, q[None, None, :], 0), axis=2)
    cols = jnp.array([UP_COLS, DOWN_COLS] * LMAX)[:, None]
    row = number // cols
    return inv.astype(jnp.int32), live, rank, row.astype(jnp.int32), (number - row * cols).astype(jnp.int32)
def body(patches, cotangent, keep_order, keep_count, destination, norm_gain, up_blocks, up_index, down_blocks, down_index, layer_count, regrow_mask):
    replicas = lax.axis_size("dp")
    replica_id = lax.axis_index("dp")
    inv, live, rank, row, col = tables(up_index, down_index)
    kept = jnp.where(jnp.arange(KMAX) < keep_count[0], keep_order[0, :KMAX], -1)
    pick = jnp.broadcast_to(kept[:, None], (KMAX, BLK)).astype(jnp.int32)
    active = jnp.broadcast_to((jnp.arange(8) < layer_count[0])[:, None], (8, BLK)).astype(jnp.int32)
    packed = chain(inv.reshape(-1), row.reshape(-1), col.reshape(-1), active, pick,
                   patches[0], cotangent[0], norm_gain, up_blocks, down_blocks)
    summed = lax.psum_scatter(packed, "dp", scatter_dimension=1, tiled=True).astype(F32)
    rows_total = float(replicas * KMAX)
    own = jnp.sqrt(jnp.mean(summed * summed, axis=(2, 3)) / rows_total + EPS_SCORE)
    every = lax.all_gather(own, "dp", axis=1, tiled=True)
    share = 2 * NB // replicas
    start = replica_id * share
    slot = rank.reshape(LMAX, 2, NB) + (jnp.arange(2) * NDEAD)[None, :, None]
    slot = lax.dynamic_slice_in_dim(slot.reshape(LMAX, 2 * NB), start, share, 1)
    alive = lax.dynamic_slice_in_dim(live.reshape(LMAX, 2 * NB), start, share, 1)
    picked = jnp.sum(jnp.where(slot[:, :, None] == jnp.arange(2 * NDEAD), every[:, None, :], 0.0), axis=2)
    eligible = jnp.logical_and(jnp.logical_not(alive), regrow_mask == 1)
    return jnp.where(eligible, picked, 0.0)


def solution(mesh):
    return jax.shard_map(
        body, mesh=mesh,
        in_specs=(
            P("dp", None, None), P("dp", None, None), P("dp", None), P("dp"), P("dp", None),
            P("section", None), P("section", None, None, None), P("section", None),
            P("section", None, None, None), P("section", None), P("section"), P("section", "dp"),
        ),
        out_specs=P("section", "dp"), check_vma=False,
    )
```

```python
import functools
import jax
import jax.numpy as jnp
from jax import lax
from jax.experimental import pallas as pl
from jax.experimental.pallas import tpu as pltpu
from jax.sharding import PartitionSpec as P

D = 1280
FF = 2560
BLK = 128
KMAX = 192
LMAX = 2
NB = 200
NLIVE = 96
NDEAD = NB - NLIVE
UP_COLS = FF // BLK
DOWN_COLS = D // BLK
PARTS = 2 * LMAX
PANELS = UP_COLS + DOWN_COLS
EPS_NORM = 1e-06
EPS_SCORE = 1e-06
MICRO = 2
ROWS = KMAX // MICRO
CHUNK = 512
MESH = pl.DeviceIdType.MESH
F32 = jnp.float32
BF16 = jnp.bfloat16
GELU_A = 0.7978845608028654
GELU_B = 0.044715


def dot(a, b):
    return jnp.dot(a, b, preferred_element_type=F32)


def dot_t(a, b):
    return lax.dot_general(a, b, (((1,), (1,)), ((), ())), preferred_element_type=F32)


def gelu(v):
    return 0.5 * v * (1.0 + jnp.tanh(GELU_A * (v + GELU_B * (v * v * v))))


def gelu_slope(v):
    sq = v * v
    t = jnp.tanh(GELU_A * (v + GELU_B * (v * sq)))
    return 0.5 * (1.0 + t) + 0.5 * v * (1.0 - t * t) * (GELU_A * (1.0 + 3.0 * GELU_B * sq))


def chain_kernel(
    inv_ref,
    active, pick_ref, patches, cotangent, gain, up_hbm, down_hbm,
    left_hbm, right_hbm,
    stage_a, stage_b, w_up, w_down, xs, gs, normed, inv_std, act, hidden, pre, grad_pre,
    left, right,
    stage_sem, left_sem, right_sem, x_send, x_recv, g_send, g_recv,
):
    sections = lax.axis_size("section")
    replica = lax.axis_index("dp")
    section = lax.axis_index("section")
    first = section == 0
    last = section == sections - 1
    stages = (stage_a, stage_b)

    def flag(l):
        return active[l:l + 1, :1] == 1

    def load(part):
        l, kind = part // 2, part % 2
        src = (up_hbm, down_hbm)[kind].at[l]
        return pltpu.make_async_copy(src, stages[part % 2].at[pl.ds(0, NLIVE)], stage_sem.at[part])

    stage_a[NLIVE] = jnp.zeros((BLK, BLK), BF16)
    stage_b[NLIVE] = jnp.zeros((BLK, BLK), BF16)
    load(0).start()
    load(1).start()

    barrier = pltpu.get_barrier_semaphore()

    @pl.when(jnp.logical_not(first))
    def _():
        pl.semaphore_signal(barrier, inc=1, device_id=(replica, section - 1), device_id_type=MESH)

    @pl.when(jnp.logical_not(last))
    def _():
        pl.semaphore_signal(barrier, inc=1, device_id=(replica, section + 1), device_id_type=MESH)

    @pl.when(jnp.logical_or(first, last))
    def _():
        pl.semaphore_wait(barrier, 1)

    @pl.when(jnp.logical_not(jnp.logical_or(first, last)))
    def _():
        pl.semaphore_wait(barrier, 2)

    def picked(table):
        hot = pick_ref[:, :1] == lax.broadcasted_iota(jnp.int32, (KMAX, table.shape[0]), 1)
        return dot(hot.astype(BF16), table[...]).astype(BF16)

    @pl.when(first)
    def _():
        xs[0] = picked(patches)

    @pl.when(last)
    def _():
        gs[LMAX] = picked(cotangent)

    for part in range(PARTS):
        load(part).wait()
        l, kind = part // 2, part % 2
        target, cols = ((w_up, UP_COLS), (w_down, DOWN_COLS))[kind]

        def place(q, carry, l=l, target=target, cols=cols, part=part):
            rb = q // cols
            cb = q - rb * cols
            target[
                l,
                pl.ds(pl.multiple_of(rb * BLK, BLK), BLK),
                pl.ds(pl.multiple_of(cb * BLK, BLK), BLK),
            ] = stages[part % 2][inv_ref[part * NB + q]]
            return carry

        lax.fori_loop(0, NB, place, 0, unroll=4)
        if part + 2 < PARTS:
            load(part + 2).start()

    def rows_of(mb):
        return pl.ds(pl.multiple_of(mb * ROWS, ROWS), ROWS)

    def cols_of(j, size):
        return pl.ds(pl.multiple_of(j * size, size), size)

    def send_x(mb):
        return pltpu.make_async_remote_copy(
            src_ref=xs.at[LMAX, rows_of(mb)], dst_ref=xs.at[0, rows_of(mb)],
            send_sem=x_send.at[mb], recv_sem=x_recv.at[mb],
            device_id=(replica, section + 1), device_id_type=MESH,
        )

    def send_g(mb):
        return pltpu.make_async_remote_copy(
            src_ref=gs.at[0, rows_of(mb)], dst_ref=gs.at[LMAX, rows_of(mb)],
            send_sem=g_send.at[mb], recv_sem=g_recv.at[mb],
            device_id=(replica, section - 1), device_id_type=MESH,
        )

    def forward(mb, carry):
        r = rows_of(mb)

        @pl.when(jnp.logical_not(first))
        def _():
            send_x(mb).wait_recv()

        for l in range(LMAX):
            x = xs[l, r, :].astype(F32)
            centred = x - jnp.mean(x, axis=-1, keepdims=True)
            inv = lax.rsqrt(jnp.mean(centred * centred, axis=-1, keepdims=True) + EPS_NORM)
            n = centred * inv
            normed[l, r, :] = n
            inv_std[l, r, :] = jnp.broadcast_to(inv, (ROWS, BLK))
            act[l, r, :] = (n * gain[l:l + 1, :]).astype(BF16)

            def up_chunk(j, c, l=l):
                cs = cols_of(j, CHUNK)
                v = dot(act[l, r, :], w_up[l, :, cs])
                pre[l, r, cs] = v
                hidden[l, r, cs] = gelu(v).astype(BF16)
                return c

            lax.fori_loop(0, FF // CHUNK, up_chunk, 0, unroll=UNROLL)

            def down_chunk(j, c, l=l):
                cs = cols_of(j, 256)
                v = dot(hidden[l, r, :], w_down[l, :, cs])
                had = xs[l, r, cs]
                moved = (had.astype(F32) + v).astype(BF16)
                xs[l + 1, r, cs] = jnp.where(flag(l), moved, had)
                return c

            lax.fori_loop(0, D // 256, down_chunk, 0, unroll=UNROLL)

        @pl.when(jnp.logical_not(last))
        def _():
            send_x(mb).start()

        return carry

    lax.fori_loop(0, MICRO, forward, 0)

    def save_left(l):
        return pltpu.make_async_copy(left.at[l], left_hbm.at[l], left_sem.at[l])

    for l in range(LMAX):
        def slopes(j, c, l=l):
            cs = cols_of(j, BLK)
            pre[l, :, cs] = gelu_slope(pre[l, :, cs])
            h = jnp.where(flag(l), hidden[l, :, cs], jnp.zeros((KMAX, BLK), BF16))
            left[l, DOWN_COLS + j] = h.T
            return c

        lax.fori_loop(0, FF // BLK, slopes, 0)

        def turn(j, c, l=l):
            a = jnp.where(flag(l), act[l, :, cols_of(j, BLK)], jnp.zeros((KMAX, BLK), BF16))
            left[l, j] = a.T
            return c

        lax.fori_loop(0, D // BLK, turn, 0)
        save_left(l).start()

    def save_right(l):
        return pltpu.make_async_copy(right.at[l], right_hbm.at[l], right_sem.at[l])

    def backward(mb, carry):
        r = rows_of(mb)

        @pl.when(jnp.logical_not(last))
        def _():
            send_g(mb).wait_recv()

        for l in reversed(range(LMAX)):
            def hidden_chunk(j, c, l=l):
                cs = cols_of(j, CHUNK)
                v = dot_t(gs[l + 1, r, :], w_down[l, cs, :])
                p = (pre[l, r, cs] * v).astype(BF16)
                grad_pre[l, r, cs] = p
                for b in range(CHUNK // BLK):
                    right[l, j * (CHUNK // BLK) + b, r, :] = p[:, b * BLK:(b + 1) * BLK]
                return c

            lax.fori_loop(0, FF // CHUNK, hidden_chunk, 0, unroll=UNROLL)

            def act_chunk(j, c, l=l):
                cs = cols_of(j, 256)
                v = dot_t(grad_pre[l, r, :], w_up[l, cs, :])
                pre[l, r, cs] = v * gain[l:l + 1, cs]
                return c

            lax.fori_loop(0, D // 256, act_chunk, 0, unroll=UNROLL)
            u = pre[l, r, :D]
            n = normed[l, r, :]
            step = inv_std[l, r, :1] * (
                u - jnp.mean(u, axis=-1, keepdims=True) - n * jnp.mean(u * n, axis=-1, keepdims=True)
            )
            had = gs[l + 1, r, :]
            for b in range(DOWN_COLS):
                right[l, UP_COLS + b, r, :] = had[:, b * BLK:(b + 1) * BLK]
            gs[l, r, :] = jnp.where(flag(l), (had.astype(F32) + step).astype(BF16), had)

        @pl.when(jnp.logical_not(first))
        def _():
            send_g(mb).start()

        return carry

    lax.fori_loop(0, MICRO, backward, 0)

    for l in range(LMAX):
        save_right(l).start()

    def drain(mb, carry):
        @pl.when(jnp.logical_not(last))
        def _():
            send_x(mb).wait_send()

        @pl.when(jnp.logical_not(first))
        def _():
            send_g(mb).wait_send()

        return carry

    lax.fori_loop(0, MICRO, drain, 0)
    for l in range(LMAX):
        save_left(l).wait()
        save_right(l).wait()


UNROLL = True


def chain(inv, active, pick, patches, cotangent, gain, up, down):
    smem = pl.BlockSpec(memory_space=pltpu.SMEM)
    vmem = pl.BlockSpec(memory_space=pltpu.VMEM)
    hbm = pl.BlockSpec(memory_space=pl.ANY)
    return pl.pallas_call(
        chain_kernel,
        out_shape=(
            jax.ShapeDtypeStruct((LMAX, PANELS, BLK, KMAX), BF16),
            jax.ShapeDtypeStruct((LMAX, PANELS, KMAX, BLK), BF16),
        ),
        in_specs=[smem] + [vmem] * 5 + [hbm] * 2,
        out_specs=(hbm, hbm),
        scratch_shapes=[
            pltpu.VMEM((NLIVE + 1, BLK, BLK), BF16),
            pltpu.VMEM((NLIVE + 1, BLK, BLK), BF16),
            pltpu.VMEM((LMAX, D, FF), BF16),
            pltpu.VMEM((LMAX, FF, D), BF16),
            pltpu.VMEM((LMAX + 1, KMAX, D), BF16),
            pltpu.VMEM((LMAX + 1, KMAX, D), BF16),
            pltpu.VMEM((LMAX, KMAX, D), F32),
            pltpu.VMEM((LMAX, KMAX, BLK), F32),
            pltpu.VMEM((LMAX, KMAX, D), BF16),
            pltpu.VMEM((LMAX, KMAX, FF), BF16),
            pltpu.VMEM((LMAX, KMAX, FF), F32),
            pltpu.VMEM((LMAX, KMAX, FF), BF16),
            pltpu.VMEM((LMAX, PANELS, BLK, KMAX), BF16),
            pltpu.VMEM((LMAX, PANELS, KMAX, BLK), BF16),
            pltpu.SemaphoreType.DMA((PARTS,)),
            pltpu.SemaphoreType.DMA((LMAX,)),
            pltpu.SemaphoreType.DMA((LMAX,)),
            pltpu.SemaphoreType.DMA((MICRO,)),
            pltpu.SemaphoreType.DMA((MICRO,)),
            pltpu.SemaphoreType.DMA((MICRO,)),
            pltpu.SemaphoreType.DMA((MICRO,)),
        ],
        compiler_params=pltpu.CompilerParams(
            collective_id=0, has_side_effects=True, vmem_limit_bytes=60 * 1024 * 1024
        ),
        cost_estimate=pl.CostEstimate(flops=35_000_000_000, bytes_accessed=30_000_000, transcendentals=2_000_000),
    )(inv, active, pick, patches, cotangent, gain, up, down)


def tables(up_index, down_index):
    listed = jnp.stack([up_index, down_index], axis=1).reshape(PARTS, NLIVE)
    hit = listed[:, :, None] == jnp.arange(NB)[None, None, :]
    live = jnp.any(hit, axis=1)
    inv = jnp.where(live, jnp.sum(jnp.where(hit, jnp.arange(NLIVE)[None, :, None], 0), axis=1), NLIVE)
    q = jnp.arange(NB)
    dead = jnp.logical_not(live)
    rank = jnp.sum((dead[:, :, None] & (q[:, None] < q[None, :])[None]).astype(jnp.int32), axis=1)
    k = jnp.arange(NDEAD)
    at = dead[:, None, :] & (rank[:, None, :] == k[None, :, None])
    number = jnp.sum(jnp.where(at, q[None, None, :], 0), axis=2)
    cols = jnp.array([UP_COLS, DOWN_COLS] * LMAX)[:, None]
    row = number // cols
    col = number - row * cols
    base = jnp.arange(PARTS)[:, None] % 2
    row = (row + base * DOWN_COLS).astype(jnp.int32)
    col = (col + base * UP_COLS).astype(jnp.int32)
    return inv.astype(jnp.int32), live, rank, row, col


RING = 4
PER = 2 * NDEAD // (RING * RING)
HALF = BLK // 2
TILE = 32


def sums_kernel(
    dead_row, dead_col, left_hbm, right_hbm, out_ref,
    left_0, left_1, right_0, right_1,
    opp_0, opp_1, nxt_0, nxt_1, prv_0, prv_1, mid_0, mid_1,
    ra_0, ra_1, rb_0, rb_1, ia_0, ia_1, ib_0, ib_1,
    sa_0, sa_1, sb_0, sb_1, ja_0, ja_1, jb_0, jb_1,
    squares, mine, row_tiles, all_tiles,
    load_sem, send_sem, recv_sem, tile_send, tile_recv, full_send, full_recv,
):
    section = lax.axis_index("section")
    replica = lax.axis_index("dp")
    px = replica // RING
    py = lax.rem(replica, RING)

    def peer(axis, step):
        if axis == 0:
            return (lax.rem(px + step, RING) * RING + py, section)
        return (px * RING + lax.rem(py + step, RING), section)

    lefts, rights = (left_1, left_0), (right_1, right_0)

    def load(h):
        l = LMAX - 1 - h
        return (
            pltpu.make_async_copy(left_hbm.at[l], lefts[h], load_sem.at[h, 0]),
            pltpu.make_async_copy(right_hbm.at[l], rights[h], load_sem.at[h, 1]),
        )

    for h in range(2):
        for copy in load(h):
            copy.start()

    barrier = pltpu.get_barrier_semaphore()
    for axis in range(2):
        for step in range(1, RING):
            pl.semaphore_signal(barrier, inc=1, device_id=peer(axis, step), device_id_type=MESH)
    pl.semaphore_wait(barrier, 2 * (RING - 1))
    for h in range(2):
        for copy in load(h):
            copy.wait()

    opp, nxt, prv, mid = (opp_0, opp_1), (nxt_0, nxt_1), (prv_0, prv_1), (mid_0, mid_1)
    ra, rb, ia, ib = (ra_0, ra_1), (rb_0, rb_1), (ia_0, ia_1), (ib_0, ib_1)
    sa, sb, ja, jb = (sa_0, sa_1), (sb_0, sb_1), (ja_0, ja_1), (jb_0, jb_1)
    place = (px, py)

    def at(axis, step):
        return lax.rem(place[axis] + step, RING)

    def block(h, f, c, g):
        where = (LMAX - 1 - h) * 2 * NDEAD + (f * PER + c) * RING + g
        return dot(lefts[h][dead_row[where]], rights[h][dead_col[where]])

    def send(h, kind, c, src, dst, axis, step):
        return pltpu.make_async_remote_copy(
            src_ref=src, dst_ref=dst, send_sem=send_sem.at[h, kind, c], recv_sem=recv_sem.at[h, kind, c],
            device_id=peer(axis, step), device_id_type=MESH,
        )

    def copies(h, c):
        first, second = h, 1 - h
        far = at(second, 2)
        return (
            send(h, 0, c, opp[h].at[c, pl.ds(0, 2)], ra[h].at[c], first, 1),
            send(h, 1, c, opp[h].at[c, pl.ds(2, 2)], rb[h].at[c], first, 3),
            send(h, 2, c, nxt[h].at[c], ia[h].at[c], first, 1),
            send(h, 3, c, prv[h].at[c], ib[h].at[c], first, 3),
            send(h, 4, c, mid[h].at[c, far, pl.ds(0, HALF)], sa[h].at[c], second, 1),
            send(h, 5, c, mid[h].at[c, far, pl.ds(HALF, HALF)], sb[h].at[c], second, 3),
            send(h, 6, c, mid[h].at[c, at(second, 1)], ja[h].at[c], second, 1),
            send(h, 7, c, mid[h].at[c, at(second, 3)], jb[h].at[c], second, 3),
        )

    def far_units(c, carry):
        for h in range(2):
            for g in range(RING):
                opp[h][c, g] = block(h, at(h, 2), c, g).astype(BF16)
            moves = copies(h, c)
            moves[0].start()
            moves[1].start()
        return carry

    def near_units(c, carry):
        for h in range(2):
            moves = copies(h, c)
            ahead = [block(h, at(h, 1), c, g) for g in range(RING)]
            behind = [block(h, at(h, 3), c, g) for g in range(RING)]
            moves[0].wait_recv()
            for g in range(RING):
                v = ahead[g] + ra[h][c, g].astype(F32) if g < 2 else ahead[g]
                nxt[h][c, g] = v.astype(BF16)
            moves[2].start()
            moves[1].wait_recv()
            for g in range(RING):
                v = behind[g] + rb[h][c, g - 2].astype(F32) if g >= 2 else behind[g]
                prv[h][c, g] = v.astype(BF16)
            moves[3].start()
        return carry

    def own_units(c, carry):
        for h in range(2):
            moves = copies(h, c)
            own = [block(h, place[h], c, g) for g in range(RING)]
            moves[2].wait_recv()
            moves[3].wait_recv()
            for g in range(RING):
                v = own[g] + ia[h][c, g].astype(F32) + ib[h][c, g].astype(F32)
                mid[h][c, g] = v.astype(BF16)
            moves[4].start()
            moves[5].start()
        return carry

    def second_axis(c, carry):
        for h in range(2):
            moves = copies(h, c)
            ahead, behind = at(1 - h, 1), at(1 - h, 3)
            moves[4].wait_recv()
            top = pl.ds(0, HALF)
            v = mid[h][c, ahead, top, :].astype(F32) + sa[h][c].astype(F32)
            mid[h][c, ahead, top, :] = v.astype(BF16)
            moves[6].start()
            moves[5].wait_recv()
            low = pl.ds(HALF, HALF)
            v = mid[h][c, behind, low, :].astype(F32) + sb[h][c].astype(F32)
            mid[h][c, behind, low, :] = v.astype(BF16)
            moves[7].start()
        return carry

    def totals(c, carry):
        for h in range(2):
            moves = copies(h, c)
            moves[6].wait_recv()
            moves[7].wait_recv()
            v = mid[h][c, place[1 - h]].astype(F32) + ja[h][c].astype(F32) + jb[h][c].astype(F32)
            squares[h, pl.ds(c, 1), :] = jnp.sum(v * v, axis=0, keepdims=True)
        return carry

    def drain(c, carry):
        for h in range(2):
            for move in copies(h, c):
                move.wait_send()
        return carry

    squares[...] = jnp.zeros_like(squares)
    for step in (far_units, near_units, own_units, second_axis, totals):
        lax.fori_loop(0, PER, step, 0)
    rows_total = float(RING * RING * KMAX)
    mean = jnp.sum(squares[...].reshape(TILE, BLK), axis=1, keepdims=True) * (1.0 / (BLK * BLK))
    mine[...] = jnp.broadcast_to(jnp.sqrt(mean / rows_total + EPS_SCORE), (TILE, BLK))

    row_tiles[px] = mine[...]
    rows = [
        pltpu.make_async_remote_copy(
            src_ref=mine, dst_ref=row_tiles.at[px], send_sem=tile_send.at[step - 1],
            recv_sem=tile_recv.at[step - 1], device_id=peer(0, step), device_id_type=MESH,
        )
        for step in range(1, RING)
    ]
    for move in rows:
        move.start()
    for move in rows:
        move.wait()
    all_tiles[py] = row_tiles[...]
    cols = [
        pltpu.make_async_remote_copy(
            src_ref=row_tiles, dst_ref=all_tiles.at[py], send_sem=full_send.at[step - 1],
            recv_sem=full_recv.at[step - 1], device_id=peer(1, step), device_id_type=MESH,
        )
        for step in range(1, RING)
    ]
    for move in cols:
        move.start()
    for move in cols:
        move.wait()
    out_ref[...] = all_tiles[...]
    lax.fori_loop(0, PER, drain, 0)


def sums(dead_row, dead_col, left, right):
    smem = pl.BlockSpec(memory_space=pltpu.SMEM)
    hbm = pl.BlockSpec(memory_space=pl.ANY)

    def blocks(*lead):
        return [pltpu.VMEM((PER, *lead, BLK), BF16)] * 2

    return pl.pallas_call(
        sums_kernel,
        out_shape=jax.ShapeDtypeStruct((RING, RING, TILE, BLK), F32),
        in_specs=[smem] * 2 + [hbm] * 2,
        out_specs=pl.BlockSpec(memory_space=pltpu.VMEM),
        scratch_shapes=[
            *[pltpu.VMEM((PANELS, BLK, KMAX), BF16)] * 2,
            *[pltpu.VMEM((PANELS, KMAX, BLK), BF16)] * 2,
            *blocks(RING, BLK), *blocks(RING, BLK), *blocks(RING, BLK), *blocks(RING, BLK),
            *blocks(2, BLK), *blocks(2, BLK), *blocks(RING, BLK), *blocks(RING, BLK),
            *blocks(HALF), *blocks(HALF), *blocks(BLK), *blocks(BLK),
            pltpu.VMEM((2, TILE // 2, BLK), F32),
            pltpu.VMEM((TILE, BLK), F32),
            pltpu.VMEM((RING, TILE, BLK), F32),
            pltpu.VMEM((RING, RING, TILE, BLK), F32),
            pltpu.SemaphoreType.DMA((2, 2)),
            pltpu.SemaphoreType.DMA((2, 8, PER)),
            pltpu.SemaphoreType.DMA((2, 8, PER)),
            *[pltpu.SemaphoreType.DMA((RING - 1,))] * 4,
        ],
        compiler_params=pltpu.CompilerParams(
            collective_id=1, has_side_effects=True, vmem_limit_bytes=60 * 1024 * 1024
        ),
        cost_estimate=pl.CostEstimate(flops=3_000_000_000, bytes_accessed=8_000_000, transcendentals=0),
    )(dead_row, dead_col, left, right)


def body(patches, cotangent, keep_order, keep_count, destination, norm_gain, up_blocks, up_index,
         down_blocks, down_index, layer_count, regrow_mask):
    replicas = lax.axis_size("dp")
    replica_id = lax.axis_index("dp")
    inv, live, rank, row, col = tables(up_index, down_index)
    kept = jnp.where(jnp.arange(KMAX) < keep_count[0], keep_order[0, :KMAX], -1)
    pick = jnp.broadcast_to(kept[:, None], (KMAX, BLK)).astype(jnp.int32)
    active = jnp.broadcast_to((jnp.arange(8) < layer_count[0])[:, None], (8, BLK)).astype(jnp.int32)
    left, right = chain(inv.reshape(-1), active, pick, patches[0], cotangent[0], norm_gain, up_blocks, down_blocks)
    tiles = sums(row.reshape(-1), col.reshape(-1), left, right)
    half = TILE // 2
    late = tiles[:, :, :PER, 0].transpose(1, 2, 0).reshape(2 * NDEAD)
    early = tiles[:, :, half:half + PER, 0].transpose(0, 2, 1).reshape(2 * NDEAD)
    every = jnp.stack([early, late])
    share = 2 * NB // replicas
    start = replica_id * share
    slot = rank.reshape(LMAX, 2, NB) + (jnp.arange(2) * NDEAD)[None, :, None]
    slot = lax.dynamic_slice_in_dim(slot.reshape(LMAX, 2 * NB), start, share, 1)
    alive = lax.dynamic_slice_in_dim(live.reshape(LMAX, 2 * NB), start, share, 1)
    picked = jnp.sum(jnp.where(slot[:, :, None] == jnp.arange(2 * NDEAD), every[:, None, :], 0.0), axis=2)
    eligible = jnp.logical_and(jnp.logical_not(alive), regrow_mask == 1)
    return jnp.where(eligible, picked, 0.0)


def solution(mesh):
    return jax.shard_map(
        body, mesh=mesh,
        in_specs=(
            P("dp", None, None), P("dp", None, None), P("dp", None), P("dp"), P("dp", None),
            P("section", None), P("section", None, None, None), P("section", None),
            P("section", None, None, None), P("section", None), P("section"), P("section", "dp"),
        ),
        out_specs=P("section", "dp"), check_vma=False,
    )
```

```python
import functools
import jax
import jax.numpy as jnp
from jax import lax
from jax.experimental import pallas as pl
from jax.experimental.pallas import tpu as pltpu
from jax.sharding import PartitionSpec as P

D = 1280
FF = 2560
BLK = 128
KMAX = 192
LMAX = 2
NB = 200
NLIVE = 96
NDEAD = NB - NLIVE
UP_COLS = FF // BLK
DOWN_COLS = D // BLK
PARTS = 2 * LMAX
PANELS = UP_COLS + DOWN_COLS
EPS_NORM = 1e-06
EPS_SCORE = 1e-06
MICRO = 2
ROWS = KMAX // MICRO
CHUNK = 512
SQ = 256
MESH = pl.DeviceIdType.MESH
F32 = jnp.float32
BF16 = jnp.bfloat16
GELU_A = 0.7978845608028654
GELU_B = 0.044715


def dot(a, b):
    return jnp.dot(a, b, preferred_element_type=F32)


def dot_t(a, b):
    return lax.dot_general(a, b, (((1,), (1,)), ((), ())), preferred_element_type=F32)


def gelu(v):
    return 0.5 * v * (1.0 + jnp.tanh(GELU_A * (v + GELU_B * (v * v * v))))


def gelu_slope(v):
    sq = v * v
    t = jnp.tanh(GELU_A * (v + GELU_B * (v * sq)))
    return 0.5 * (1.0 + t) + 0.5 * v * (1.0 - t * t) * (GELU_A * (1.0 + 3.0 * GELU_B * sq))


def chain_kernel(
    inv_ref,
    active, pick_ref, patches, cotangent, gain, up_hbm, down_hbm,
    left_hbm, right_hbm,
    stage_a, stage_b, up_0, up_1, down_0, down_1, spare, xs, gs, normed, inv_std, act, hidden, pre, grad_pre,
    left, right,
    stage_sem, left_sem, right_sem, x_send, x_recv, g_send, g_recv,
):
    sections = lax.axis_size("section")
    replica = lax.axis_index("dp")
    section = lax.axis_index("section")
    first = section == 0
    last = section == sections - 1
    stages = (stage_a, stage_b)
    w_up, w_down = (up_0, up_1), (down_0, down_1)
    w_up_t, w_down_t = (down_0, down_1), (up_1, spare)

    def flag(l):
        return active[l:l + 1, :1] == 1

    def load(part):
        l, kind = part // 2, part % 2
        src = (up_hbm, down_hbm)[kind].at[l]
        return pltpu.make_async_copy(src, stages[part % 2].at[pl.ds(0, NLIVE)], stage_sem.at[part])

    stage_a[NLIVE] = jnp.zeros((BLK, BLK), BF16)
    stage_b[NLIVE] = jnp.zeros((BLK, BLK), BF16)
    load(0).start()
    load(1).start()

    barrier = pltpu.get_barrier_semaphore()

    @pl.when(jnp.logical_not(first))
    def _():
        pl.semaphore_signal(barrier, inc=1, device_id=(replica, section - 1), device_id_type=MESH)

    @pl.when(jnp.logical_not(last))
    def _():
        pl.semaphore_signal(barrier, inc=1, device_id=(replica, section + 1), device_id_type=MESH)

    @pl.when(jnp.logical_or(first, last))
    def _():
        pl.semaphore_wait(barrier, 1)

    @pl.when(jnp.logical_not(jnp.logical_or(first, last)))
    def _():
        pl.semaphore_wait(barrier, 2)

    def picked(table):
        hot = pick_ref[:, :1] == lax.broadcasted_iota(jnp.int32, (KMAX, table.shape[0]), 1)
        return dot(hot.astype(BF16), table[...]).astype(BF16)

    @pl.when(first)
    def _():
        xs[0] = picked(patches)

    @pl.when(last)
    def _():
        gs[LMAX] = picked(cotangent)

    for part in range(PARTS):
        load(part).wait()
        l, kind = part // 2, part % 2
        target, cols = ((w_up, UP_COLS), (w_down, DOWN_COLS))[kind]

        def place(rb, carry, l=l, target=target, cols=cols, part=part):
            rs = pl.ds(pl.multiple_of(rb * BLK, BLK), BLK)
            for cb in range(cols):
                target[l][rs, cb * BLK:(cb + 1) * BLK] = stages[part % 2][inv_ref[part * NB + rb * cols + cb]]
            return carry

        lax.fori_loop(0, NB // cols, place, 0)
        if part + 2 < PARTS:
            load(part + 2).start()

    def rows_of(mb):
        return pl.ds(pl.multiple_of(mb * ROWS, ROWS), ROWS)

    def cols_of(j, size):
        return pl.ds(pl.multiple_of(j * size, size), size)

    def send_x(mb):
        return pltpu.make_async_remote_copy(
            src_ref=xs.at[LMAX, rows_of(mb)], dst_ref=xs.at[0, rows_of(mb)],
            send_sem=x_send.at[mb], recv_sem=x_recv.at[mb],
            device_id=(replica, section + 1), device_id_type=MESH,
        )

    def send_g(mb):
        return pltpu.make_async_remote_copy(
            src_ref=gs.at[0, rows_of(mb)], dst_ref=gs.at[LMAX, rows_of(mb)],
            send_sem=g_send.at[mb], recv_sem=g_recv.at[mb],
            device_id=(replica, section - 1), device_id_type=MESH,
        )

    def forward(mb, carry):
        r = rows_of(mb)

        @pl.when(jnp.logical_not(first))
        def _():
            send_x(mb).wait_recv()

        for l in range(LMAX):
            x = xs[l, r, :].astype(F32)
            centred = x - jnp.mean(x, axis=-1, keepdims=True)
            inv = lax.rsqrt(jnp.mean(centred * centred, axis=-1, keepdims=True) + EPS_NORM)
            n = centred * inv
            normed[l, r, :] = n
            inv_std[l, r, :] = jnp.broadcast_to(inv, (ROWS, BLK))
            act[l, r, :] = (n * gain[l:l + 1, :]).astype(BF16)

            def up_chunk(j, c, l=l):
                cs = cols_of(j, CHUNK)
                v = dot(act[l, r, :], w_up[l][:, cs])
                pre[l, r, cs] = v
                hidden[l, r, cs] = gelu(v).astype(BF16)
                return c

            lax.fori_loop(0, FF // CHUNK, up_chunk, 0, unroll=True)

            def down_chunk(j, c, l=l):
                cs = cols_of(j, 256)
                v = dot(hidden[l, r, :], w_down[l][:, cs])
                had = xs[l, r, cs]
                moved = (had.astype(F32) + v).astype(BF16)
                xs[l + 1, r, cs] = jnp.where(flag(l), moved, had)
                return c

            lax.fori_loop(0, D // 256, down_chunk, 0, unroll=True)

        @pl.when(jnp.logical_not(last))
        def _():
            send_x(mb).start()

        return carry

    lax.fori_loop(0, MICRO, forward, 0)

    def save_left(l):
        return pltpu.make_async_copy(left.at[l], left_hbm.at[l], left_sem.at[l])

    for l in range(LMAX):
        def slopes(j, c, l=l):
            cs = cols_of(j, BLK)
            pre[l, :, cs] = gelu_slope(pre[l, :, cs])
            h = jnp.where(flag(l), hidden[l, :, cs], jnp.zeros((KMAX, BLK), BF16))
            left[l, DOWN_COLS + j] = h.T
            return c

        lax.fori_loop(0, FF // BLK, slopes, 0)

        def turn(j, c, l=l):
            a = jnp.where(flag(l), act[l, :, cols_of(j, BLK)], jnp.zeros((KMAX, BLK), BF16))
            left[l, j] = a.T
            return c

        lax.fori_loop(0, D // BLK, turn, 0)
        save_left(l).start()

    unit = (
        lax.broadcasted_iota(jnp.int32, (SQ, SQ), 0) == lax.broadcasted_iota(jnp.int32, (SQ, SQ), 1)
    ).astype(BF16)
    for source, target in ((down_1, spare), (up_1, down_1), (down_0, up_1), (up_0, down_0)):
        def flip(i, c, source=source, target=target):
            rs = cols_of(i, SQ)
            for j in range(source.shape[1] // SQ):
                tile = source[rs, j * SQ:(j + 1) * SQ]
                target[j * SQ:(j + 1) * SQ, rs] = dot_t(unit, tile).astype(BF16)
            return c

        lax.fori_loop(0, source.shape[0] // SQ, flip, 0)

    def save_right(l):
        return pltpu.make_async_copy(right.at[l], right_hbm.at[l], right_sem.at[l])

    def backward(mb, carry):
        r = rows_of(mb)

        @pl.when(jnp.logical_not(last))
        def _():
            send_g(mb).wait_recv()

        for l in reversed(range(LMAX)):
            def hidden_chunk(j, c, l=l):
                cs = cols_of(j, CHUNK)
                v = dot(gs[l + 1, r, :], w_down_t[l][:, cs])
                p = (pre[l, r, cs] * v).astype(BF16)
                grad_pre[l, r, cs] = p
                for b in range(CHUNK // BLK):
                    right[l, j * (CHUNK // BLK) + b, r, :] = p[:, b * BLK:(b + 1) * BLK]
                return c

            lax.fori_loop(0, FF // CHUNK, hidden_chunk, 0, unroll=True)

            def act_chunk(j, c, l=l):
                cs = cols_of(j, 256)
                v = dot(grad_pre[l, r, :], w_up_t[l][:, cs])
                pre[l, r, cs] = v * gain[l:l + 1, cs]
                return c

            lax.fori_loop(0, D // 256, act_chunk, 0, unroll=True)
            u = pre[l, r, :D]
            n = normed[l, r, :]
            step = inv_std[l, r, :1] * (
                u - jnp.mean(u, axis=-1, keepdims=True) - n * jnp.mean(u * n, axis=-1, keepdims=True)
            )
            had = gs[l + 1, r, :]
            for b in range(DOWN_COLS):
                right[l, UP_COLS + b, r, :] = had[:, b * BLK:(b + 1) * BLK]
            gs[l, r, :] = jnp.where(flag(l), (had.astype(F32) + step).astype(BF16), had)

        @pl.when(jnp.logical_not(first))
        def _():
            send_g(mb).start()

        return carry

    lax.fori_loop(0, MICRO, backward, 0)

    for l in range(LMAX):
        save_right(l).start()

    def drain(mb, carry):
        @pl.when(jnp.logical_not(last))
        def _():
            send_x(mb).wait_send()

        @pl.when(jnp.logical_not(first))
        def _():
            send_g(mb).wait_send()

        return carry

    lax.fori_loop(0, MICRO, drain, 0)
    for l in range(LMAX):
        save_left(l).wait()
        save_right(l).wait()


def chain(inv, active, pick, patches, cotangent, gain, up, down):
    smem = pl.BlockSpec(memory_space=pltpu.SMEM)
    vmem = pl.BlockSpec(memory_space=pltpu.VMEM)
    hbm = pl.BlockSpec(memory_space=pl.ANY)
    return pl.pallas_call(
        chain_kernel,
        out_shape=(
            jax.ShapeDtypeStruct((LMAX, PANELS, BLK, KMAX), BF16),
            jax.ShapeDtypeStruct((LMAX, PANELS, KMAX, BLK), BF16),
        ),
        in_specs=[smem] + [vmem] * 5 + [hbm] * 2,
        out_specs=(hbm, hbm),
        scratch_shapes=[
            pltpu.VMEM((NLIVE + 1, BLK, BLK), BF16),
            pltpu.VMEM((NLIVE + 1, BLK, BLK), BF16),
            *[pltpu.VMEM((D, FF), BF16)] * 2,
            *[pltpu.VMEM((FF, D), BF16)] * 2,
            pltpu.VMEM((D, FF), BF16),
            pltpu.VMEM((LMAX + 1, KMAX, D), BF16),
            pltpu.VMEM((LMAX + 1, KMAX, D), BF16),
            pltpu.VMEM((LMAX, KMAX, D), F32),
            pltpu.VMEM((LMAX, KMAX, BLK), F32),
            pltpu.VMEM((LMAX, KMAX, D), BF16),
            pltpu.VMEM((LMAX, KMAX, FF), BF16),
            pltpu.VMEM((LMAX, KMAX, FF), F32),
            pltpu.VMEM((LMAX, KMAX, FF), BF16),
            pltpu.VMEM((LMAX, PANELS, BLK, KMAX), BF16),
            pltpu.VMEM((LMAX, PANELS, KMAX, BLK), BF16),
            pltpu.SemaphoreType.DMA((PARTS,)),
            pltpu.SemaphoreType.DMA((LMAX,)),
            pltpu.SemaphoreType.DMA((LMAX,)),
            pltpu.SemaphoreType.DMA((MICRO,)),
            pltpu.SemaphoreType.DMA((MICRO,)),
            pltpu.SemaphoreType.DMA((MICRO,)),
            pltpu.SemaphoreType.DMA((MICRO,)),
        ],
        compiler_params=pltpu.CompilerParams(
            collective_id=0, has_side_effects=True, vmem_limit_bytes=60 * 1024 * 1024
        ),
        cost_estimate=pl.CostEstimate(flops=35_000_000_000, bytes_accessed=30_000_000, transcendentals=2_000_000),
    )(inv, active, pick, patches, cotangent, gain, up, down)


def tables(up_index, down_index):
    listed = jnp.stack([up_index, down_index], axis=1).reshape(PARTS, NLIVE)
    hit = listed[:, :, None] == jnp.arange(NB)[None, None, :]
    live = jnp.any(hit, axis=1)
    inv = jnp.where(live, jnp.sum(jnp.where(hit, jnp.arange(NLIVE)[None, :, None], 0), axis=1), NLIVE)
    q = jnp.arange(NB)
    dead = jnp.logical_not(live)
    rank = jnp.sum((dead[:, :, None] & (q[:, None] < q[None, :])[None]).astype(jnp.int32), axis=1)
    k = jnp.arange(NDEAD)
    at = dead[:, None, :] & (rank[:, None, :] == k[None, :, None])
    number = jnp.sum(jnp.where(at, q[None, None, :], 0), axis=2)
    cols = jnp.array([UP_COLS, DOWN_COLS] * LMAX)[:, None]
    row = number // cols
    col = number - row * cols
    base = jnp.arange(PARTS)[:, None] % 2
    row = (row + base * DOWN_COLS).astype(jnp.int32)
    col = (col + base * UP_COLS).astype(jnp.int32)
    return inv.astype(jnp.int32), live, rank, row, col


RING = 4
PER = 2 * NDEAD // (RING * RING)
HALF = BLK // 2
TILE = 32


def sums_kernel(
    dead_row, dead_col, left_hbm, right_hbm, out_ref,
    left_0, left_1, right_0, right_1,
    opp_0, opp_1, nxt_0, nxt_1, prv_0, prv_1, mid_0, mid_1,
    ra_0, ra_1, rb_0, rb_1, ia_0, ia_1, ib_0, ib_1,
    sa_0, sa_1, sb_0, sb_1, ja_0, ja_1, jb_0, jb_1,
    squares, mine, row_tiles, all_tiles,
    load_sem, send_sem, recv_sem, tile_send, tile_recv, full_send, full_recv,
):
    section = lax.axis_index("section")
    replica = lax.axis_index("dp")
    px = replica // RING
    py = lax.rem(replica, RING)

    def peer(axis, step):
        if axis == 0:
            return (lax.rem(px + step, RING) * RING + py, section)
        return (px * RING + lax.rem(py + step, RING), section)

    lefts, rights = (left_1, left_0), (right_1, right_0)

    def load(h):
        l = LMAX - 1 - h
        return (
            pltpu.make_async_copy(left_hbm.at[l], lefts[h], load_sem.at[h, 0]),
            pltpu.make_async_copy(right_hbm.at[l], rights[h], load_sem.at[h, 1]),
        )

    for h in range(2):
        for copy in load(h):
            copy.start()

    barrier = pltpu.get_barrier_semaphore()
    for axis in range(2):
        for step in range(1, RING):
            pl.semaphore_signal(barrier, inc=1, device_id=peer(axis, step), device_id_type=MESH)
    pl.semaphore_wait(barrier, 2 * (RING - 1))
    for h in range(2):
        for copy in load(h):
            copy.wait()

    opp, nxt, prv, mid = (opp_0, opp_1), (nxt_0, nxt_1), (prv_0, prv_1), (mid_0, mid_1)
    ra, rb, ia, ib = (ra_0, ra_1), (rb_0, rb_1), (ia_0, ia_1), (ib_0, ib_1)
    sa, sb, ja, jb = (sa_0, sa_1), (sb_0, sb_1), (ja_0, ja_1), (jb_0, jb_1)
    place = (px, py)

    def at(axis, step):
        return lax.rem(place[axis] + step, RING)

    def block(h, f, c, g):
        where = (LMAX - 1 - h) * 2 * NDEAD + (f * PER + c) * RING + g
        return dot(lefts[h][dead_row[where]], rights[h][dead_col[where]])

    def send(h, kind, c, src, dst, axis, step):
        return pltpu.make_async_remote_copy(
            src_ref=src, dst_ref=dst, send_sem=send_sem.at[h, kind, c], recv_sem=recv_sem.at[h, kind, c],
            device_id=peer(axis, step), device_id_type=MESH,
        )

    def copies(h, c):
        first, second = h, 1 - h
        far = at(second, 2)
        return (
            send(h, 0, c, opp[h].at[c, pl.ds(0, 2)], ra[h].at[c], first, 1),
            send(h, 1, c, opp[h].at[c, pl.ds(2, 2)], rb[h].at[c], first, 3),
            send(h, 2, c, nxt[h].at[c], ia[h].at[c], first, 1),
            send(h, 3, c, prv[h].at[c], ib[h].at[c], first, 3),
            send(h, 4, c, mid[h].at[c, far, pl.ds(0, HALF)], sa[h].at[c], second, 1),
            send(h, 5, c, mid[h].at[c, far, pl.ds(HALF, HALF)], sb[h].at[c], second, 3),
            send(h, 6, c, mid[h].at[c, at(second, 1)], ja[h].at[c], second, 1),
            send(h, 7, c, mid[h].at[c, at(second, 3)], jb[h].at[c], second, 3),
        )

    def far_units(c, carry):
        for h in range(2):
            for g in range(RING):
                opp[h][c, g] = block(h, at(h, 2), c, g).astype(BF16)
            moves = copies(h, c)
            moves[0].start()
            moves[1].start()
        return carry

    def near_units(c, carry):
        for h in range(2):
            moves = copies(h, c)
            ahead = [block(h, at(h, 1), c, g) for g in range(RING)]
            behind = [block(h, at(h, 3), c, g) for g in range(RING)]
            moves[0].wait_recv()
            for g in range(RING):
                v = ahead[g] + ra[h][c, g].astype(F32) if g < 2 else ahead[g]
                nxt[h][c, g] = v.astype(BF16)
            moves[2].start()
            moves[1].wait_recv()
            for g in range(RING):
                v = behind[g] + rb[h][c, g - 2].astype(F32) if g >= 2 else behind[g]
                prv[h][c, g] = v.astype(BF16)
            moves[3].start()
        return carry

    def own_units(c, carry):
        for h in range(2):
            moves = copies(h, c)
            own = [block(h, place[h], c, g) for g in range(RING)]
            moves[2].wait_recv()
            moves[3].wait_recv()
            for g in range(RING):
                v = own[g] + ia[h][c, g].astype(F32) + ib[h][c, g].astype(F32)
                mid[h][c, g] = v.astype(BF16)
            moves[4].start()
            moves[5].start()
        return carry

    def second_axis(c, carry):
        for h in range(2):
            moves = copies(h, c)
            ahead, behind = at(1 - h, 1), at(1 - h, 3)
            moves[4].wait_recv()
            top = pl.ds(0, HALF)
            v = mid[h][c, ahead, top, :].astype(F32) + sa[h][c].astype(F32)
            mid[h][c, ahead, top, :] = v.astype(BF16)
            moves[6].start()
            moves[5].wait_recv()
            low = pl.ds(HALF, HALF)
            v = mid[h][c, behind, low, :].astype(F32) + sb[h][c].astype(F32)
            mid[h][c, behind, low, :] = v.astype(BF16)
            moves[7].start()
        return carry

    def totals(c, carry):
        for h in range(2):
            moves = copies(h, c)
            moves[6].wait_recv()
            moves[7].wait_recv()
            v = mid[h][c, place[1 - h]].astype(F32) + ja[h][c].astype(F32) + jb[h][c].astype(F32)
            squares[h, pl.ds(c, 1), :] = jnp.sum(v * v, axis=0, keepdims=True)
        return carry

    def drain(c, carry):
        for h in range(2):
            for move in copies(h, c):
                move.wait_send()
        return carry

    squares[...] = jnp.zeros_like(squares)
    for step in (far_units, near_units, own_units, second_axis, totals):
        lax.fori_loop(0, PER, step, 0)
    rows_total = float(RING * RING * KMAX)
    mean = jnp.sum(squares[...].reshape(TILE, BLK), axis=1, keepdims=True) * (1.0 / (BLK * BLK))
    mine[...] = jnp.broadcast_to(jnp.sqrt(mean / rows_total + EPS_SCORE), (TILE, BLK))

    row_tiles[px] = mine[...]
    rows = [
        pltpu.make_async_remote_copy(
            src_ref=mine, dst_ref=row_tiles.at[px], send_sem=tile_send.at[step - 1],
            recv_sem=tile_recv.at[step - 1], device_id=peer(0, step), device_id_type=MESH,
        )
        for step in range(1, RING)
    ]
    for move in rows:
        move.start()
    for move in rows:
        move.wait()
    all_tiles[py] = row_tiles[...]
    cols = [
        pltpu.make_async_remote_copy(
            src_ref=row_tiles, dst_ref=all_tiles.at[py], send_sem=full_send.at[step - 1],
            recv_sem=full_recv.at[step - 1], device_id=peer(1, step), device_id_type=MESH,
        )
        for step in range(1, RING)
    ]
    for move in cols:
        move.start()
    for move in cols:
        move.wait()
    out_ref[...] = all_tiles[...]
    lax.fori_loop(0, PER, drain, 0)


def sums(dead_row, dead_col, left, right):
    smem = pl.BlockSpec(memory_space=pltpu.SMEM)
    hbm = pl.BlockSpec(memory_space=pl.ANY)

    def blocks(*lead):
        return [pltpu.VMEM((PER, *lead, BLK), BF16)] * 2

    return pl.pallas_call(
        sums_kernel,
        out_shape=jax.ShapeDtypeStruct((RING, RING, TILE, BLK), F32),
        in_specs=[smem] * 2 + [hbm] * 2,
        out_specs=pl.BlockSpec(memory_space=pltpu.VMEM),
        scratch_shapes=[
            *[pltpu.VMEM((PANELS, BLK, KMAX), BF16)] * 2,
            *[pltpu.VMEM((PANELS, KMAX, BLK), BF16)] * 2,
            *blocks(RING, BLK), *blocks(RING, BLK), *blocks(RING, BLK), *blocks(RING, BLK),
            *blocks(2, BLK), *blocks(2, BLK), *blocks(RING, BLK), *blocks(RING, BLK),
            *blocks(HALF), *blocks(HALF), *blocks(BLK), *blocks(BLK),
            pltpu.VMEM((2, TILE // 2, BLK), F32),
            pltpu.VMEM((TILE, BLK), F32),
            pltpu.VMEM((RING, TILE, BLK), F32),
            pltpu.VMEM((RING, RING, TILE, BLK), F32),
            pltpu.SemaphoreType.DMA((2, 2)),
            pltpu.SemaphoreType.DMA((2, 8, PER)),
            pltpu.SemaphoreType.DMA((2, 8, PER)),
            *[pltpu.SemaphoreType.DMA((RING - 1,))] * 4,
        ],
        compiler_params=pltpu.CompilerParams(
            collective_id=1, has_side_effects=True, vmem_limit_bytes=60 * 1024 * 1024
        ),
        cost_estimate=pl.CostEstimate(flops=3_000_000_000, bytes_accessed=8_000_000, transcendentals=0),
    )(dead_row, dead_col, left, right)


def body(patches, cotangent, keep_order, keep_count, destination, norm_gain, up_blocks, up_index,
         down_blocks, down_index, layer_count, regrow_mask):
    replicas = lax.axis_size("dp")
    replica_id = lax.axis_index("dp")
    inv, live, rank, row, col = tables(up_index, down_index)
    kept = jnp.where(jnp.arange(KMAX) < keep_count[0], keep_order[0, :KMAX], -1)
    pick = jnp.broadcast_to(kept[:, None], (KMAX, BLK)).astype(jnp.int32)
    active = jnp.broadcast_to((jnp.arange(8) < layer_count[0])[:, None], (8, BLK)).astype(jnp.int32)
    left, right = chain(inv.reshape(-1), active, pick, patches[0], cotangent[0], norm_gain, up_blocks, down_blocks)
    tiles = sums(row.reshape(-1), col.reshape(-1), left, right)
    half = TILE // 2
    late = tiles[:, :, :PER, 0].transpose(1, 2, 0).reshape(2 * NDEAD)
    early = tiles[:, :, half:half + PER, 0].transpose(0, 2, 1).reshape(2 * NDEAD)
    every = jnp.stack([early, late])
    share = 2 * NB // replicas
    start = replica_id * share
    slot = rank.reshape(LMAX, 2, NB) + (jnp.arange(2) * NDEAD)[None, :, None]
    slot = lax.dynamic_slice_in_dim(slot.reshape(LMAX, 2 * NB), start, share, 1)
    alive = lax.dynamic_slice_in_dim(live.reshape(LMAX, 2 * NB), start, share, 1)
    picked = jnp.sum(jnp.where(slot[:, :, None] == jnp.arange(2 * NDEAD), every[:, None, :], 0.0), axis=2)
    eligible = jnp.logical_and(jnp.logical_not(alive), regrow_mask == 1)
    return jnp.where(eligible, picked, 0.0)


def solution(mesh):
    return jax.shard_map(
        body, mesh=mesh,
        in_specs=(
            P("dp", None, None), P("dp", None, None), P("dp", None), P("dp"), P("dp", None),
            P("section", None), P("section", None, None, None), P("section", None),
            P("section", None, None, None), P("section", None), P("section"), P("section", "dp"),
        ),
        out_specs=P("section", "dp"), check_vma=False,
    )
```

```python
import functools
import jax
import jax.numpy as jnp
import numpy as np
from jax import lax
from jax.experimental import pallas as pl
from jax.experimental.pallas import tpu as pltpu
from jax.sharding import PartitionSpec as P

D = 1280
FF = 2560
BLK = 128
KMAX = 192
LMAX = 2
NB = 200
NLIVE = 96
NDEAD = NB - NLIVE
UP_COLS = FF // BLK
DOWN_COLS = D // BLK
PARTS = 2 * LMAX
PANELS = UP_COLS + DOWN_COLS
RING = 4
MOST = 2 * NDEAD
FEW = 128
HALF = BLK // 2
TILE = 32
OWN = 2 * NB // (RING * RING)
WIDE = 256
EPS_NORM = 1e-06
EPS_SCORE = 1e-06
MICRO = 2
ROWS = KMAX // MICRO
CHUNK = 512
SQ = 256
MESH = pl.DeviceIdType.MESH
F32 = jnp.float32
BF16 = jnp.bfloat16
GELU_A = 0.7978845608028654
GELU_B = 0.044715


def dot(a, b):
    return jnp.dot(a, b, preferred_element_type=F32)


def dot_t(a, b):
    return lax.dot_general(a, b, (((1,), (1,)), ((), ())), preferred_element_type=F32)


def gelu(v):
    return 0.5 * v * (1.0 + jnp.tanh(GELU_A * (v + GELU_B * (v * v * v))))


def gelu_slope(v):
    sq = v * v
    t = jnp.tanh(GELU_A * (v + GELU_B * (v * sq)))
    return 0.5 * (1.0 + t) + 0.5 * v * (1.0 - t * t) * (GELU_A * (1.0 + 3.0 * GELU_B * sq))


def chain_kernel(
    inv_ref,
    active, pick_ref, mask, dead, panels, patches, cotangent, gain, up_hbm, down_hbm,
    left_hbm, right_hbm, slots_out, rank_out, wanted_out, most_out,
    stage_a, stage_b, up_0, up_1, down_0, down_1, spare, xs, gs, normed, inv_std, act, hidden, pre, grad_pre,
    left, right, row_tiles, all_tiles, most, most_up, most_down,
    stage_sem, left_sem, right_sem, x_send, x_recv, g_send, g_recv,
    tile_send, tile_recv, all_send, all_recv, most_send, most_recv,
):
    sections = lax.axis_size("section")
    replica = lax.axis_index("dp")
    section = lax.axis_index("section")
    first = section == 0
    last = section == sections - 1
    stages = (stage_a, stage_b)
    w_up, w_down = (up_0, up_1), (down_0, down_1)
    w_up_t, w_down_t = (down_0, down_1), (up_1, spare)

    def flag(l):
        return active[l:l + 1, :1] == 1

    def load(part):
        l, kind = part // 2, part % 2
        src = (up_hbm, down_hbm)[kind].at[l]
        return pltpu.make_async_copy(src, stages[part % 2].at[pl.ds(0, NLIVE)], stage_sem.at[part])

    stage_a[NLIVE] = jnp.zeros((BLK, BLK), BF16)
    stage_b[NLIVE] = jnp.zeros((BLK, BLK), BF16)
    load(0).start()
    load(1).start()

    barrier = pltpu.get_barrier_semaphore()

    @pl.when(jnp.logical_not(first))
    def _():
        pl.semaphore_signal(barrier, inc=1, device_id=(replica, section - 1), device_id_type=MESH)

    @pl.when(jnp.logical_not(last))
    def _():
        pl.semaphore_signal(barrier, inc=1, device_id=(replica, section + 1), device_id_type=MESH)

    px = replica // RING
    py = lax.rem(replica, RING)

    def along_y(step):
        return (px * RING + lax.rem(py + step, RING), section)

    def along_x(step):
        return (lax.rem(px + step, RING) * RING + py, section)

    for step in range(1, RING):
        pl.semaphore_signal(barrier, inc=1, device_id=along_y(step), device_id_type=MESH)
        pl.semaphore_signal(barrier, inc=1, device_id=along_x(step), device_id_type=MESH)

    def moves(source, target, sends, recvs, to):
        return [
            pltpu.make_async_remote_copy(
                src_ref=source, dst_ref=target, send_sem=sends.at[step - 1], recv_sem=recvs.at[step - 1],
                device_id=to(step), device_id_type=MESH,
            )
            for step in range(1, RING)
        ]

    def row_moves():
        return moves(mask, row_tiles.at[py], tile_send, tile_recv, along_y)

    def all_moves():
        return moves(row_tiles, all_tiles.at[px], all_send, all_recv, along_x)

    def picked(table):
        hot = pick_ref[:, :1] == lax.broadcasted_iota(jnp.int32, (KMAX, table.shape[0]), 1)
        return dot(hot.astype(BF16), table[...]).astype(BF16)

    @pl.when(first)
    def _():
        xs[0] = picked(patches)

    @pl.when(last)
    def _():
        gs[LMAX] = picked(cotangent)

    @pl.when(jnp.logical_or(first, last))
    def _():
        pl.semaphore_wait(barrier, 2 * (RING - 1) + 1)

    @pl.when(jnp.logical_not(jnp.logical_or(first, last)))
    def _():
        pl.semaphore_wait(barrier, 2 * (RING - 1) + 2)

    row_tiles[py] = mask[...]
    for move in row_moves():
        move.start()

    def after_part(part):
        if part == 1:
            for move in row_moves():
                move.wait()
            all_tiles[px] = row_tiles[...]
            for move in all_moves():
                move.start()

    def settle():
        for move in all_moves():
            move.wait()
        count = jnp.zeros((1, 1), F32)
        lanes = lax.broadcasted_iota(jnp.int32, (BLK, BLK), 0)
        later = lanes < lax.broadcasted_iota(jnp.int32, (BLK, BLK), 1)
        later = later.astype(BF16)
        ones = jnp.ones((BLK, BLK), BF16)
        n = RING * RING
        under = lax.broadcasted_iota(jnp.int32, (n, n), 0) > lax.broadcasted_iota(jnp.int32, (n, n), 1)
        spots = lax.broadcasted_iota(jnp.int32, (BLK, WIDE), 1).astype(F32)
        for l in range(LMAX):
            asked = all_tiles[:, :, l, :].reshape(n, BLK) * dead[l]
            flat = asked.astype(BF16)
            totals = dot(flat, ones)
            rank = dot(flat, later) + dot(under.astype(BF16), totals.astype(BF16))
            rank_out[l] = rank
            wanted_out[l] = asked
            count = jnp.maximum(count, jnp.sum(totals[:, :1], axis=0, keepdims=True))
            turned = jnp.where(asked > 0.5, rank, -1.0).T
            found = jnp.zeros((8, WIDE), F32)
            for d in range(n):
                hot = (turned[:, d:d + 1] == spots).astype(BF16)
                found = found + dot(panels[d], hot)
            slots_out[l] = found.astype(jnp.int32)
        most[...] = jnp.broadcast_to(count, (8, BLK))

    def pass_up():
        return pltpu.make_async_remote_copy(
            src_ref=most, dst_ref=most_up, send_sem=most_send.at[0], recv_sem=most_recv.at[0],
            device_id=(replica, section + 1), device_id_type=MESH,
        )

    def pass_down():
        return pltpu.make_async_remote_copy(
            src_ref=most, dst_ref=most_down, send_sem=most_send.at[1], recv_sem=most_recv.at[1],
            device_id=(replica, section - 1), device_id_type=MESH,
        )

    for part in range(PARTS):
        load(part).wait()
        l, kind = part // 2, part % 2
        target, cols = ((w_up, UP_COLS), (w_down, DOWN_COLS))[kind]

        def place(rb, carry, l=l, target=target, cols=cols, part=part):
            rs = pl.ds(pl.multiple_of(rb * BLK, BLK), BLK)
            for cb in range(cols):
                target[l][rs, cb * BLK:(cb + 1) * BLK] = stages[part % 2][inv_ref[part * NB + rb * cols + cb]]
            return carry

        lax.fori_loop(0, NB // cols, place, 0)
        after_part(part)
        if part + 2 < PARTS:
            load(part + 2).start()

    def rows_of(mb):
        return pl.ds(pl.multiple_of(mb * ROWS, ROWS), ROWS)

    def cols_of(j, size):
        return pl.ds(pl.multiple_of(j * size, size), size)

    def send_x(mb):
        return pltpu.make_async_remote_copy(
            src_ref=xs.at[LMAX, rows_of(mb)], dst_ref=xs.at[0, rows_of(mb)],
            send_sem=x_send.at[mb], recv_sem=x_recv.at[mb],
            device_id=(replica, section + 1), device_id_type=MESH,
        )

    def send_g(mb):
        return pltpu.make_async_remote_copy(
            src_ref=gs.at[0, rows_of(mb)], dst_ref=gs.at[LMAX, rows_of(mb)],
            send_sem=g_send.at[mb], recv_sem=g_recv.at[mb],
            device_id=(replica, section - 1), device_id_type=MESH,
        )

    def forward(mb, carry):
        r = rows_of(mb)

        @pl.when(jnp.logical_not(first))
        def _():
            send_x(mb).wait_recv()

        for l in range(LMAX):
            x = xs[l, r, :].astype(F32)
            centred = x - jnp.mean(x, axis=-1, keepdims=True)
            inv = lax.rsqrt(jnp.mean(centred * centred, axis=-1, keepdims=True) + EPS_NORM)
            n = centred * inv
            normed[l, r, :] = n
            inv_std[l, r, :] = jnp.broadcast_to(inv, (ROWS, BLK))
            act[l, r, :] = (n * gain[l:l + 1, :]).astype(BF16)

            def up_chunk(j, c, l=l):
                cs = cols_of(j, CHUNK)
                v = dot(act[l, r, :], w_up[l][:, cs])
                pre[l, r, cs] = v
                hidden[l, r, cs] = gelu(v).astype(BF16)
                return c

            lax.fori_loop(0, FF // CHUNK, up_chunk, 0, unroll=True)

            def down_chunk(j, c, l=l):
                cs = cols_of(j, 256)
                v = dot(hidden[l, r, :], w_down[l][:, cs])
                had = xs[l, r, cs]
                moved = (had.astype(F32) + v).astype(BF16)
                xs[l + 1, r, cs] = jnp.where(flag(l), moved, had)
                return c

            lax.fori_loop(0, D // 256, down_chunk, 0, unroll=True)

        @pl.when(jnp.logical_not(last))
        def _():
            send_x(mb).start()

        return carry

    @pl.when(jnp.logical_not(first))
    def _():
        settle()

    lax.fori_loop(0, MICRO, forward, 0)

    @pl.when(first)
    def _():
        settle()

    @pl.when(jnp.logical_not(first))
    def _():
        pass_up().wait_recv()
        most[...] = jnp.maximum(most[...], most_up[...])

    @pl.when(jnp.logical_not(last))
    def _():
        pass_up().start()


    def save_left(l):
        return pltpu.make_async_copy(left.at[l], left_hbm.at[l], left_sem.at[l])

    for l in range(LMAX):
        def slopes(j, c, l=l):
            cs = cols_of(j, BLK)
            pre[l, :, cs] = gelu_slope(pre[l, :, cs])
            h = jnp.where(flag(l), hidden[l, :, cs], jnp.zeros((KMAX, BLK), BF16))
            left[l, DOWN_COLS + j] = h.T
            return c

        lax.fori_loop(0, FF // BLK, slopes, 0)

        def turn(j, c, l=l):
            a = jnp.where(flag(l), act[l, :, cols_of(j, BLK)], jnp.zeros((KMAX, BLK), BF16))
            left[l, j] = a.T
            return c

        lax.fori_loop(0, D // BLK, turn, 0)
        save_left(l).start()

    unit = (
        lax.broadcasted_iota(jnp.int32, (SQ, SQ), 0) == lax.broadcasted_iota(jnp.int32, (SQ, SQ), 1)
    ).astype(BF16)
    for source, target in ((down_1, spare), (up_1, down_1), (down_0, up_1), (up_0, down_0)):
        def flip(i, c, source=source, target=target):
            rs = cols_of(i, SQ)
            for j in range(source.shape[1] // SQ):
                tile = source[rs, j * SQ:(j + 1) * SQ]
                target[j * SQ:(j + 1) * SQ, rs] = dot_t(unit, tile).astype(BF16)
            return c

        lax.fori_loop(0, source.shape[0] // SQ, flip, 0)

    def save_right(l):
        return pltpu.make_async_copy(right.at[l], right_hbm.at[l], right_sem.at[l])

    def backward(mb, carry):
        r = rows_of(mb)

        @pl.when(jnp.logical_not(last))
        def _():
            send_g(mb).wait_recv()

        for l in reversed(range(LMAX)):
            def hidden_chunk(j, c, l=l):
                cs = cols_of(j, CHUNK)
                v = dot(gs[l + 1, r, :], w_down_t[l][:, cs])
                p = (pre[l, r, cs] * v).astype(BF16)
                grad_pre[l, r, cs] = p
                for b in range(CHUNK // BLK):
                    right[l, j * (CHUNK // BLK) + b, r, :] = p[:, b * BLK:(b + 1) * BLK]
                return c

            lax.fori_loop(0, FF // CHUNK, hidden_chunk, 0, unroll=True)

            def act_chunk(j, c, l=l):
                cs = cols_of(j, 256)
                v = dot(grad_pre[l, r, :], w_up_t[l][:, cs])
                pre[l, r, cs] = v * gain[l:l + 1, cs]
                return c

            lax.fori_loop(0, D // 256, act_chunk, 0, unroll=True)
            u = pre[l, r, :D]
            n = normed[l, r, :]
            step = inv_std[l, r, :1] * (
                u - jnp.mean(u, axis=-1, keepdims=True) - n * jnp.mean(u * n, axis=-1, keepdims=True)
            )
            had = gs[l + 1, r, :]
            for b in range(DOWN_COLS):
                right[l, UP_COLS + b, r, :] = had[:, b * BLK:(b + 1) * BLK]
            gs[l, r, :] = jnp.where(flag(l), (had.astype(F32) + step).astype(BF16), had)

        @pl.when(jnp.logical_not(first))
        def _():
            send_g(mb).start()

        return carry

    lax.fori_loop(0, MICRO, backward, 0)

    @pl.when(jnp.logical_not(last))
    def _():
        pass_up().wait_send()
        pass_down().wait_recv()
        most[...] = jnp.maximum(most[...], most_down[...])

    @pl.when(jnp.logical_not(first))
    def _():
        pass_down().start()

    most_out[...] = most[...]

    for l in range(LMAX):
        save_right(l).start()

    def drain(mb, carry):
        @pl.when(jnp.logical_not(last))
        def _():
            send_x(mb).wait_send()

        @pl.when(jnp.logical_not(first))
        def _():
            send_g(mb).wait_send()

        return carry

    lax.fori_loop(0, MICRO, drain, 0)

    @pl.when(jnp.logical_not(first))
    def _():
        pass_down().wait_send()

    for l in range(LMAX):
        save_left(l).wait()
        save_right(l).wait()


def chain(inv, active, pick, mask, dead, panels, patches, cotangent, gain, up, down):
    smem = pl.BlockSpec(memory_space=pltpu.SMEM)
    vmem = pl.BlockSpec(memory_space=pltpu.VMEM)
    hbm = pl.BlockSpec(memory_space=pl.ANY)
    return pl.pallas_call(
        chain_kernel,
        out_shape=(
            jax.ShapeDtypeStruct((LMAX, PANELS, BLK, KMAX), BF16),
            jax.ShapeDtypeStruct((LMAX, PANELS, KMAX, BLK), BF16),
            jax.ShapeDtypeStruct((LMAX, 8, WIDE), jnp.int32),
            jax.ShapeDtypeStruct((LMAX, RING * RING, BLK), F32),
            jax.ShapeDtypeStruct((LMAX, RING * RING, BLK), F32),
            jax.ShapeDtypeStruct((8, BLK), F32),
        ),
        in_specs=[smem] + [vmem] * 8 + [hbm] * 2,
        out_specs=(hbm, hbm, vmem, vmem, vmem, vmem),
        scratch_shapes=[
            pltpu.VMEM((NLIVE + 1, BLK, BLK), BF16),
            pltpu.VMEM((NLIVE + 1, BLK, BLK), BF16),
            *[pltpu.VMEM((D, FF), BF16)] * 2,
            *[pltpu.VMEM((FF, D), BF16)] * 2,
            pltpu.VMEM((D, FF), BF16),
            pltpu.VMEM((LMAX + 1, KMAX, D), BF16),
            pltpu.VMEM((LMAX + 1, KMAX, D), BF16),
            pltpu.VMEM((LMAX, KMAX, D), F32),
            pltpu.VMEM((LMAX, KMAX, BLK), F32),
            pltpu.VMEM((LMAX, KMAX, D), BF16),
            pltpu.VMEM((LMAX, KMAX, FF), BF16),
            pltpu.VMEM((LMAX, KMAX, FF), F32),
            pltpu.VMEM((LMAX, KMAX, FF), BF16),
            pltpu.VMEM((LMAX, PANELS, BLK, KMAX), BF16),
            pltpu.VMEM((LMAX, PANELS, KMAX, BLK), BF16),
            pltpu.VMEM((RING, 8, BLK), F32),
            pltpu.VMEM((RING, RING, 8, BLK), F32),
            *[pltpu.VMEM((8, BLK), F32)] * 3,
            pltpu.SemaphoreType.DMA((PARTS,)),
            pltpu.SemaphoreType.DMA((LMAX,)),
            pltpu.SemaphoreType.DMA((LMAX,)),
            pltpu.SemaphoreType.DMA((MICRO,)),
            pltpu.SemaphoreType.DMA((MICRO,)),
            pltpu.SemaphoreType.DMA((MICRO,)),
            pltpu.SemaphoreType.DMA((MICRO,)),
            *[pltpu.SemaphoreType.DMA((RING - 1,))] * 4,
            *[pltpu.SemaphoreType.DMA((2,))] * 2,
        ],
        compiler_params=pltpu.CompilerParams(
            collective_id=0, has_side_effects=True, vmem_limit_bytes=60 * 1024 * 1024
        ),
        cost_estimate=pl.CostEstimate(flops=35_000_000_000, bytes_accessed=30_000_000, transcendentals=2_000_000),
    )(inv, active, pick, mask, dead, panels, patches, cotangent, gain, up, down)


def live_tables(up_index, down_index):
    listed = jnp.stack([up_index, down_index], axis=1).reshape(PARTS, NLIVE)
    hit = listed[:, :, None] == jnp.arange(NB)[None, None, :]
    live = jnp.any(hit, axis=1)
    inv = jnp.where(live, jnp.sum(jnp.where(hit, jnp.arange(NLIVE)[None, :, None], 0), axis=1), NLIVE)
    return inv.astype(jnp.int32), live.reshape(LMAX, 2 * NB)


def sums_kernel(
    PER, slots, left_hbm, right_hbm, out_ref,
    left_0, left_1, right_0, right_1,
    opp_0, opp_1, nxt_0, nxt_1, prv_0, prv_1, mid_0, mid_1,
    ra_0, ra_1, rb_0, rb_1, ia_0, ia_1, ib_0, ib_1,
    sa_0, sa_1, sb_0, sb_1, ja_0, ja_1, jb_0, jb_1,
    squares, mine, row_tiles, all_tiles,
    load_sem, send_sem, recv_sem, tile_send, tile_recv, full_send, full_recv,
):
    section = lax.axis_index("section")
    replica = lax.axis_index("dp")
    px = replica // RING
    py = lax.rem(replica, RING)

    def peer(axis, step):
        if axis == 0:
            return (lax.rem(px + step, RING) * RING + py, section)
        return (px * RING + lax.rem(py + step, RING), section)

    lefts, rights = (left_1, left_0), (right_1, right_0)

    def load(h):
        l = LMAX - 1 - h
        return (
            pltpu.make_async_copy(left_hbm.at[l], lefts[h], load_sem.at[h, 0]),
            pltpu.make_async_copy(right_hbm.at[l], rights[h], load_sem.at[h, 1]),
        )

    for h in range(2):
        for copy in load(h):
            copy.start()

    barrier = pltpu.get_barrier_semaphore()
    for axis in range(2):
        for step in range(1, RING):
            pl.semaphore_signal(barrier, inc=1, device_id=peer(axis, step), device_id_type=MESH)
    pl.semaphore_wait(barrier, 2 * (RING - 1))
    for h in range(2):
        for copy in load(h):
            copy.wait()

    opp, nxt, prv, mid = (opp_0, opp_1), (nxt_0, nxt_1), (prv_0, prv_1), (mid_0, mid_1)
    ra, rb, ia, ib = (ra_0, ra_1), (rb_0, rb_1), (ia_0, ia_1), (ib_0, ib_1)
    sa, sb, ja, jb = (sa_0, sa_1), (sb_0, sb_1), (ja_0, ja_1), (jb_0, jb_1)
    place = (px, py)

    def at(axis, step):
        return lax.rem(place[axis] + step, RING)

    def block(h, f, c, g):
        l, s = LMAX - 1 - h, (f * PER + c) * RING + g
        return dot(lefts[h][slots[l, 0, s]], rights[h][slots[l, 1, s]])

    def send(h, kind, c, src, dst, axis, step):
        return pltpu.make_async_remote_copy(
            src_ref=src, dst_ref=dst, send_sem=send_sem.at[h, kind, c], recv_sem=recv_sem.at[h, kind, c],
            device_id=peer(axis, step), device_id_type=MESH,
        )

    def copies(h, c):
        first, second = h, 1 - h
        far = at(second, 2)
        return (
            send(h, 0, c, opp[h].at[c, pl.ds(0, 2)], ra[h].at[c], first, 1),
            send(h, 1, c, opp[h].at[c, pl.ds(2, 2)], rb[h].at[c], first, 3),
            send(h, 2, c, nxt[h].at[c], ia[h].at[c], first, 1),
            send(h, 3, c, prv[h].at[c], ib[h].at[c], first, 3),
            send(h, 4, c, mid[h].at[c, far, pl.ds(0, HALF)], sa[h].at[c], second, 1),
            send(h, 5, c, mid[h].at[c, far, pl.ds(HALF, HALF)], sb[h].at[c], second, 3),
            send(h, 6, c, mid[h].at[c, at(second, 1)], ja[h].at[c], second, 1),
            send(h, 7, c, mid[h].at[c, at(second, 3)], jb[h].at[c], second, 3),
        )

    def far_units(c, carry):
        for h in range(2):
            for g in range(RING):
                opp[h][c, g] = block(h, at(h, 2), c, g).astype(BF16)
            moves = copies(h, c)
            moves[0].start()
            moves[1].start()
        return carry

    def near_units(c, carry):
        for h in range(2):
            moves = copies(h, c)
            ahead = [block(h, at(h, 1), c, g) for g in range(RING)]
            behind = [block(h, at(h, 3), c, g) for g in range(RING)]
            moves[0].wait_recv()
            for g in range(RING):
                v = ahead[g] + ra[h][c, g].astype(F32) if g < 2 else ahead[g]
                nxt[h][c, g] = v.astype(BF16)
            moves[2].start()
            moves[1].wait_recv()
            for g in range(RING):
                v = behind[g] + rb[h][c, g - 2].astype(F32) if g >= 2 else behind[g]
                prv[h][c, g] = v.astype(BF16)
            moves[3].start()
        return carry

    def own_units(c, carry):
        for h in range(2):
            moves = copies(h, c)
            own = [block(h, place[h], c, g) for g in range(RING)]
            moves[2].wait_recv()
            moves[3].wait_recv()
            for g in range(RING):
                v = own[g] + ia[h][c, g].astype(F32) + ib[h][c, g].astype(F32)
                mid[h][c, g] = v.astype(BF16)
            moves[4].start()
            moves[5].start()
        return carry

    def second_axis(c, carry):
        for h in range(2):
            moves = copies(h, c)
            ahead, behind = at(1 - h, 1), at(1 - h, 3)
            moves[4].wait_recv()
            top = pl.ds(0, HALF)
            v = mid[h][c, ahead, top, :].astype(F32) + sa[h][c].astype(F32)
            mid[h][c, ahead, top, :] = v.astype(BF16)
            moves[6].start()
            moves[5].wait_recv()
            low = pl.ds(HALF, HALF)
            v = mid[h][c, behind, low, :].astype(F32) + sb[h][c].astype(F32)
            mid[h][c, behind, low, :] = v.astype(BF16)
            moves[7].start()
        return carry

    def totals(c, carry):
        for h in range(2):
            moves = copies(h, c)
            moves[6].wait_recv()
            moves[7].wait_recv()
            v = mid[h][c, place[1 - h]].astype(F32) + ja[h][c].astype(F32) + jb[h][c].astype(F32)
            squares[h, pl.ds(c, 1), :] = jnp.sum(v * v, axis=0, keepdims=True)
        return carry

    def drain(c, carry):
        for h in range(2):
            for move in copies(h, c):
                move.wait_send()
        return carry

    squares[...] = jnp.zeros_like(squares)
    for step in (far_units, near_units, own_units, second_axis, totals):
        lax.fori_loop(0, PER, step, 0)
    rows_total = float(RING * RING * KMAX)
    mean = jnp.sum(squares[...].reshape(TILE, BLK), axis=1, keepdims=True) * (1.0 / (BLK * BLK))
    mine[...] = jnp.broadcast_to(jnp.sqrt(mean / rows_total + EPS_SCORE), (TILE, BLK))

    row_tiles[px] = mine[...]
    rows = [
        pltpu.make_async_remote_copy(
            src_ref=mine, dst_ref=row_tiles.at[px], send_sem=tile_send.at[step - 1],
            recv_sem=tile_recv.at[step - 1], device_id=peer(0, step), device_id_type=MESH,
        )
        for step in range(1, RING)
    ]
    for move in rows:
        move.start()
    for move in rows:
        move.wait()
    all_tiles[py] = row_tiles[...]
    cols = [
        pltpu.make_async_remote_copy(
            src_ref=row_tiles, dst_ref=all_tiles.at[py], send_sem=full_send.at[step - 1],
            recv_sem=full_recv.at[step - 1], device_id=peer(1, step), device_id_type=MESH,
        )
        for step in range(1, RING)
    ]
    for move in cols:
        move.start()
    for move in cols:
        move.wait()
    out_ref[...] = all_tiles[...]
    lax.fori_loop(0, PER, drain, 0)


def sums(size, number, slots, left, right):
    PER = size // (RING * RING)
    smem = pl.BlockSpec(memory_space=pltpu.SMEM)
    hbm = pl.BlockSpec(memory_space=pl.ANY)

    def blocks(*lead):
        return [pltpu.VMEM((PER, *lead, BLK), BF16)] * 2

    return pl.pallas_call(
        functools.partial(sums_kernel, PER),
        out_shape=jax.ShapeDtypeStruct((RING, RING, TILE, BLK), F32),
        in_specs=[smem] + [hbm] * 2,
        out_specs=pl.BlockSpec(memory_space=pltpu.VMEM),
        scratch_shapes=[
            *[pltpu.VMEM((PANELS, BLK, KMAX), BF16)] * 2,
            *[pltpu.VMEM((PANELS, KMAX, BLK), BF16)] * 2,
            *blocks(RING, BLK), *blocks(RING, BLK), *blocks(RING, BLK), *blocks(RING, BLK),
            *blocks(2, BLK), *blocks(2, BLK), *blocks(RING, BLK), *blocks(RING, BLK),
            *blocks(HALF), *blocks(HALF), *blocks(BLK), *blocks(BLK),
            pltpu.VMEM((2, TILE // 2, BLK), F32),
            pltpu.VMEM((TILE, BLK), F32),
            pltpu.VMEM((RING, TILE, BLK), F32),
            pltpu.VMEM((RING, RING, TILE, BLK), F32),
            pltpu.SemaphoreType.DMA((2, 2)),
            pltpu.SemaphoreType.DMA((2, 8, PER)),
            pltpu.SemaphoreType.DMA((2, 8, PER)),
            *[pltpu.SemaphoreType.DMA((RING - 1,))] * 4,
        ],
        compiler_params=pltpu.CompilerParams(
            collective_id=number, has_side_effects=True, vmem_limit_bytes=60 * 1024 * 1024
        ),
        cost_estimate=pl.CostEstimate(flops=3_000_000_000, bytes_accessed=8_000_000, transcendentals=0),
    )(slots, left, right)


def every_score(size, number, slots, left, right):
    per = size // (RING * RING)
    tiles = sums(size, number, slots, left, right)
    half = TILE // 2
    late = tiles[:, :, :per, 0].transpose(1, 2, 0).reshape(size)
    early = tiles[:, :, half:half + per, 0].transpose(0, 2, 1).reshape(size)
    return jnp.pad(jnp.stack([early, late]), ((0, 0), (0, MOST - size)))


def panel_numbers():
    q = np.arange(2 * NB)
    lower = q >= NB
    inner = np.where(lower, q - NB, q)
    cols = np.where(lower, DOWN_COLS, UP_COLS)
    row = np.where(lower, inner // cols + DOWN_COLS, inner // cols)
    col = np.where(lower, inner % cols + UP_COLS, inner % cols)
    table = np.zeros((RING * RING, 8, BLK), np.float32)
    table[:, 0, :OWN] = row.reshape(-1, OWN)
    table[:, 1, :OWN] = col.reshape(-1, OWN)
    return jnp.asarray(table, BF16)


def body(patches, cotangent, keep_order, keep_count, destination, norm_gain, up_blocks, up_index,
         down_blocks, down_index, layer_count, regrow_mask):
    replica_id = lax.axis_index("dp")
    inv, live = live_tables(up_index, down_index)
    dead = jnp.logical_not(live).reshape(LMAX, RING * RING, OWN)
    dead = jnp.pad(dead.astype(F32), ((0, 0), (0, 0), (0, BLK - OWN)))
    mask = jnp.pad((regrow_mask == 1).astype(F32), ((0, 8 - LMAX), (0, BLK - OWN)))
    kept = jnp.where(jnp.arange(KMAX) < keep_count[0], keep_order[0, :KMAX], -1)
    pick = jnp.broadcast_to(kept[:, None], (KMAX, BLK)).astype(jnp.int32)
    active = jnp.broadcast_to((jnp.arange(8) < layer_count[0])[:, None], (8, BLK)).astype(jnp.int32)
    left, right, slots, rank, wanted, most = chain(
        inv.reshape(-1), active, pick, mask, dead, panel_numbers(), patches[0], cotangent[0], norm_gain,
        up_blocks, down_blocks,
    )
    every = lax.cond(
        most[0, 0] < FEW + 0.5,
        functools.partial(every_score, FEW, 1),
        functools.partial(every_score, MOST, 2),
        slots, left, right,
    )
    rank = lax.dynamic_index_in_dim(rank, replica_id, 1, keepdims=False)[:, :OWN]
    wanted = lax.dynamic_index_in_dim(wanted, replica_id, 1, keepdims=False)[:, :OWN]
    spots = jnp.arange(MOST).astype(F32)
    picked = jnp.sum(jnp.where(rank[:, :, None] == spots, every[:, None, :], 0.0), axis=2)
    return jnp.where(wanted > 0.5, picked, 0.0)


def solution(mesh):
    return jax.shard_map(
        body, mesh=mesh,
        in_specs=(
            P("dp", None, None), P("dp", None, None), P("dp", None), P("dp"), P("dp", None),
            P("section", None), P("section", None, None, None), P("section", None),
            P("section", None, None, None), P("section", None), P("section"), P("section", "dp"),
        ),
        out_specs=P("section", "dp"), check_vma=False,
    )
```

```python
import functools
import jax
import jax.numpy as jnp
import numpy as np
from jax import lax
from jax.experimental import pallas as pl
from jax.experimental.pallas import tpu as pltpu
from jax.sharding import PartitionSpec as P

D = 1280
FF = 2560
BLK = 128
KMAX = 192
LMAX = 2
NB = 200
NLIVE = 96
NDEAD = NB - NLIVE
UP_COLS = FF // BLK
DOWN_COLS = D // BLK
PARTS = 2 * LMAX
PANELS = UP_COLS + DOWN_COLS
RING = 4
MOST = 2 * NDEAD
FEW = 128
HALF = BLK // 2
TILE = 32
OWN = 2 * NB // (RING * RING)
WIDE = 256
EPS_NORM = 1e-06
EPS_SCORE = 1e-06
MICRO = 2
ROWS = KMAX // MICRO
CHUNK = 512
SQ = 256
FLIP = 5
MESH = pl.DeviceIdType.MESH
F32 = jnp.float32
BF16 = jnp.bfloat16
GELU_A = 0.7978845608028654
GELU_B = 0.044715


def dot(a, b):
    return jnp.dot(a, b, preferred_element_type=F32)


def dot_t(a, b):
    return lax.dot_general(a, b, (((1,), (1,)), ((), ())), preferred_element_type=F32)


def gelu(v):
    return 0.5 * v * (1.0 + jnp.tanh(GELU_A * (v + GELU_B * (v * v * v))))


def gelu_slope(v):
    sq = v * v
    t = jnp.tanh(GELU_A * (v + GELU_B * (v * sq)))
    return 0.5 * (1.0 + t) + 0.5 * v * (1.0 - t * t) * (GELU_A * (1.0 + 3.0 * GELU_B * sq))


def chain_kernel(
    inv_ref,
    count_ref, order, kept, asked_ref, dead, panels, patches, cotangent, gain, up_hbm, down_hbm,
    left_hbm, right_hbm, slots_out, own_out, most_out,
    stage_a, stage_b, up_0, up_1, down_0, down_1, spare, xs, gs, normed, inv_std, act, hidden, pre, grad_pre,
    left, right, mask, row_tiles, all_tiles, most, most_up, most_down,
    stage_sem, left_sem, right_sem, x_send, x_recv, g_send, g_recv,
    tile_send, tile_recv, all_send, all_recv, most_send, most_recv,
):
    sections = lax.axis_size("section")
    replica = lax.axis_index("dp")
    section = lax.axis_index("section")
    first = section == 0
    last = section == sections - 1
    stages = (stage_a, stage_b)
    w_up, w_down = (up_0, up_1), (down_0, down_1)
    w_up_t, w_down_t = (down_0, down_1), (up_1, spare)

    def flag(l):
        return count_ref[:, :] > l

    def load(part):
        l, kind = part // 2, part % 2
        src = (up_hbm, down_hbm)[kind].at[l]
        return pltpu.make_async_copy(src, stages[part % 2].at[pl.ds(0, NLIVE)], stage_sem.at[part])

    stage_a[NLIVE] = jnp.zeros((BLK, BLK), BF16)
    stage_b[NLIVE] = jnp.zeros((BLK, BLK), BF16)
    load(0).start()
    load(1).start()

    barrier = pltpu.get_barrier_semaphore()

    @pl.when(jnp.logical_not(first))
    def _():
        pl.semaphore_signal(barrier, inc=1, device_id=(replica, section - 1), device_id_type=MESH)

    @pl.when(jnp.logical_not(last))
    def _():
        pl.semaphore_signal(barrier, inc=1, device_id=(replica, section + 1), device_id_type=MESH)

    px = replica // RING
    py = lax.rem(replica, RING)

    def along_y(step):
        return (px * RING + lax.rem(py + step, RING), section)

    def along_x(step):
        return (lax.rem(px + step, RING) * RING + py, section)

    for step in range(1, RING):
        pl.semaphore_signal(barrier, inc=1, device_id=along_y(step), device_id_type=MESH)
        pl.semaphore_signal(barrier, inc=1, device_id=along_x(step), device_id_type=MESH)

    def moves(source, target, sends, recvs, to):
        return [
            pltpu.make_async_remote_copy(
                src_ref=source, dst_ref=target, send_sem=sends.at[step - 1], recv_sem=recvs.at[step - 1],
                device_id=to(step), device_id_type=MESH,
            )
            for step in range(1, RING)
        ]

    def row_moves():
        return moves(mask, row_tiles.at[py], tile_send, tile_recv, along_y)

    def all_moves():
        return moves(row_tiles, all_tiles.at[px], all_send, all_recv, along_x)

    def picked(table):
        size = table.shape[0]
        hot = jnp.logical_and(
            lax.broadcasted_iota(jnp.int32, (size, KMAX), 0) == order[:, :KMAX],
            lax.broadcasted_iota(jnp.int32, (size, KMAX), 1) < kept[:, :],
        )
        return lax.dot_general(
            hot.astype(BF16), table[...], (((0,), (0,)), ((), ())), preferred_element_type=F32
        ).astype(BF16)

    @pl.when(first)
    def _():
        xs[0] = picked(patches)

    @pl.when(last)
    def _():
        gs[LMAX] = picked(cotangent)

    @pl.when(jnp.logical_or(first, last))
    def _():
        pl.semaphore_wait(barrier, 2 * (RING - 1) + 1)

    @pl.when(jnp.logical_not(jnp.logical_or(first, last)))
    def _():
        pl.semaphore_wait(barrier, 2 * (RING - 1) + 2)

    mask[...] = jnp.zeros((8, BLK), F32)
    mask[:LMAX, :OWN] = (asked_ref[...] == 1).astype(F32)
    row_tiles[py] = mask[...]
    for move in row_moves():
        move.start()

    def after_part(part):
        if part == 1:
            for move in row_moves():
                move.wait()
            all_tiles[px] = row_tiles[...]
            for move in all_moves():
                move.start()

    def settle():
        for move in all_moves():
            move.wait()
        count = jnp.zeros((1, 1), F32)
        lanes = lax.broadcasted_iota(jnp.int32, (BLK, BLK), 0)
        later = lanes < lax.broadcasted_iota(jnp.int32, (BLK, BLK), 1)
        later = later.astype(BF16)
        ones = jnp.ones((BLK, BLK), BF16)
        n = RING * RING
        under = lax.broadcasted_iota(jnp.int32, (n, n), 0) > lax.broadcasted_iota(jnp.int32, (n, n), 1)
        spots = lax.broadcasted_iota(jnp.int32, (BLK, WIDE), 1).astype(F32)
        for l in range(LMAX):
            asked = all_tiles[:, :, l, :].reshape(n, BLK) * dead[l]
            flat = asked.astype(BF16)
            totals = dot(flat, ones)
            rank = dot(flat, later) + dot(under.astype(BF16), totals.astype(BF16))
            mine = lax.broadcasted_iota(jnp.int32, (n, BLK), 0) == replica
            own_out[l:l + 1, :] = jnp.sum(jnp.where(mine, rank, 0.0), axis=0, keepdims=True)
            own_out[LMAX + l:LMAX + l + 1, :] = jnp.sum(jnp.where(mine, asked, 0.0), axis=0, keepdims=True)
            count = jnp.maximum(count, jnp.sum(totals[:, :1], axis=0, keepdims=True))
            turned = jnp.where(asked > 0.5, rank, -1.0).T
            found = jnp.zeros((8, WIDE), F32)
            for d in range(n):
                hot = (turned[:, d:d + 1] == spots).astype(BF16)
                found = found + dot(panels[d], hot)
            slots_out[l] = found.astype(jnp.int32)
        most[...] = jnp.broadcast_to(count, (8, BLK))

    def pass_up():
        return pltpu.make_async_remote_copy(
            src_ref=most, dst_ref=most_up, send_sem=most_send.at[0], recv_sem=most_recv.at[0],
            device_id=(replica, section + 1), device_id_type=MESH,
        )

    def pass_down():
        return pltpu.make_async_remote_copy(
            src_ref=most, dst_ref=most_down, send_sem=most_send.at[1], recv_sem=most_recv.at[1],
            device_id=(replica, section - 1), device_id_type=MESH,
        )

    for part in range(PARTS):
        load(part).wait()
        l, kind = part // 2, part % 2
        target, cols = ((w_up, UP_COLS), (w_down, DOWN_COLS))[kind]

        def place(rb, carry, l=l, target=target, cols=cols, part=part):
            rs = pl.ds(pl.multiple_of(rb * BLK, BLK), BLK)
            for cb in range(cols):
                target[l][rs, cb * BLK:(cb + 1) * BLK] = stages[part % 2][inv_ref[part * NB + rb * cols + cb]]
            return carry

        lax.fori_loop(0, NB // cols, place, 0)
        after_part(part)
        if part + 2 < PARTS:
            load(part + 2).start()

    def rows_of(mb):
        return pl.ds(pl.multiple_of(mb * ROWS, ROWS), ROWS)

    def cols_of(j, size):
        return pl.ds(pl.multiple_of(j * size, size), size)

    def send_x(mb):
        return pltpu.make_async_remote_copy(
            src_ref=xs.at[LMAX, rows_of(mb)], dst_ref=xs.at[0, rows_of(mb)],
            send_sem=x_send.at[mb], recv_sem=x_recv.at[mb],
            device_id=(replica, section + 1), device_id_type=MESH,
        )

    def send_g(mb):
        return pltpu.make_async_remote_copy(
            src_ref=gs.at[0, rows_of(mb)], dst_ref=gs.at[LMAX, rows_of(mb)],
            send_sem=g_send.at[mb], recv_sem=g_recv.at[mb],
            device_id=(replica, section - 1), device_id_type=MESH,
        )

    def forward(mb, carry):
        r = rows_of(mb)

        @pl.when(jnp.logical_not(first))
        def _():
            send_x(mb).wait_recv()

        for l in range(LMAX):
            x = xs[l, r, :].astype(F32)
            centred = x - jnp.mean(x, axis=-1, keepdims=True)
            inv = lax.rsqrt(jnp.mean(centred * centred, axis=-1, keepdims=True) + EPS_NORM)
            n = centred * inv
            normed[l, r, :] = n
            inv_std[l, r, :] = jnp.broadcast_to(inv, (ROWS, BLK))
            act[l, r, :] = (n * gain[l:l + 1, :]).astype(BF16)

            def up_chunk(j, c, l=l):
                cs = cols_of(j, CHUNK)
                v = dot(act[l, r, :], w_up[l][:, cs])
                pre[l, r, cs] = v
                hidden[l, r, cs] = gelu(v).astype(BF16)
                return c

            lax.fori_loop(0, FF // CHUNK, up_chunk, 0, unroll=True)

            def down_chunk(j, c, l=l):
                cs = cols_of(j, 256)
                v = dot(hidden[l, r, :], w_down[l][:, cs])
                had = xs[l, r, cs]
                moved = (had.astype(F32) + v).astype(BF16)
                xs[l + 1, r, cs] = jnp.where(flag(l), moved, had)
                return c

            lax.fori_loop(0, D // 256, down_chunk, 0, unroll=True)

        @pl.when(jnp.logical_not(last))
        def _():
            send_x(mb).start()

        return carry

    @pl.when(jnp.logical_not(first))
    def _():
        settle()

    lax.fori_loop(0, MICRO, forward, 0)

    @pl.when(first)
    def _():
        settle()

    @pl.when(jnp.logical_not(first))
    def _():
        pass_up().wait_recv()
        most[...] = jnp.maximum(most[...], most_up[...])

    @pl.when(jnp.logical_not(last))
    def _():
        pass_up().start()


    def save_left(l):
        return pltpu.make_async_copy(left.at[l], left_hbm.at[l], left_sem.at[l])

    def keep_left():
        for l in range(LMAX):
            for j in range(UP_COLS):
                h = jnp.where(flag(l), hidden[l, :, j * BLK:(j + 1) * BLK], jnp.zeros((KMAX, BLK), BF16))
                left[l, DOWN_COLS + j] = h.T
            for j in range(DOWN_COLS):
                a = jnp.where(flag(l), act[l, :, j * BLK:(j + 1) * BLK], jnp.zeros((KMAX, BLK), BF16))
                left[l, j] = a.T
            save_left(l).start()

    @pl.when(jnp.logical_not(last))
    def _():
        keep_left()

    for source, target in ((down_1, spare), (up_1, down_1), (down_0, up_1), (up_0, down_0)):
        def flip(i, c, source=source, target=target):
            rs = cols_of(i, SQ)
            for j in range(source.shape[1] // SQ):
                target[j * SQ:(j + 1) * SQ, rs] = source[rs, j * SQ:(j + 1) * SQ].T
            return c

        lax.fori_loop(0, source.shape[0] // SQ, flip, 0, unroll=FLIP)

    def save_right(l):
        return pltpu.make_async_copy(right.at[l], right_hbm.at[l], right_sem.at[l])

    def backward(mb, carry):
        r = rows_of(mb)

        @pl.when(jnp.logical_not(last))
        def _():
            send_g(mb).wait_recv()

        for l in reversed(range(LMAX)):
            def hidden_chunk(j, c, l=l):
                cs = cols_of(j, CHUNK)
                v = dot(gs[l + 1, r, :], w_down_t[l][:, cs])
                p = (gelu_slope(pre[l, r, cs]) * v).astype(BF16)
                grad_pre[l, r, cs] = p
                for b in range(CHUNK // BLK):
                    right[l, j * (CHUNK // BLK) + b, r, :] = p[:, b * BLK:(b + 1) * BLK]
                return c

            lax.fori_loop(0, FF // CHUNK, hidden_chunk, 0, unroll=True)

            def act_chunk(j, c, l=l):
                cs = cols_of(j, 256)
                v = dot(grad_pre[l, r, :], w_up_t[l][:, cs])
                pre[l, r, cs] = v * gain[l:l + 1, cs]
                return c

            lax.fori_loop(0, D // 256, act_chunk, 0, unroll=True)
            u = pre[l, r, :D]
            n = normed[l, r, :]
            step = inv_std[l, r, :1] * (
                u - jnp.mean(u, axis=-1, keepdims=True) - n * jnp.mean(u * n, axis=-1, keepdims=True)
            )
            had = gs[l + 1, r, :]
            for b in range(DOWN_COLS):
                right[l, UP_COLS + b, r, :] = had[:, b * BLK:(b + 1) * BLK]
            gs[l, r, :] = jnp.where(flag(l), (had.astype(F32) + step).astype(BF16), had)

        @pl.when(jnp.logical_not(first))
        def _():
            send_g(mb).start()

        return carry

    lax.fori_loop(0, MICRO, backward, 0)

    @pl.when(jnp.logical_not(last))
    def _():
        pass_up().wait_send()
        pass_down().wait_recv()
        most[...] = jnp.maximum(most[...], most_down[...])

    @pl.when(jnp.logical_not(first))
    def _():
        pass_down().start()

    most_out[...] = most[...]

    for l in range(LMAX):
        save_right(l).start()

    @pl.when(last)
    def _():
        keep_left()

    def drain(mb, carry):
        @pl.when(jnp.logical_not(last))
        def _():
            send_x(mb).wait_send()

        @pl.when(jnp.logical_not(first))
        def _():
            send_g(mb).wait_send()

        return carry

    lax.fori_loop(0, MICRO, drain, 0)

    @pl.when(jnp.logical_not(first))
    def _():
        pass_down().wait_send()

    for l in range(LMAX):
        save_left(l).wait()
        save_right(l).wait()


def chain(inv, count, order, kept, asked, dead, panels, patches, cotangent, gain, up, down):
    smem = pl.BlockSpec(memory_space=pltpu.SMEM)
    vmem = pl.BlockSpec(memory_space=pltpu.VMEM)
    hbm = pl.BlockSpec(memory_space=pl.ANY)
    return pl.pallas_call(
        chain_kernel,
        out_shape=(
            jax.ShapeDtypeStruct((LMAX, PANELS, BLK, KMAX), BF16),
            jax.ShapeDtypeStruct((LMAX, PANELS, KMAX, BLK), BF16),
            jax.ShapeDtypeStruct((LMAX, 8, WIDE), jnp.int32),
            jax.ShapeDtypeStruct((2 * LMAX, BLK), F32),
            jax.ShapeDtypeStruct((8, BLK), F32),
        ),
        in_specs=[smem] + [vmem] * 9 + [hbm] * 2,
        out_specs=(hbm, hbm, vmem, vmem, vmem),
        scratch_shapes=[
            pltpu.VMEM((NLIVE + 1, BLK, BLK), BF16),
            pltpu.VMEM((NLIVE + 1, BLK, BLK), BF16),
            *[pltpu.VMEM((D, FF), BF16)] * 2,
            *[pltpu.VMEM((FF, D), BF16)] * 2,
            pltpu.VMEM((D, FF), BF16),
            pltpu.VMEM((LMAX + 1, KMAX, D), BF16),
            pltpu.VMEM((LMAX + 1, KMAX, D), BF16),
            pltpu.VMEM((LMAX, KMAX, D), F32),
            pltpu.VMEM((LMAX, KMAX, BLK), F32),
            pltpu.VMEM((LMAX, KMAX, D), BF16),
            pltpu.VMEM((LMAX, KMAX, FF), BF16),
            pltpu.VMEM((LMAX, KMAX, FF), F32),
            pltpu.VMEM((LMAX, KMAX, FF), BF16),
            pltpu.VMEM((LMAX, PANELS, BLK, KMAX), BF16),
            pltpu.VMEM((LMAX, PANELS, KMAX, BLK), BF16),
            pltpu.VMEM((8, BLK), F32),
            pltpu.VMEM((RING, 8, BLK), F32),
            pltpu.VMEM((RING, RING, 8, BLK), F32),
            *[pltpu.VMEM((8, BLK), F32)] * 3,
            pltpu.SemaphoreType.DMA((PARTS,)),
            pltpu.SemaphoreType.DMA((LMAX,)),
            pltpu.SemaphoreType.DMA((LMAX,)),
            pltpu.SemaphoreType.DMA((MICRO,)),
            pltpu.SemaphoreType.DMA((MICRO,)),
            pltpu.SemaphoreType.DMA((MICRO,)),
            pltpu.SemaphoreType.DMA((MICRO,)),
            *[pltpu.SemaphoreType.DMA((RING - 1,))] * 4,
            *[pltpu.SemaphoreType.DMA((2,))] * 2,
        ],
        compiler_params=pltpu.CompilerParams(
            collective_id=0, has_side_effects=True, vmem_limit_bytes=60 * 1024 * 1024
        ),
        cost_estimate=pl.CostEstimate(flops=35_000_000_000, bytes_accessed=30_000_000, transcendentals=2_000_000),
    )(inv, count, order, kept, asked, dead, panels, patches, cotangent, gain, up, down)


def live_tables(up_index, down_index):
    listed = jnp.stack([up_index, down_index], axis=1).reshape(PARTS, NLIVE)
    hit = listed[:, :, None] == jnp.arange(NB)[None, None, :]
    live = jnp.any(hit, axis=1)
    inv = jnp.where(live, jnp.sum(jnp.where(hit, jnp.arange(NLIVE)[None, :, None], 0), axis=1), NLIVE)
    return inv.astype(jnp.int32), live.reshape(LMAX, 2 * NB)


def sums_kernel(
    PER, slots, left_hbm, right_hbm, out_ref,
    left_0, left_1, right_0, right_1,
    opp_0, opp_1, nxt_0, nxt_1, prv_0, prv_1, mid_0, mid_1,
    ra_0, ra_1, rb_0, rb_1, ia_0, ia_1, ib_0, ib_1,
    sa_0, sa_1, sb_0, sb_1, ja_0, ja_1, jb_0, jb_1,
    squares, mine, all_tiles,
    load_sem, send_sem, recv_sem, tile_send, tile_recv,
):
    section = lax.axis_index("section")
    replica = lax.axis_index("dp")
    px = replica // RING
    py = lax.rem(replica, RING)

    def peer(axis, step):
        if axis == 0:
            return (lax.rem(px + step, RING) * RING + py, section)
        return (px * RING + lax.rem(py + step, RING), section)

    lefts, rights = (left_1, left_0), (right_1, right_0)

    def load(h):
        l = LMAX - 1 - h
        return (
            pltpu.make_async_copy(left_hbm.at[l], lefts[h], load_sem.at[h, 0]),
            pltpu.make_async_copy(right_hbm.at[l], rights[h], load_sem.at[h, 1]),
        )

    for h in range(2):
        for copy in load(h):
            copy.start()

    barrier = pltpu.get_barrier_semaphore()
    everyone = RING * RING

    def other(step):
        return (lax.rem(replica + step, everyone), section)

    for step in range(1, everyone):
        pl.semaphore_signal(barrier, inc=1, device_id=other(step), device_id_type=MESH)
    pl.semaphore_wait(barrier, everyone - 1)
    for h in range(2):
        for copy in load(h):
            copy.wait()

    opp, nxt, prv, mid = (opp_0, opp_1), (nxt_0, nxt_1), (prv_0, prv_1), (mid_0, mid_1)
    ra, rb, ia, ib = (ra_0, ra_1), (rb_0, rb_1), (ia_0, ia_1), (ib_0, ib_1)
    sa, sb, ja, jb = (sa_0, sa_1), (sb_0, sb_1), (ja_0, ja_1), (jb_0, jb_1)
    place = (px, py)

    def at(axis, step):
        return lax.rem(place[axis] + step, RING)

    def block(h, f, c, g):
        l, s = LMAX - 1 - h, (f * PER + c) * RING + g
        return dot(lefts[h][slots[l, 0, s]], rights[h][slots[l, 1, s]])

    def send(h, kind, c, src, dst, axis, step):
        return pltpu.make_async_remote_copy(
            src_ref=src, dst_ref=dst, send_sem=send_sem.at[h, kind, c], recv_sem=recv_sem.at[h, kind, c],
            device_id=peer(axis, step), device_id_type=MESH,
        )

    def copies(h, c):
        first, second = h, 1 - h
        far = at(second, 2)
        return (
            send(h, 0, c, opp[h].at[c, pl.ds(0, 2)], ra[h].at[c], first, 1),
            send(h, 1, c, opp[h].at[c, pl.ds(2, 2)], rb[h].at[c], first, 3),
            send(h, 2, c, nxt[h].at[c], ia[h].at[c], first, 1),
            send(h, 3, c, prv[h].at[c], ib[h].at[c], first, 3),
            send(h, 4, c, mid[h].at[c, far, pl.ds(0, HALF)], sa[h].at[c], second, 1),
            send(h, 5, c, mid[h].at[c, far, pl.ds(HALF, HALF)], sb[h].at[c], second, 3),
            send(h, 6, c, mid[h].at[c, at(second, 1)], ja[h].at[c], second, 1),
            send(h, 7, c, mid[h].at[c, at(second, 3)], jb[h].at[c], second, 3),
        )

    def far_units(c, carry):
        for h in range(2):
            for g in range(RING):
                opp[h][c, g] = block(h, at(h, 2), c, g).astype(BF16)
            moves = copies(h, c)
            moves[0].start()
            moves[1].start()
        return carry

    def near_units(c, carry):
        for h in range(2):
            moves = copies(h, c)
            ahead = [block(h, at(h, 1), c, g) for g in range(RING)]
            behind = [block(h, at(h, 3), c, g) for g in range(RING)]
            moves[0].wait_recv()
            for g in range(RING):
                v = ahead[g] + ra[h][c, g].astype(F32) if g < 2 else ahead[g]
                nxt[h][c, g] = v.astype(BF16)
            moves[2].start()
            moves[1].wait_recv()
            for g in range(RING):
                v = behind[g] + rb[h][c, g - 2].astype(F32) if g >= 2 else behind[g]
                prv[h][c, g] = v.astype(BF16)
            moves[3].start()
        return carry

    def own_units(c, carry):
        for h in range(2):
            moves = copies(h, c)
            own = [block(h, place[h], c, g) for g in range(RING)]
            moves[2].wait_recv()
            moves[3].wait_recv()
            for g in range(RING):
                v = own[g] + ia[h][c, g].astype(F32) + ib[h][c, g].astype(F32)
                mid[h][c, g] = v.astype(BF16)
            moves[4].start()
            moves[5].start()
        return carry

    def second_axis(c, carry):
        for h in range(2):
            moves = copies(h, c)
            ahead, behind = at(1 - h, 1), at(1 - h, 3)
            moves[4].wait_recv()
            top = pl.ds(0, HALF)
            v = mid[h][c, ahead, top, :].astype(F32) + sa[h][c].astype(F32)
            mid[h][c, ahead, top, :] = v.astype(BF16)
            moves[6].start()
            moves[5].wait_recv()
            low = pl.ds(HALF, HALF)
            v = mid[h][c, behind, low, :].astype(F32) + sb[h][c].astype(F32)
            mid[h][c, behind, low, :] = v.astype(BF16)
            moves[7].start()
        return carry

    def totals(c, carry):
        for h in range(2):
            moves = copies(h, c)
            moves[6].wait_recv()
            moves[7].wait_recv()
            v = mid[h][c, place[1 - h]].astype(F32) + ja[h][c].astype(F32) + jb[h][c].astype(F32)
            squares[h, pl.ds(c, 1), :] = jnp.sum(v * v, axis=0, keepdims=True)
        return carry

    def drain(c, carry):
        for h in range(2):
            for move in copies(h, c):
                move.wait_send()
        return carry

    squares[...] = jnp.zeros_like(squares)
    for step in (far_units, near_units, own_units, second_axis, totals):
        lax.fori_loop(0, PER, step, 0)
    rows_total = float(RING * RING * KMAX)
    mean = jnp.sum(squares[...].reshape(TILE, BLK), axis=1, keepdims=True) * (1.0 / (BLK * BLK))
    mine[...] = jnp.broadcast_to(jnp.sqrt(mean / rows_total + EPS_SCORE), (TILE, BLK))

    all_tiles[replica] = mine[...]

    def tile(step):
        return pltpu.make_async_remote_copy(
            src_ref=mine, dst_ref=all_tiles.at[replica], send_sem=tile_send.at[step - 1],
            recv_sem=tile_recv.at[step - 1], device_id=other(step), device_id_type=MESH,
        )

    for step in range(1, everyone):
        tile(step).start()
    for step in range(1, everyone):
        tile(step).wait()
    out_ref[...] = all_tiles[...]
    lax.fori_loop(0, PER, drain, 0)


def sums(size, number, slots, left, right):
    PER = size // (RING * RING)
    smem = pl.BlockSpec(memory_space=pltpu.SMEM)
    hbm = pl.BlockSpec(memory_space=pl.ANY)

    def blocks(*lead):
        return [pltpu.VMEM((PER, *lead, BLK), BF16)] * 2

    return pl.pallas_call(
        functools.partial(sums_kernel, PER),
        out_shape=jax.ShapeDtypeStruct((RING * RING, TILE, BLK), F32),
        in_specs=[smem] + [hbm] * 2,
        out_specs=pl.BlockSpec(memory_space=pltpu.VMEM),
        scratch_shapes=[
            *[pltpu.VMEM((PANELS, BLK, KMAX), BF16)] * 2,
            *[pltpu.VMEM((PANELS, KMAX, BLK), BF16)] * 2,
            *blocks(RING, BLK), *blocks(RING, BLK), *blocks(RING, BLK), *blocks(RING, BLK),
            *blocks(2, BLK), *blocks(2, BLK), *blocks(RING, BLK), *blocks(RING, BLK),
            *blocks(HALF), *blocks(HALF), *blocks(BLK), *blocks(BLK),
            pltpu.VMEM((2, TILE // 2, BLK), F32),
            pltpu.VMEM((TILE, BLK), F32),
            pltpu.VMEM((RING * RING, TILE, BLK), F32),
            pltpu.SemaphoreType.DMA((2, 2)),
            pltpu.SemaphoreType.DMA((2, 8, PER)),
            pltpu.SemaphoreType.DMA((2, 8, PER)),
            *[pltpu.SemaphoreType.DMA((RING * RING - 1,))] * 2,
        ],
        compiler_params=pltpu.CompilerParams(
            collective_id=number, has_side_effects=True, vmem_limit_bytes=60 * 1024 * 1024
        ),
        cost_estimate=pl.CostEstimate(flops=3_000_000_000, bytes_accessed=8_000_000, transcendentals=0),
    )(slots, left, right)


def every_score(size, number, slots, left, right):
    per = size // (RING * RING)
    tiles = sums(size, number, slots, left, right)
    half = TILE // 2
    tiles = tiles[:, :, 0].reshape(RING, RING, TILE)
    late = tiles[:, :, :per].transpose(0, 2, 1).reshape(size)
    early = tiles[:, :, half:half + per].transpose(1, 2, 0).reshape(size)
    return jnp.pad(jnp.stack([early, late]), ((0, 0), (0, MOST - size)))


def panel_numbers():
    q = np.arange(2 * NB)
    lower = q >= NB
    inner = np.where(lower, q - NB, q)
    cols = np.where(lower, DOWN_COLS, UP_COLS)
    row = np.where(lower, inner // cols + DOWN_COLS, inner // cols)
    col = np.where(lower, inner % cols + UP_COLS, inner % cols)
    table = np.zeros((RING * RING, 8, BLK), np.float32)
    table[:, 0, :OWN] = row.reshape(-1, OWN)
    table[:, 1, :OWN] = col.reshape(-1, OWN)
    return jnp.asarray(table, BF16)


def body(patches, cotangent, keep_order, keep_count, destination, norm_gain, up_blocks, up_index,
         down_blocks, down_index, layer_count, regrow_mask):
    inv, live = live_tables(up_index, down_index)
    dead = jnp.logical_not(live).reshape(LMAX, RING * RING, OWN)
    dead = jnp.pad(dead.astype(F32), ((0, 0), (0, 0), (0, BLK - OWN)))
    left, right, slots, own, most = chain(
        inv.reshape(-1), layer_count.reshape(1, 1), keep_order, keep_count.reshape(1, 1), regrow_mask, dead,
        panel_numbers(), patches[0], cotangent[0], norm_gain,
        up_blocks, down_blocks,
    )
    every = lax.cond(
        most[0, 0] < FEW + 0.5,
        functools.partial(every_score, FEW, 1),
        functools.partial(every_score, MOST, 2),
        slots, left, right,
    )
    rank, wanted = own[:LMAX, :OWN], own[LMAX:, :OWN]
    spots = jnp.arange(MOST).astype(F32)
    picked = jnp.sum(jnp.where(rank[:, :, None] == spots, every[:, None, :], 0.0), axis=2)
    return jnp.where(wanted > 0.5, picked, 0.0)


def solution(mesh):
    return jax.shard_map(
        body, mesh=mesh,
        in_specs=(
            P("dp", None, None), P("dp", None, None), P("dp", None), P("dp"), P("dp", None),
            P("section", None), P("section", None, None, None), P("section", None),
            P("section", None, None, None), P("section", None), P("section"), P("section", "dp"),
        ),
        out_specs=P("section", "dp"), check_vma=False,
    )
```

```python
import functools
import jax
import jax.numpy as jnp
import numpy as np
from jax import lax
from jax.experimental import pallas as pl
from jax.experimental.pallas import tpu as pltpu
from jax.sharding import PartitionSpec as P

D = 1280
FF = 2560
BLK = 128
KMAX = 192
LMAX = 2
NB = 200
NLIVE = 96
NDEAD = NB - NLIVE
UP_COLS = FF // BLK
DOWN_COLS = D // BLK
PARTS = 2 * LMAX
PANELS = UP_COLS + DOWN_COLS
RING = 4
MOST = 2 * NDEAD
FEW = 128
HALF = BLK // 2
TILE = 32
OWN = 2 * NB // (RING * RING)
WIDE = 256
EPS_NORM = 1e-06
EPS_SCORE = 1e-06
MICRO = 2
ROWS = KMAX // MICRO
CHUNK = 512
SQ = 256
FLIP = 5
MESH = pl.DeviceIdType.MESH
F32 = jnp.float32
BF16 = jnp.bfloat16
GELU_A = 0.7978845608028654
GELU_B = 0.044715


def dot(a, b):
    return jnp.dot(a, b, preferred_element_type=F32)


def dot_t(a, b):
    return lax.dot_general(a, b, (((1,), (1,)), ((), ())), preferred_element_type=F32)


def gelu(v):
    return 0.5 * v * (1.0 + jnp.tanh(GELU_A * (v + GELU_B * (v * v * v))))


def gelu_slope(v):
    sq = v * v
    t = jnp.tanh(GELU_A * (v + GELU_B * (v * sq)))
    return 0.5 * (1.0 + t) + 0.5 * v * (1.0 - t * t) * (GELU_A * (1.0 + 3.0 * GELU_B * sq))


def chain_kernel(
    inv_ref,
    count_ref, order, kept, asked_ref, dead, panels, patches, cotangent, gain, up_hbm, down_hbm,
    left_hbm, right_hbm, slots_out, own_out, most_out,
    stage_a, stage_b, up_0, up_1, down_0, down_1, spare, xs, gs, normed, inv_std, act, hidden, pre, grad_pre,
    left, right, mask, row_tiles, all_tiles, most, most_up, most_down,
    stage_sem, left_sem, right_sem, x_send, x_recv, g_send, g_recv,
    tile_send, tile_recv, all_send, all_recv, most_send, most_recv,
):
    sections = lax.axis_size("section")
    replica = lax.axis_index("dp")
    section = lax.axis_index("section")
    first = section == 0
    last = section == sections - 1
    stages = (stage_a, stage_b)
    w_up, w_down = (up_0, up_1), (down_0, down_1)
    w_up_t, w_down_t = (down_0, down_1), (up_1, spare)

    def flag(l):
        return count_ref[:, :] > l

    def load(part):
        l, kind = part // 2, part % 2
        src = (up_hbm, down_hbm)[kind].at[l]
        return pltpu.make_async_copy(src, stages[part % 2].at[pl.ds(0, NLIVE)], stage_sem.at[part])

    stage_a[NLIVE] = jnp.zeros((BLK, BLK), BF16)
    stage_b[NLIVE] = jnp.zeros((BLK, BLK), BF16)
    load(0).start()
    load(1).start()

    barrier = pltpu.get_barrier_semaphore()

    @pl.when(jnp.logical_not(first))
    def _():
        pl.semaphore_signal(barrier, inc=1, device_id=(replica, section - 1), device_id_type=MESH)

    @pl.when(jnp.logical_not(last))
    def _():
        pl.semaphore_signal(barrier, inc=1, device_id=(replica, section + 1), device_id_type=MESH)

    px = replica // RING
    py = lax.rem(replica, RING)

    def along_y(step):
        return (px * RING + lax.rem(py + step, RING), section)

    def along_x(step):
        return (lax.rem(px + step, RING) * RING + py, section)

    for step in range(1, RING):
        pl.semaphore_signal(barrier, inc=1, device_id=along_y(step), device_id_type=MESH)
        pl.semaphore_signal(barrier, inc=1, device_id=along_x(step), device_id_type=MESH)

    def moves(source, target, sends, recvs, to):
        return [
            pltpu.make_async_remote_copy(
                src_ref=source, dst_ref=target, send_sem=sends.at[step - 1], recv_sem=recvs.at[step - 1],
                device_id=to(step), device_id_type=MESH,
            )
            for step in range(1, RING)
        ]

    def row_moves():
        return moves(mask, row_tiles.at[py], tile_send, tile_recv, along_y)

    def all_moves():
        return moves(row_tiles, all_tiles.at[px], all_send, all_recv, along_x)

    def picked(table):
        size = table.shape[0]
        hot = jnp.logical_and(
            lax.broadcasted_iota(jnp.int32, (size, KMAX), 0) == order[:, :KMAX],
            lax.broadcasted_iota(jnp.int32, (size, KMAX), 1) < kept[:, :],
        )
        return lax.dot_general(
            hot.astype(BF16), table[...], (((0,), (0,)), ((), ())), preferred_element_type=F32
        ).astype(BF16)

    @pl.when(first)
    def _():
        xs[0] = picked(patches)

    @pl.when(last)
    def _():
        gs[LMAX] = picked(cotangent)

    mask[...] = jnp.zeros((8, BLK), F32)
    mask[:LMAX, :OWN] = (asked_ref[...] == 1).astype(F32)
    row_tiles[py] = mask[...]

    def meet():
        @pl.when(jnp.logical_or(first, last))
        def _():
            pl.semaphore_wait(barrier, 2 * (RING - 1) + 1)

        @pl.when(jnp.logical_not(jnp.logical_or(first, last)))
        def _():
            pl.semaphore_wait(barrier, 2 * (RING - 1) + 2)

        for move in row_moves():
            move.start()

    def settle():
        for move in row_moves():
            move.wait()
        all_tiles[px] = row_tiles[...]
        for move in all_moves():
            move.start()
        for move in all_moves():
            move.wait()
        count = jnp.zeros((1, 1), F32)
        lanes = lax.broadcasted_iota(jnp.int32, (BLK, BLK), 0)
        later = lanes < lax.broadcasted_iota(jnp.int32, (BLK, BLK), 1)
        later = later.astype(BF16)
        ones = jnp.ones((BLK, BLK), BF16)
        n = RING * RING
        under = lax.broadcasted_iota(jnp.int32, (n, n), 0) > lax.broadcasted_iota(jnp.int32, (n, n), 1)
        spots = lax.broadcasted_iota(jnp.int32, (BLK, WIDE), 1).astype(F32)
        for l in range(LMAX):
            asked = all_tiles[:, :, l, :].reshape(n, BLK) * dead[l]
            flat = asked.astype(BF16)
            totals = dot(flat, ones)
            rank = dot(flat, later) + dot(under.astype(BF16), totals.astype(BF16))
            mine = lax.broadcasted_iota(jnp.int32, (n, BLK), 0) == replica
            own_out[l:l + 1, :] = jnp.sum(jnp.where(mine, rank, 0.0), axis=0, keepdims=True)
            own_out[LMAX + l:LMAX + l + 1, :] = jnp.sum(jnp.where(mine, asked, 0.0), axis=0, keepdims=True)
            count = jnp.maximum(count, jnp.sum(totals[:, :1], axis=0, keepdims=True))
            turned = jnp.where(asked > 0.5, rank, -1.0).T
            found = jnp.zeros((8, WIDE), F32)
            for d in range(n):
                hot = (turned[:, d:d + 1] == spots).astype(BF16)
                found = found + dot(panels[d], hot)
            slots_out[l] = found.astype(jnp.int32)
        most[...] = jnp.broadcast_to(count, (8, BLK))

    def pass_up():
        return pltpu.make_async_remote_copy(
            src_ref=most, dst_ref=most_up, send_sem=most_send.at[0], recv_sem=most_recv.at[0],
            device_id=(replica, section + 1), device_id_type=MESH,
        )

    def pass_down():
        return pltpu.make_async_remote_copy(
            src_ref=most, dst_ref=most_down, send_sem=most_send.at[1], recv_sem=most_recv.at[1],
            device_id=(replica, section - 1), device_id_type=MESH,
        )

    for part in range(PARTS):
        load(part).wait()
        l, kind = part // 2, part % 2
        target, cols = ((w_up, UP_COLS), (w_down, DOWN_COLS))[kind]

        def place(rb, carry, l=l, target=target, cols=cols, part=part):
            rs = pl.ds(pl.multiple_of(rb * BLK, BLK), BLK)
            for cb in range(cols):
                target[l][rs, cb * BLK:(cb + 1) * BLK] = stages[part % 2][inv_ref[part * NB + rb * cols + cb]]
            return carry

        lax.fori_loop(0, NB // cols, place, 0)
        if part == 1:
            meet()
        if part + 2 < PARTS:
            load(part + 2).start()

    def rows_of(mb):
        return pl.ds(pl.multiple_of(mb * ROWS, ROWS), ROWS)

    def cols_of(j, size):
        return pl.ds(pl.multiple_of(j * size, size), size)

    def send_x(mb):
        return pltpu.make_async_remote_copy(
            src_ref=xs.at[LMAX, rows_of(mb)], dst_ref=xs.at[0, rows_of(mb)],
            send_sem=x_send.at[mb], recv_sem=x_recv.at[mb],
            device_id=(replica, section + 1), device_id_type=MESH,
        )

    def send_g(mb):
        return pltpu.make_async_remote_copy(
            src_ref=gs.at[0, rows_of(mb)], dst_ref=gs.at[LMAX, rows_of(mb)],
            send_sem=g_send.at[mb], recv_sem=g_recv.at[mb],
            device_id=(replica, section - 1), device_id_type=MESH,
        )

    def forward(mb, carry):
        r = rows_of(mb)

        @pl.when(jnp.logical_not(first))
        def _():
            send_x(mb).wait_recv()

        for l in range(LMAX):
            x = xs[l, r, :].astype(F32)
            centred = x - jnp.mean(x, axis=-1, keepdims=True)
            inv = lax.rsqrt(jnp.mean(centred * centred, axis=-1, keepdims=True) + EPS_NORM)
            n = centred * inv
            normed[l, r, :] = n
            inv_std[l, r, :] = jnp.broadcast_to(inv, (ROWS, BLK))
            act[l, r, :] = (n * gain[l:l + 1, :]).astype(BF16)

            def up_chunk(j, c, l=l):
                cs = cols_of(j, CHUNK)
                v = dot(act[l, r, :], w_up[l][:, cs])
                pre[l, r, cs] = v
                hidden[l, r, cs] = gelu(v).astype(BF16)
                return c

            lax.fori_loop(0, FF // CHUNK, up_chunk, 0, unroll=True)

            def down_chunk(j, c, l=l):
                cs = cols_of(j, 256)
                v = dot(hidden[l, r, :], w_down[l][:, cs])
                had = xs[l, r, cs]
                moved = (had.astype(F32) + v).astype(BF16)
                xs[l + 1, r, cs] = jnp.where(flag(l), moved, had)
                return c

            lax.fori_loop(0, D // 256, down_chunk, 0, unroll=True)

        @pl.when(jnp.logical_not(last))
        def _():
            send_x(mb).start()

        return carry

    def turn_matrix(source, target):
        def flip(i, c):
            rs = cols_of(i, SQ)
            for j in range(source.shape[1] // SQ):
                target[j * SQ:(j + 1) * SQ, rs] = source[rs, j * SQ:(j + 1) * SQ].T
            return c

        lax.fori_loop(0, source.shape[0] // SQ, flip, 0, unroll=FLIP)

    @pl.when(jnp.logical_not(first))
    def _():
        settle()

    @pl.when(last)
    def _():
        turn_matrix(down_1, spare)

    lax.fori_loop(0, MICRO, forward, 0)

    @pl.when(first)
    def _():
        settle()

    @pl.when(jnp.logical_not(first))
    def _():
        pass_up().wait_recv()
        most[...] = jnp.maximum(most[...], most_up[...])

    @pl.when(jnp.logical_not(last))
    def _():
        pass_up().start()


    def save_left(l):
        return pltpu.make_async_copy(left.at[l], left_hbm.at[l], left_sem.at[l])

    def keep_left():
        for l in range(LMAX):
            for j in range(UP_COLS):
                h = jnp.where(flag(l), hidden[l, :, j * BLK:(j + 1) * BLK], jnp.zeros((KMAX, BLK), BF16))
                left[l, DOWN_COLS + j] = h.T
            for j in range(DOWN_COLS):
                a = jnp.where(flag(l), act[l, :, j * BLK:(j + 1) * BLK], jnp.zeros((KMAX, BLK), BF16))
                left[l, j] = a.T
            save_left(l).start()

    @pl.when(jnp.logical_not(last))
    def _():
        keep_left()

    @pl.when(jnp.logical_not(last))
    def _():
        turn_matrix(down_1, spare)

    for source, target in ((up_1, down_1), (down_0, up_1), (up_0, down_0)):
        turn_matrix(source, target)

    def save_right(l):
        return pltpu.make_async_copy(right.at[l], right_hbm.at[l], right_sem.at[l])

    def backward(mb, carry):
        r = rows_of(mb)

        @pl.when(jnp.logical_not(last))
        def _():
            send_g(mb).wait_recv()

        for l in reversed(range(LMAX)):
            def hidden_chunk(j, c, l=l):
                cs = cols_of(j, CHUNK)
                v = dot(gs[l + 1, r, :], w_down_t[l][:, cs])
                p = (gelu_slope(pre[l, r, cs]) * v).astype(BF16)
                grad_pre[l, r, cs] = p
                for b in range(CHUNK // BLK):
                    right[l, j * (CHUNK // BLK) + b, r, :] = p[:, b * BLK:(b + 1) * BLK]
                return c

            lax.fori_loop(0, FF // CHUNK, hidden_chunk, 0, unroll=True)

            def act_chunk(j, c, l=l):
                cs = cols_of(j, 256)
                v = dot(grad_pre[l, r, :], w_up_t[l][:, cs])
                pre[l, r, cs] = v * gain[l:l + 1, cs]
                return c

            lax.fori_loop(0, D // 256, act_chunk, 0, unroll=True)
            u = pre[l, r, :D]
            n = normed[l, r, :]
            step = inv_std[l, r, :1] * (
                u - jnp.mean(u, axis=-1, keepdims=True) - n * jnp.mean(u * n, axis=-1, keepdims=True)
            )
            had = gs[l + 1, r, :]
            for b in range(DOWN_COLS):
                right[l, UP_COLS + b, r, :] = had[:, b * BLK:(b + 1) * BLK]
            gs[l, r, :] = jnp.where(flag(l), (had.astype(F32) + step).astype(BF16), had)

        @pl.when(jnp.logical_not(first))
        def _():
            send_g(mb).start()

        return carry

    lax.fori_loop(0, MICRO, backward, 0)

    @pl.when(jnp.logical_not(last))
    def _():
        pass_up().wait_send()
        pass_down().wait_recv()
        most[...] = jnp.maximum(most[...], most_down[...])

    @pl.when(jnp.logical_not(first))
    def _():
        pass_down().start()

    most_out[...] = most[:1, :1]

    for l in range(LMAX):
        save_right(l).start()

    @pl.when(last)
    def _():
        keep_left()

    def drain(mb, carry):
        @pl.when(jnp.logical_not(last))
        def _():
            send_x(mb).wait_send()

        @pl.when(jnp.logical_not(first))
        def _():
            send_g(mb).wait_send()

        return carry

    lax.fori_loop(0, MICRO, drain, 0)

    @pl.when(jnp.logical_not(first))
    def _():
        pass_down().wait_send()

    for l in range(LMAX):
        save_left(l).wait()
        save_right(l).wait()


def chain(inv, count, order, kept, asked, dead, panels, patches, cotangent, gain, up, down):
    smem = pl.BlockSpec(memory_space=pltpu.SMEM)
    vmem = pl.BlockSpec(memory_space=pltpu.VMEM)
    hbm = pl.BlockSpec(memory_space=pl.ANY)
    return pl.pallas_call(
        chain_kernel,
        out_shape=(
            jax.ShapeDtypeStruct((LMAX, PANELS, BLK, KMAX), BF16),
            jax.ShapeDtypeStruct((LMAX, PANELS, KMAX, BLK), BF16),
            jax.ShapeDtypeStruct((LMAX, 8, WIDE), jnp.int32),
            jax.ShapeDtypeStruct((2 * LMAX, BLK), F32),
            jax.ShapeDtypeStruct((1, 1), F32),
        ),
        in_specs=[smem] + [vmem] * 9 + [hbm] * 2,
        out_specs=(hbm, hbm, vmem, vmem, vmem),
        scratch_shapes=[
            pltpu.VMEM((NLIVE + 1, BLK, BLK), BF16),
            pltpu.VMEM((NLIVE + 1, BLK, BLK), BF16),
            *[pltpu.VMEM((D, FF), BF16)] * 2,
            *[pltpu.VMEM((FF, D), BF16)] * 2,
            pltpu.VMEM((D, FF), BF16),
            pltpu.VMEM((LMAX + 1, KMAX, D), BF16),
            pltpu.VMEM((LMAX + 1, KMAX, D), BF16),
            pltpu.VMEM((LMAX, KMAX, D), F32),
            pltpu.VMEM((LMAX, KMAX, BLK), F32),
            pltpu.VMEM((LMAX, KMAX, D), BF16),
            pltpu.VMEM((LMAX, KMAX, FF), BF16),
            pltpu.VMEM((LMAX, KMAX, FF), F32),
            pltpu.VMEM((LMAX, KMAX, FF), BF16),
            pltpu.VMEM((LMAX, PANELS, BLK, KMAX), BF16),
            pltpu.VMEM((LMAX, PANELS, KMAX, BLK), BF16),
            pltpu.VMEM((8, BLK), F32),
            pltpu.VMEM((RING, 8, BLK), F32),
            pltpu.VMEM((RING, RING, 8, BLK), F32),
            *[pltpu.VMEM((8, BLK), F32)] * 3,
            pltpu.SemaphoreType.DMA((PARTS,)),
            pltpu.SemaphoreType.DMA((LMAX,)),
            pltpu.SemaphoreType.DMA((LMAX,)),
            pltpu.SemaphoreType.DMA((MICRO,)),
            pltpu.SemaphoreType.DMA((MICRO,)),
            pltpu.SemaphoreType.DMA((MICRO,)),
            pltpu.SemaphoreType.DMA((MICRO,)),
            *[pltpu.SemaphoreType.DMA((RING - 1,))] * 4,
            *[pltpu.SemaphoreType.DMA((2,))] * 2,
        ],
        compiler_params=pltpu.CompilerParams(
            collective_id=0, has_side_effects=True, vmem_limit_bytes=60 * 1024 * 1024
        ),
        cost_estimate=pl.CostEstimate(flops=35_000_000_000, bytes_accessed=30_000_000, transcendentals=2_000_000),
    )(inv, count, order, kept, asked, dead, panels, patches, cotangent, gain, up, down)


def live_tables(up_index, down_index):
    listed = jnp.stack([up_index, down_index], axis=1).reshape(PARTS, NLIVE)
    hit = listed[:, :, None] == jnp.arange(NB)[None, None, :]
    live = jnp.any(hit, axis=1)
    inv = jnp.where(live, jnp.sum(jnp.where(hit, jnp.arange(NLIVE)[None, :, None], 0), axis=1), NLIVE)
    return inv.astype(jnp.int32), live.reshape(LMAX, 2 * NB)


def sums_kernel(
    PER, slots, left_hbm, right_hbm, out_ref,
    left_0, left_1, right_0, right_1,
    opp_0, opp_1, nxt_0, nxt_1, prv_0, prv_1, mid_0, mid_1,
    ra_0, ra_1, rb_0, rb_1, ia_0, ia_1, ib_0, ib_1,
    sa_0, sa_1, sb_0, sb_1, ja_0, ja_1, jb_0, jb_1,
    squares, mine, all_tiles,
    load_sem, send_sem, recv_sem, tile_send, tile_recv,
):
    section = lax.axis_index("section")
    replica = lax.axis_index("dp")
    px = replica // RING
    py = lax.rem(replica, RING)

    def peer(axis, step):
        if axis == 0:
            return (lax.rem(px + step, RING) * RING + py, section)
        return (px * RING + lax.rem(py + step, RING), section)

    lefts, rights = (left_1, left_0), (right_1, right_0)

    def load(h):
        l = LMAX - 1 - h
        return (
            pltpu.make_async_copy(left_hbm.at[l], lefts[h], load_sem.at[h, 0]),
            pltpu.make_async_copy(right_hbm.at[l], rights[h], load_sem.at[h, 1]),
        )

    for h in range(2):
        for copy in load(h):
            copy.start()

    barrier = pltpu.get_barrier_semaphore()
    everyone = RING * RING

    def other(step):
        return (lax.rem(replica + step, everyone), section)

    for step in range(1, everyone):
        pl.semaphore_signal(barrier, inc=1, device_id=other(step), device_id_type=MESH)
    pl.semaphore_wait(barrier, everyone - 1)
    for h in range(2):
        for copy in load(h):
            copy.wait()

    opp, nxt, prv, mid = (opp_0, opp_1), (nxt_0, nxt_1), (prv_0, prv_1), (mid_0, mid_1)
    ra, rb, ia, ib = (ra_0, ra_1), (rb_0, rb_1), (ia_0, ia_1), (ib_0, ib_1)
    sa, sb, ja, jb = (sa_0, sa_1), (sb_0, sb_1), (ja_0, ja_1), (jb_0, jb_1)
    place = (px, py)

    def at(axis, step):
        return lax.rem(place[axis] + step, RING)

    def block(h, f, c, g):
        l, s = LMAX - 1 - h, (f * PER + c) * RING + g
        return dot(lefts[h][slots[l, 0, s]], rights[h][slots[l, 1, s]])

    def send(h, kind, c, src, dst, axis, step):
        return pltpu.make_async_remote_copy(
            src_ref=src, dst_ref=dst, send_sem=send_sem.at[h, kind, c], recv_sem=recv_sem.at[h, kind, c],
            device_id=peer(axis, step), device_id_type=MESH,
        )

    def copies(h, c):
        first, second = h, 1 - h
        far = at(second, 2)
        return (
            send(h, 0, c, opp[h].at[c, pl.ds(0, 2)], ra[h].at[c], first, 1),
            send(h, 1, c, opp[h].at[c, pl.ds(2, 2)], rb[h].at[c], first, 3),
            send(h, 2, c, nxt[h].at[c], ia[h].at[c], first, 1),
            send(h, 3, c, prv[h].at[c], ib[h].at[c], first, 3),
            send(h, 4, c, mid[h].at[c, far, pl.ds(0, HALF)], sa[h].at[c], second, 1),
            send(h, 5, c, mid[h].at[c, far, pl.ds(HALF, HALF)], sb[h].at[c], second, 3),
            send(h, 6, c, mid[h].at[c, at(second, 1)], ja[h].at[c], second, 1),
            send(h, 7, c, mid[h].at[c, at(second, 3)], jb[h].at[c], second, 3),
        )

    def far_blocks(c):
        for h in range(2):
            for g in range(RING):
                opp[h][c, g] = block(h, at(h, 2), c, g).astype(BF16)

    def far_sends(c):
        for h in range(2):
            moves = copies(h, c)
            moves[0].start()
            moves[1].start()

    def far_units(c, carry):
        far_blocks(c)
        far_sends(c)
        return carry

    def near_units(c, carry):
        for h in range(2):
            moves = copies(h, c)
            ahead = [block(h, at(h, 1), c, g) for g in range(RING)]
            behind = [block(h, at(h, 3), c, g) for g in range(RING)]
            moves[0].wait_recv()
            for g in range(RING):
                v = ahead[g] + ra[h][c, g].astype(F32) if g < 2 else ahead[g]
                nxt[h][c, g] = v.astype(BF16)
            moves[2].start()
            moves[1].wait_recv()
            for g in range(RING):
                v = behind[g] + rb[h][c, g - 2].astype(F32) if g >= 2 else behind[g]
                prv[h][c, g] = v.astype(BF16)
            moves[3].start()
        return carry

    def own_units(c, carry):
        for h in range(2):
            moves = copies(h, c)
            own = [block(h, place[h], c, g) for g in range(RING)]
            moves[2].wait_recv()
            moves[3].wait_recv()
            for g in range(RING):
                v = own[g] + ia[h][c, g].astype(F32) + ib[h][c, g].astype(F32)
                mid[h][c, g] = v.astype(BF16)
            moves[4].start()
            moves[5].start()
        return carry

    def second_axis(c, carry):
        for h in range(2):
            moves = copies(h, c)
            ahead, behind = at(1 - h, 1), at(1 - h, 3)
            moves[4].wait_recv()
            top = pl.ds(0, HALF)
            v = mid[h][c, ahead, top, :].astype(F32) + sa[h][c].astype(F32)
            mid[h][c, ahead, top, :] = v.astype(BF16)
            moves[6].start()
            moves[5].wait_recv()
            low = pl.ds(HALF, HALF)
            v = mid[h][c, behind, low, :].astype(F32) + sb[h][c].astype(F32)
            mid[h][c, behind, low, :] = v.astype(BF16)
            moves[7].start()
        return carry

    def totals(c, carry):
        for h in range(2):
            moves = copies(h, c)
            moves[6].wait_recv()
            moves[7].wait_recv()
            v = mid[h][c, place[1 - h]].astype(F32) + ja[h][c].astype(F32) + jb[h][c].astype(F32)
            squares[pl.ds(h * (TILE // 2) + c, 1), :] = jnp.sum(v * v, axis=0, keepdims=True)
        return carry

    def drain(c, carry):
        for h in range(2):
            for move in copies(h, c):
                move.wait_send()
        return carry

    squares[...] = jnp.zeros_like(squares)
    for step in (far_units, near_units, own_units, second_axis, totals):
        lax.fori_loop(0, PER, step, 0)
    rows_total = float(RING * RING * KMAX)
    mean = jnp.sum(squares[...].T, axis=0, keepdims=True) * (1.0 / (BLK * BLK))
    mine[...] = jnp.broadcast_to(jnp.sqrt(mean / rows_total + EPS_SCORE), (8, BLK))

    all_tiles[replica] = mine[...]

    def tile(step):
        return pltpu.make_async_remote_copy(
            src_ref=mine, dst_ref=all_tiles.at[replica], send_sem=tile_send.at[step - 1],
            recv_sem=tile_recv.at[step - 1], device_id=other(step), device_id_type=MESH,
        )

    for step in range(1, everyone):
        tile(step).start()
    for step in range(1, everyone):
        tile(step).wait()
    out_ref[...] = all_tiles[:, 0, :]
    lax.fori_loop(0, PER, drain, 0)


def sums(size, number, slots, left, right):
    PER = size // (RING * RING)
    smem = pl.BlockSpec(memory_space=pltpu.SMEM)
    hbm = pl.BlockSpec(memory_space=pl.ANY)

    def blocks(*lead):
        return [pltpu.VMEM((PER, *lead, BLK), BF16)] * 2

    return pl.pallas_call(
        functools.partial(sums_kernel, PER),
        out_shape=jax.ShapeDtypeStruct((RING * RING, BLK), F32),
        in_specs=[smem] + [hbm] * 2,
        out_specs=pl.BlockSpec(memory_space=pltpu.VMEM),
        scratch_shapes=[
            *[pltpu.VMEM((PANELS, BLK, KMAX), BF16)] * 2,
            *[pltpu.VMEM((PANELS, KMAX, BLK), BF16)] * 2,
            *blocks(RING, BLK), *blocks(RING, BLK), *blocks(RING, BLK), *blocks(RING, BLK),
            *blocks(2, BLK), *blocks(2, BLK), *blocks(RING, BLK), *blocks(RING, BLK),
            *blocks(HALF), *blocks(HALF), *blocks(BLK), *blocks(BLK),
            pltpu.VMEM((BLK, BLK), F32),
            pltpu.VMEM((8, BLK), F32),
            pltpu.VMEM((RING * RING, 8, BLK), F32),
            pltpu.SemaphoreType.DMA((2, 2)),
            pltpu.SemaphoreType.DMA((2, 8, PER)),
            pltpu.SemaphoreType.DMA((2, 8, PER)),
            *[pltpu.SemaphoreType.DMA((RING * RING - 1,))] * 2,
        ],
        compiler_params=pltpu.CompilerParams(
            collective_id=number, has_side_effects=True, vmem_limit_bytes=60 * 1024 * 1024
        ),
        cost_estimate=pl.CostEstimate(flops=3_000_000_000, bytes_accessed=8_000_000, transcendentals=0),
    )(slots, left, right)


def every_score(size, number, slots, left, right):
    per = size // (RING * RING)
    tiles = sums(size, number, slots, left, right)
    half = TILE // 2
    tiles = tiles[:, :TILE].reshape(RING, RING, TILE)
    late = tiles[:, :, :per].transpose(0, 2, 1).reshape(size)
    early = tiles[:, :, half:half + per].transpose(1, 2, 0).reshape(size)
    return jnp.pad(jnp.stack([early, late]), ((0, 0), (0, MOST - size)))


def panel_numbers():
    q = np.arange(2 * NB)
    lower = q >= NB
    inner = np.where(lower, q - NB, q)
    cols = np.where(lower, DOWN_COLS, UP_COLS)
    row = np.where(lower, inner // cols + DOWN_COLS, inner // cols)
    col = np.where(lower, inner % cols + UP_COLS, inner % cols)
    table = np.zeros((RING * RING, 8, BLK), np.float32)
    table[:, 0, :OWN] = row.reshape(-1, OWN)
    table[:, 1, :OWN] = col.reshape(-1, OWN)
    return jnp.asarray(table, BF16)


def body(patches, cotangent, keep_order, keep_count, destination, norm_gain, up_blocks, up_index,
         down_blocks, down_index, layer_count, regrow_mask):
    inv, live = live_tables(up_index, down_index)
    dead = jnp.logical_not(live).reshape(LMAX, RING * RING, OWN)
    dead = jnp.pad(dead.astype(F32), ((0, 0), (0, 0), (0, BLK - OWN)))
    left, right, slots, own, most = chain(
        inv.reshape(-1), layer_count.reshape(1, 1), keep_order, keep_count.reshape(1, 1), regrow_mask, dead,
        panel_numbers(), patches[0], cotangent[0], norm_gain,
        up_blocks, down_blocks,
    )
    every = lax.cond(
        most[0, 0] < FEW + 0.5,
        functools.partial(every_score, FEW, 1),
        functools.partial(every_score, MOST, 2),
        slots, left, right,
    )
    rank, wanted = own[:LMAX, :OWN], own[LMAX:, :OWN]
    spots = jnp.arange(MOST).astype(F32)
    picked = jnp.sum(jnp.where(rank[:, :, None] == spots, every[:, None, :], 0.0), axis=2)
    return jnp.where(wanted > 0.5, picked, 0.0)


def solution(mesh):
    return jax.shard_map(
        body, mesh=mesh,
        in_specs=(
            P("dp", None, None), P("dp", None, None), P("dp", None), P("dp"), P("dp", None),
            P("section", None), P("section", None, None, None), P("section", None),
            P("section", None, None, None), P("section", None), P("section"), P("section", "dp"),
        ),
        out_specs=P("section", "dp"), check_vma=False,
    )
```

```python
import functools
import jax
import jax.numpy as jnp
import numpy as np
from jax import lax
from jax.experimental import pallas as pl
from jax.experimental.pallas import tpu as pltpu
from jax.sharding import PartitionSpec as P

D = 1280
FF = 2560
BLK = 128
KMAX = 192
LMAX = 2
NB = 200
NLIVE = 96
NDEAD = NB - NLIVE
UP_COLS = FF // BLK
DOWN_COLS = D // BLK
PARTS = 2 * LMAX
PANELS = UP_COLS + DOWN_COLS
RING = 4
MOST = 2 * NDEAD
FEW = 128
HALF = BLK // 2
TILE = 32
OWN = 2 * NB // (RING * RING)
WIDE = 256
EPS_NORM = 1e-06
EPS_SCORE = 1e-06
MICRO = 2
ROWS = KMAX // MICRO
CHUNK = 512
SQ = 256
FLIP = 5
MESH = pl.DeviceIdType.MESH
F32 = jnp.float32
BF16 = jnp.bfloat16
GELU_A = 0.7978845608028654
GELU_B = 0.044715


def dot(a, b):
    return jnp.dot(a, b, preferred_element_type=F32)


def dot_t(a, b):
    return lax.dot_general(a, b, (((1,), (1,)), ((), ())), preferred_element_type=F32)


def gelu(v):
    return 0.5 * v * (1.0 + jnp.tanh(GELU_A * (v + GELU_B * (v * v * v))))


def gelu_slope(v):
    sq = v * v
    t = jnp.tanh(GELU_A * (v + GELU_B * (v * sq)))
    return 0.5 * (1.0 + t) + 0.5 * v * (1.0 - t * t) * (GELU_A * (1.0 + 3.0 * GELU_B * sq))


def chain_kernel(
    inv_ref,
    count_ref, order, kept, asked_ref, dead, panels, patches, cotangent, gain, up_hbm, down_hbm,
    left_hbm, right_hbm, slots_out, own_out, most_out,
    stage_a, stage_b, up_0, up_1, down_0, down_1, spare, xs, gs, normed, inv_std, act, hidden, pre, grad_pre,
    left, right, mask, row_tiles, all_tiles, most, most_up, most_down,
    stage_sem, left_sem, right_sem, x_send, x_recv, g_send, g_recv,
    tile_send, tile_recv, all_send, all_recv, most_send, most_recv,
):
    sections = lax.axis_size("section")
    replica = lax.axis_index("dp")
    section = lax.axis_index("section")
    first = section == 0
    last = section == sections - 1
    stages = (stage_a, stage_b)
    w_up, w_down = (up_0, up_1), (down_0, down_1)
    w_up_t, w_down_t = (down_0, down_1), (up_1, spare)

    def flag(l):
        return count_ref[:, :] > l

    def load(part):
        l, kind = part // 2, part % 2
        src = (up_hbm, down_hbm)[kind].at[l]
        return pltpu.make_async_copy(src, stages[part % 2].at[pl.ds(0, NLIVE)], stage_sem.at[part])

    stage_a[NLIVE] = jnp.zeros((BLK, BLK), BF16)
    stage_b[NLIVE] = jnp.zeros((BLK, BLK), BF16)
    load(0).start()
    load(1).start()

    barrier = pltpu.get_barrier_semaphore()

    @pl.when(jnp.logical_not(first))
    def _():
        pl.semaphore_signal(barrier, inc=1, device_id=(replica, section - 1), device_id_type=MESH)

    @pl.when(jnp.logical_not(last))
    def _():
        pl.semaphore_signal(barrier, inc=1, device_id=(replica, section + 1), device_id_type=MESH)

    px = replica // RING
    py = lax.rem(replica, RING)

    def along_y(step):
        return (px * RING + lax.rem(py + step, RING), section)

    def along_x(step):
        return (lax.rem(px + step, RING) * RING + py, section)

    for step in range(1, RING):
        pl.semaphore_signal(barrier, inc=1, device_id=along_y(step), device_id_type=MESH)
        pl.semaphore_signal(barrier, inc=1, device_id=along_x(step), device_id_type=MESH)

    def moves(source, target, sends, recvs, to):
        return [
            pltpu.make_async_remote_copy(
                src_ref=source, dst_ref=target, send_sem=sends.at[step - 1], recv_sem=recvs.at[step - 1],
                device_id=to(step), device_id_type=MESH,
            )
            for step in range(1, RING)
        ]

    def row_moves():
        return moves(mask, row_tiles.at[py], tile_send, tile_recv, along_y)

    def all_moves():
        return moves(row_tiles, all_tiles.at[px], all_send, all_recv, along_x)

    def picked(table):
        size = table.shape[0]
        hot = jnp.logical_and(
            lax.broadcasted_iota(jnp.int32, (size, KMAX), 0) == order[:, :KMAX],
            lax.broadcasted_iota(jnp.int32, (size, KMAX), 1) < kept[:, :],
        )
        return lax.dot_general(
            hot.astype(BF16), table[...], (((0,), (0,)), ((), ())), preferred_element_type=F32
        ).astype(BF16)

    @pl.when(first)
    def _():
        xs[0] = picked(patches)

    @pl.when(last)
    def _():
        gs[LMAX] = picked(cotangent)

    mask[...] = jnp.zeros((8, BLK), F32)
    mask[:LMAX, :OWN] = (asked_ref[...] == 1).astype(F32)
    row_tiles[py] = mask[...]

    def meet():
        @pl.when(jnp.logical_or(first, last))
        def _():
            pl.semaphore_wait(barrier, 2 * (RING - 1) + 1)

        @pl.when(jnp.logical_not(jnp.logical_or(first, last)))
        def _():
            pl.semaphore_wait(barrier, 2 * (RING - 1) + 2)

        for move in row_moves():
            move.start()

    def settle():
        for move in row_moves():
            move.wait()
        all_tiles[px] = row_tiles[...]
        for move in all_moves():
            move.start()
        for move in all_moves():
            move.wait()
        count = jnp.zeros((1, 1), F32)
        lanes = lax.broadcasted_iota(jnp.int32, (BLK, BLK), 0)
        later = lanes < lax.broadcasted_iota(jnp.int32, (BLK, BLK), 1)
        later = later.astype(BF16)
        ones = jnp.ones((BLK, BLK), BF16)
        n = RING * RING
        under = lax.broadcasted_iota(jnp.int32, (n, n), 0) > lax.broadcasted_iota(jnp.int32, (n, n), 1)
        spots = lax.broadcasted_iota(jnp.int32, (BLK, WIDE), 1).astype(F32)
        for l in range(LMAX):
            asked = all_tiles[:, :, l, :].reshape(n, BLK) * dead[l]
            flat = asked.astype(BF16)
            totals = dot(flat, ones)
            rank = dot(flat, later) + dot(under.astype(BF16), totals.astype(BF16))
            mine = lax.broadcasted_iota(jnp.int32, (n, BLK), 0) == replica
            own_out[l:l + 1, :] = jnp.sum(jnp.where(mine, rank, 0.0), axis=0, keepdims=True)
            own_out[LMAX + l:LMAX + l + 1, :] = jnp.sum(jnp.where(mine, asked, 0.0), axis=0, keepdims=True)
            count = jnp.maximum(count, jnp.sum(totals[:, :1], axis=0, keepdims=True))
            turned = jnp.where(asked > 0.5, rank, -1.0).T
            found = jnp.zeros((8, WIDE), F32)
            for d in range(n):
                hot = (turned[:, d:d + 1] == spots).astype(BF16)
                found = found + dot(panels[d], hot)
            slots_out[l] = found.astype(jnp.int32)
        most[...] = jnp.broadcast_to(count, (8, BLK))

    def pass_up():
        return pltpu.make_async_remote_copy(
            src_ref=most, dst_ref=most_up, send_sem=most_send.at[0], recv_sem=most_recv.at[0],
            device_id=(replica, section + 1), device_id_type=MESH,
        )

    def pass_down():
        return pltpu.make_async_remote_copy(
            src_ref=most, dst_ref=most_down, send_sem=most_send.at[1], recv_sem=most_recv.at[1],
            device_id=(replica, section - 1), device_id_type=MESH,
        )

    for part in range(PARTS):
        load(part).wait()
        l, kind = part // 2, part % 2
        target, cols = ((w_up, UP_COLS), (w_down, DOWN_COLS))[kind]

        def place(rb, carry, l=l, target=target, cols=cols, part=part):
            rs = pl.ds(pl.multiple_of(rb * BLK, BLK), BLK)
            for cb in range(cols):
                target[l][rs, cb * BLK:(cb + 1) * BLK] = stages[part % 2][inv_ref[part * NB + rb * cols + cb]]
            return carry

        lax.fori_loop(0, NB // cols, place, 0)
        if part == 1:
            meet()
        if part + 2 < PARTS:
            load(part + 2).start()

    def rows_of(mb):
        return pl.ds(pl.multiple_of(mb * ROWS, ROWS), ROWS)

    def cols_of(j, size):
        return pl.ds(pl.multiple_of(j * size, size), size)

    def send_x(mb):
        return pltpu.make_async_remote_copy(
            src_ref=xs.at[LMAX, rows_of(mb)], dst_ref=xs.at[0, rows_of(mb)],
            send_sem=x_send.at[mb], recv_sem=x_recv.at[mb],
            device_id=(replica, section + 1), device_id_type=MESH,
        )

    def send_g(mb):
        return pltpu.make_async_remote_copy(
            src_ref=gs.at[0, rows_of(mb)], dst_ref=gs.at[LMAX, rows_of(mb)],
            send_sem=g_send.at[mb], recv_sem=g_recv.at[mb],
            device_id=(replica, section - 1), device_id_type=MESH,
        )

    def forward(mb, carry):
        r = rows_of(mb)

        @pl.when(jnp.logical_not(first))
        def _():
            send_x(mb).wait_recv()

        for l in range(LMAX):
            x = xs[l, r, :].astype(F32)
            centred = x - jnp.mean(x, axis=-1, keepdims=True)
            inv = lax.rsqrt(jnp.mean(centred * centred, axis=-1, keepdims=True) + EPS_NORM)
            n = centred * inv
            normed[l, r, :] = n
            inv_std[l, r, :] = jnp.broadcast_to(inv, (ROWS, BLK))
            act[l, r, :] = (n * gain[l:l + 1, :]).astype(BF16)

            def up_chunk(j, c, l=l):
                cs = cols_of(j, CHUNK)
                v = dot(act[l, r, :], w_up[l][:, cs])
                pre[l, r, cs] = v
                hidden[l, r, cs] = gelu(v).astype(BF16)
                return c

            lax.fori_loop(0, FF // CHUNK, up_chunk, 0, unroll=True)

            def down_chunk(j, c, l=l):
                cs = cols_of(j, 256)
                v = dot(hidden[l, r, :], w_down[l][:, cs])
                had = xs[l, r, cs]
                moved = (had.astype(F32) + v).astype(BF16)
                xs[l + 1, r, cs] = jnp.where(flag(l), moved, had)
                return c

            lax.fori_loop(0, D // 256, down_chunk, 0, unroll=True)

        @pl.when(jnp.logical_not(last))
        def _():
            send_x(mb).start()

        return carry

    def turn_matrix(source, target):
        def flip(i, c):
            rs = cols_of(i, SQ)
            for j in range(source.shape[1] // SQ):
                target[j * SQ:(j + 1) * SQ, rs] = source[rs, j * SQ:(j + 1) * SQ].T
            return c

        lax.fori_loop(0, source.shape[0] // SQ, flip, 0, unroll=FLIP)

    @pl.when(jnp.logical_not(first))
    def _():
        settle()

    @pl.when(last)
    def _():
        turn_matrix(down_1, spare)

    lax.fori_loop(0, MICRO, forward, 0)

    @pl.when(first)
    def _():
        settle()

    @pl.when(jnp.logical_not(first))
    def _():
        pass_up().wait_recv()
        most[...] = jnp.maximum(most[...], most_up[...])

    @pl.when(jnp.logical_not(last))
    def _():
        pass_up().start()


    def save_left(l):
        return pltpu.make_async_copy(left.at[l], left_hbm.at[l], left_sem.at[l])

    def keep_left():
        for l in range(LMAX):
            for j in range(UP_COLS):
                h = jnp.where(flag(l), hidden[l, :, j * BLK:(j + 1) * BLK], jnp.zeros((KMAX, BLK), BF16))
                left[l, DOWN_COLS + j] = h.T
            for j in range(DOWN_COLS):
                a = jnp.where(flag(l), act[l, :, j * BLK:(j + 1) * BLK], jnp.zeros((KMAX, BLK), BF16))
                left[l, j] = a.T
            save_left(l).start()

    @pl.when(jnp.logical_not(last))
    def _():
        keep_left()

    @pl.when(jnp.logical_not(last))
    def _():
        turn_matrix(down_1, spare)

    for source, target in ((up_1, down_1), (down_0, up_1), (up_0, down_0)):
        turn_matrix(source, target)

    def save_right(l):
        return pltpu.make_async_copy(right.at[l], right_hbm.at[l], right_sem.at[l])

    def backward(mb, carry):
        r = rows_of(mb)

        @pl.when(jnp.logical_not(last))
        def _():
            send_g(mb).wait_recv()

        for l in reversed(range(LMAX)):
            def hidden_chunk(j, c, l=l):
                cs = cols_of(j, CHUNK)
                v = dot(gs[l + 1, r, :], w_down_t[l][:, cs])
                p = (gelu_slope(pre[l, r, cs]) * v).astype(BF16)
                grad_pre[l, r, cs] = p
                for b in range(CHUNK // BLK):
                    right[l, j * (CHUNK // BLK) + b, r, :] = p[:, b * BLK:(b + 1) * BLK]
                return c

            lax.fori_loop(0, FF // CHUNK, hidden_chunk, 0, unroll=True)

            def act_chunk(j, c, l=l):
                cs = cols_of(j, 256)
                v = dot(grad_pre[l, r, :], w_up_t[l][:, cs])
                pre[l, r, cs] = v * gain[l:l + 1, cs]
                return c

            lax.fori_loop(0, D // 256, act_chunk, 0, unroll=True)
            u = pre[l, r, :D]
            n = normed[l, r, :]
            step = inv_std[l, r, :1] * (
                u - jnp.mean(u, axis=-1, keepdims=True) - n * jnp.mean(u * n, axis=-1, keepdims=True)
            )
            had = gs[l + 1, r, :]
            for b in range(DOWN_COLS):
                right[l, UP_COLS + b, r, :] = had[:, b * BLK:(b + 1) * BLK]
            gs[l, r, :] = jnp.where(flag(l), (had.astype(F32) + step).astype(BF16), had)
            if l > 0:
                @pl.when(mb == MICRO - 1)
                def _(l=l):
                    save_right(l).start()

        @pl.when(jnp.logical_not(first))
        def _():
            send_g(mb).start()

        return carry

    lax.fori_loop(0, MICRO, backward, 0)

    @pl.when(jnp.logical_not(last))
    def _():
        pass_up().wait_send()
        pass_down().wait_recv()
        most[...] = jnp.maximum(most[...], most_down[...])

    @pl.when(jnp.logical_not(first))
    def _():
        pass_down().start()

    most_out[...] = most[:1, :1]

    save_right(0).start()

    @pl.when(last)
    def _():
        keep_left()

    def drain(mb, carry):
        @pl.when(jnp.logical_not(last))
        def _():
            send_x(mb).wait_send()

        @pl.when(jnp.logical_not(first))
        def _():
            send_g(mb).wait_send()

        return carry

    lax.fori_loop(0, MICRO, drain, 0)

    @pl.when(jnp.logical_not(first))
    def _():
        pass_down().wait_send()

    for l in range(LMAX):
        save_left(l).wait()
        save_right(l).wait()


def chain(inv, count, order, kept, asked, dead, panels, patches, cotangent, gain, up, down):
    smem = pl.BlockSpec(memory_space=pltpu.SMEM)
    vmem = pl.BlockSpec(memory_space=pltpu.VMEM)
    hbm = pl.BlockSpec(memory_space=pl.ANY)
    return pl.pallas_call(
        chain_kernel,
        out_shape=(
            jax.ShapeDtypeStruct((LMAX, PANELS, BLK, KMAX), BF16),
            jax.ShapeDtypeStruct((LMAX, PANELS, KMAX, BLK), BF16),
            jax.ShapeDtypeStruct((LMAX, 8, WIDE), jnp.int32),
            jax.ShapeDtypeStruct((2 * LMAX, BLK), F32),
            jax.ShapeDtypeStruct((1, 1), F32),
        ),
        in_specs=[smem] + [vmem] * 9 + [hbm] * 2,
        out_specs=(hbm, hbm, vmem, vmem, vmem),
        scratch_shapes=[
            pltpu.VMEM((NLIVE + 1, BLK, BLK), BF16),
            pltpu.VMEM((NLIVE + 1, BLK, BLK), BF16),
            *[pltpu.VMEM((D, FF), BF16)] * 2,
            *[pltpu.VMEM((FF, D), BF16)] * 2,
            pltpu.VMEM((D, FF), BF16),
            pltpu.VMEM((LMAX + 1, KMAX, D), BF16),
            pltpu.VMEM((LMAX + 1, KMAX, D), BF16),
            pltpu.VMEM((LMAX, KMAX, D), F32),
            pltpu.VMEM((LMAX, KMAX, BLK), F32),
            pltpu.VMEM((LMAX, KMAX, D), BF16),
            pltpu.VMEM((LMAX, KMAX, FF), BF16),
            pltpu.VMEM((LMAX, KMAX, FF), F32),
            pltpu.VMEM((LMAX, KMAX, FF), BF16),
            pltpu.VMEM((LMAX, PANELS, BLK, KMAX), BF16),
            pltpu.VMEM((LMAX, PANELS, KMAX, BLK), BF16),
            pltpu.VMEM((8, BLK), F32),
            pltpu.VMEM((RING, 8, BLK), F32),
            pltpu.VMEM((RING, RING, 8, BLK), F32),
            *[pltpu.VMEM((8, BLK), F32)] * 3,
            pltpu.SemaphoreType.DMA((PARTS,)),
            pltpu.SemaphoreType.DMA((LMAX,)),
            pltpu.SemaphoreType.DMA((LMAX,)),
            pltpu.SemaphoreType.DMA((MICRO,)),
            pltpu.SemaphoreType.DMA((MICRO,)),
            pltpu.SemaphoreType.DMA((MICRO,)),
            pltpu.SemaphoreType.DMA((MICRO,)),
            *[pltpu.SemaphoreType.DMA((RING - 1,))] * 4,
            *[pltpu.SemaphoreType.DMA((2,))] * 2,
        ],
        compiler_params=pltpu.CompilerParams(
            collective_id=0, has_side_effects=True, vmem_limit_bytes=60 * 1024 * 1024
        ),
        cost_estimate=pl.CostEstimate(flops=35_000_000_000, bytes_accessed=30_000_000, transcendentals=2_000_000),
    )(inv, count, order, kept, asked, dead, panels, patches, cotangent, gain, up, down)


def live_tables(up_index, down_index):
    listed = jnp.stack([up_index, down_index], axis=1).reshape(PARTS, NLIVE)
    hit = listed[:, :, None] == jnp.arange(NB)[None, None, :]
    live = jnp.any(hit, axis=1)
    inv = jnp.where(live, jnp.sum(jnp.where(hit, jnp.arange(NLIVE)[None, :, None], 0), axis=1), NLIVE)
    return inv.astype(jnp.int32), live.reshape(LMAX, 2 * NB)


def sums_kernel(
    PER, slots, left_hbm, right_hbm, out_ref,
    left_0, left_1, right_0, right_1,
    opp_0, opp_1, nxt_0, nxt_1, prv_0, prv_1, mid_0, mid_1,
    ra_0, ra_1, rb_0, rb_1, ia_0, ia_1, ib_0, ib_1,
    sa_0, sa_1, sb_0, sb_1, ja_0, ja_1, jb_0, jb_1,
    squares, mine, all_tiles,
    load_sem, send_sem, recv_sem, tile_send, tile_recv,
):
    section = lax.axis_index("section")
    replica = lax.axis_index("dp")
    px = replica // RING
    py = lax.rem(replica, RING)

    def peer(axis, step):
        if axis == 0:
            return (lax.rem(px + step, RING) * RING + py, section)
        return (px * RING + lax.rem(py + step, RING), section)

    lefts, rights = (left_1, left_0), (right_1, right_0)

    def load(h):
        l = LMAX - 1 - h
        return (
            pltpu.make_async_copy(left_hbm.at[l], lefts[h], load_sem.at[h, 0]),
            pltpu.make_async_copy(right_hbm.at[l], rights[h], load_sem.at[h, 1]),
        )

    for h in range(2):
        for copy in load(h):
            copy.start()

    barrier = pltpu.get_barrier_semaphore()
    everyone = RING * RING

    def other(step):
        return (lax.rem(replica + step, everyone), section)

    for step in range(1, everyone):
        pl.semaphore_signal(barrier, inc=1, device_id=other(step), device_id_type=MESH)
    pl.semaphore_wait(barrier, everyone - 1)
    for h in range(2):
        for copy in load(h):
            copy.wait()

    opp, nxt, prv, mid = (opp_0, opp_1), (nxt_0, nxt_1), (prv_0, prv_1), (mid_0, mid_1)
    ra, rb, ia, ib = (ra_0, ra_1), (rb_0, rb_1), (ia_0, ia_1), (ib_0, ib_1)
    sa, sb, ja, jb = (sa_0, sa_1), (sb_0, sb_1), (ja_0, ja_1), (jb_0, jb_1)
    place = (px, py)

    def at(axis, step):
        return lax.rem(place[axis] + step, RING)

    def block(h, f, c, g):
        l, s = LMAX - 1 - h, (f * PER + c) * RING + g
        return dot(lefts[h][slots[l, 0, s]], rights[h][slots[l, 1, s]])

    def send(h, kind, c, src, dst, axis, step):
        return pltpu.make_async_remote_copy(
            src_ref=src, dst_ref=dst, send_sem=send_sem.at[h, kind, c], recv_sem=recv_sem.at[h, kind, c],
            device_id=peer(axis, step), device_id_type=MESH,
        )

    def copies(h, c):
        first, second = h, 1 - h
        far = at(second, 2)
        return (
            send(h, 0, c, opp[h].at[c, pl.ds(0, 2)], ra[h].at[c], first, 1),
            send(h, 1, c, opp[h].at[c, pl.ds(2, 2)], rb[h].at[c], first, 3),
            send(h, 2, c, nxt[h].at[c], ia[h].at[c], first, 1),
            send(h, 3, c, prv[h].at[c], ib[h].at[c], first, 3),
            send(h, 4, c, mid[h].at[c, far, pl.ds(0, HALF)], sa[h].at[c], second, 1),
            send(h, 5, c, mid[h].at[c, far, pl.ds(HALF, HALF)], sb[h].at[c], second, 3),
            send(h, 6, c, mid[h].at[c, at(second, 1)], ja[h].at[c], second, 1),
            send(h, 7, c, mid[h].at[c, at(second, 3)], jb[h].at[c], second, 3),
        )

    def far_blocks(c):
        for h in range(2):
            for g in range(RING):
                opp[h][c, g] = block(h, at(h, 2), c, g).astype(BF16)

    def far_sends(c):
        for h in range(2):
            moves = copies(h, c)
            moves[0].start()
            moves[1].start()

    def far_units(c, carry):
        far_blocks(c)
        far_sends(c)
        return carry

    def near_units(c, carry):
        for h in range(2):
            moves = copies(h, c)
            ahead = [block(h, at(h, 1), c, g) for g in range(RING)]
            behind = [block(h, at(h, 3), c, g) for g in range(RING)]
            moves[0].wait_recv()
            for g in range(RING):
                v = ahead[g] + ra[h][c, g].astype(F32) if g < 2 else ahead[g]
                nxt[h][c, g] = v.astype(BF16)
            moves[2].start()
            moves[1].wait_recv()
            for g in range(RING):
                v = behind[g] + rb[h][c, g - 2].astype(F32) if g >= 2 else behind[g]
                prv[h][c, g] = v.astype(BF16)
            moves[3].start()
        return carry

    def own_units(c, carry):
        for h in range(2):
            moves = copies(h, c)
            own = [block(h, place[h], c, g) for g in range(RING)]
            moves[2].wait_recv()
            moves[3].wait_recv()
            for g in range(RING):
                v = own[g] + ia[h][c, g].astype(F32) + ib[h][c, g].astype(F32)
                mid[h][c, g] = v.astype(BF16)
            moves[4].start()
            moves[5].start()
        return carry

    def second_axis(c, carry):
        for h in range(2):
            moves = copies(h, c)
            ahead, behind = at(1 - h, 1), at(1 - h, 3)
            moves[4].wait_recv()
            top = pl.ds(0, HALF)
            v = mid[h][c, ahead, top, :].astype(F32) + sa[h][c].astype(F32)
            mid[h][c, ahead, top, :] = v.astype(BF16)
            moves[6].start()
            moves[5].wait_recv()
            low = pl.ds(HALF, HALF)
            v = mid[h][c, behind, low, :].astype(F32) + sb[h][c].astype(F32)
            mid[h][c, behind, low, :] = v.astype(BF16)
            moves[7].start()
        return carry

    def totals(c, carry):
        for h in range(2):
            moves = copies(h, c)
            moves[6].wait_recv()
            moves[7].wait_recv()
            v = mid[h][c, place[1 - h]].astype(F32) + ja[h][c].astype(F32) + jb[h][c].astype(F32)
            squares[pl.ds(h * (TILE // 2) + c, 1), :] = jnp.sum(v * v, axis=0, keepdims=True)
        return carry

    def drain(c, carry):
        for h in range(2):
            for move in copies(h, c):
                move.wait_send()
        return carry

    squares[...] = jnp.zeros_like(squares)
    for step in (far_units, near_units, own_units, second_axis, totals):
        lax.fori_loop(0, PER, step, 0)
    rows_total = float(RING * RING * KMAX)
    mean = jnp.sum(squares[...].T, axis=0, keepdims=True) * (1.0 / (BLK * BLK))
    mine[...] = jnp.broadcast_to(jnp.sqrt(mean / rows_total + EPS_SCORE), (8, BLK))

    all_tiles[replica] = mine[...]

    def tile(step):
        return pltpu.make_async_remote_copy(
            src_ref=mine, dst_ref=all_tiles.at[replica], send_sem=tile_send.at[step - 1],
            recv_sem=tile_recv.at[step - 1], device_id=other(step), device_id_type=MESH,
        )

    for step in range(1, everyone):
        tile(step).start()
    for step in range(1, everyone):
        tile(step).wait()
    out_ref[...] = all_tiles[:, 0, :]
    lax.fori_loop(0, PER, drain, 0)


def sums(size, number, slots, left, right):
    PER = size // (RING * RING)
    smem = pl.BlockSpec(memory_space=pltpu.SMEM)
    hbm = pl.BlockSpec(memory_space=pl.ANY)

    def blocks(*lead):
        return [pltpu.VMEM((PER, *lead, BLK), BF16)] * 2

    return pl.pallas_call(
        functools.partial(sums_kernel, PER),
        out_shape=jax.ShapeDtypeStruct((RING * RING, BLK), F32),
        in_specs=[smem] + [hbm] * 2,
        out_specs=pl.BlockSpec(memory_space=pltpu.VMEM),
        scratch_shapes=[
            *[pltpu.VMEM((PANELS, BLK, KMAX), BF16)] * 2,
            *[pltpu.VMEM((PANELS, KMAX, BLK), BF16)] * 2,
            *blocks(RING, BLK), *blocks(RING, BLK), *blocks(RING, BLK), *blocks(RING, BLK),
            *blocks(2, BLK), *blocks(2, BLK), *blocks(RING, BLK), *blocks(RING, BLK),
            *blocks(HALF), *blocks(HALF), *blocks(BLK), *blocks(BLK),
            pltpu.VMEM((BLK, BLK), F32),
            pltpu.VMEM((8, BLK), F32),
            pltpu.VMEM((RING * RING, 8, BLK), F32),
            pltpu.SemaphoreType.DMA((2, 2)),
            pltpu.SemaphoreType.DMA((2, 8, PER)),
            pltpu.SemaphoreType.DMA((2, 8, PER)),
            *[pltpu.SemaphoreType.DMA((RING * RING - 1,))] * 2,
        ],
        compiler_params=pltpu.CompilerParams(
            collective_id=number, has_side_effects=True, vmem_limit_bytes=60 * 1024 * 1024
        ),
        cost_estimate=pl.CostEstimate(flops=3_000_000_000, bytes_accessed=8_000_000, transcendentals=0),
    )(slots, left, right)


def every_score(size, number, slots, left, right):
    per = size // (RING * RING)
    tiles = sums(size, number, slots, left, right)
    half = TILE // 2
    tiles = tiles[:, :TILE].reshape(RING, RING, TILE)
    late = tiles[:, :, :per].transpose(0, 2, 1).reshape(size)
    early = tiles[:, :, half:half + per].transpose(1, 2, 0).reshape(size)
    return jnp.pad(jnp.stack([early, late]), ((0, 0), (0, MOST - size)))


def panel_numbers():
    q = np.arange(2 * NB)
    lower = q >= NB
    inner = np.where(lower, q - NB, q)
    cols = np.where(lower, DOWN_COLS, UP_COLS)
    row = np.where(lower, inner // cols + DOWN_COLS, inner // cols)
    col = np.where(lower, inner % cols + UP_COLS, inner % cols)
    table = np.zeros((RING * RING, 8, BLK), np.float32)
    table[:, 0, :OWN] = row.reshape(-1, OWN)
    table[:, 1, :OWN] = col.reshape(-1, OWN)
    return jnp.asarray(table, BF16)


def body(patches, cotangent, keep_order, keep_count, destination, norm_gain, up_blocks, up_index,
         down_blocks, down_index, layer_count, regrow_mask):
    inv, live = live_tables(up_index, down_index)
    dead = jnp.logical_not(live).reshape(LMAX, RING * RING, OWN)
    dead = jnp.pad(dead.astype(F32), ((0, 0), (0, 0), (0, BLK - OWN)))
    left, right, slots, own, most = chain(
        inv.reshape(-1), layer_count.reshape(1, 1), keep_order, keep_count.reshape(1, 1), regrow_mask, dead,
        panel_numbers(), patches[0], cotangent[0], norm_gain,
        up_blocks, down_blocks,
    )
    every = lax.cond(
        most[0, 0] < FEW + 0.5,
        functools.partial(every_score, FEW, 1),
        functools.partial(every_score, MOST, 2),
        slots, left, right,
    )
    rank, wanted = own[:LMAX, :OWN], own[LMAX:, :OWN]
    spots = jnp.arange(MOST).astype(F32)
    picked = jnp.sum(jnp.where(rank[:, :, None] == spots, every[:, None, :], 0.0), axis=2)
    return jnp.where(wanted > 0.5, picked, 0.0)


def solution(mesh):
    return jax.shard_map(
        body, mesh=mesh,
        in_specs=(
            P("dp", None, None), P("dp", None, None), P("dp", None), P("dp"), P("dp", None),
            P("section", None), P("section", None, None, None), P("section", None),
            P("section", None, None, None), P("section", None), P("section"), P("section", "dp"),
        ),
        out_specs=P("section", "dp"), check_vma=False,
    )
```
